32 devices in a mesh: groups: 2 (over y), vox: 4 (over z), spot: 2 (over x), rep: 2 (over core).
Axes of the slice: x: 2, y: 2, z: 4, core: 2. Of those that a mesh axis runs over, the one named last changes fastest.
Arguments:
- dose_blocks: bfloat16 [128, 2, 48, 128, 128], P(('groups', 'vox'), 'spot', 'rep'), parts along dimension 0, may hold values from -0.078125 to 0.078125
- block_cols: int32 [128, 2, 48], P(('groups', 'vox'), 'spot', 'rep'), parts along dimension 0, may hold values from 0 to 63, as said below
- block_exps: int32 [128, 2, 48], P(('groups', 'vox'), 'spot', 'rep'), parts along dimension 0, may hold values from -1 to 1
- live_counts: int32 [128, 2], P(('groups', 'vox'), 'spot'), parts along dimension 0, may hold values from 1 to 48
- labels: int32 [16384], P(('groups', 'vox', 'spot', 'rep')), parts along dimension 0, may hold values from 0 to 7
- upper_dose: float32 [16], P('groups'), parts along dimension 0, may hold values from -0.5 to 1
- upper_weight: float32 [16], P('groups'), parts along dimension 0, may hold values from 0.5 to 2
- lower_dose: float32 [16], P('groups'), parts along dimension 0, may hold values from -1.5 to 0
- lower_weight: float32 [16], P('groups'), parts along dimension 0, may hold values from 0.5 to 2
- initial_spot_weights: float32 [32, 2, 8192], P('groups', 'spot', 'vox'), parts along dimension 0, may hold values from 0.5 to 2
Outputs:
- final_weights: float32 [32, 2, 8192], P('groups', 'spot', 'vox'), parts along dimension 0
- last_gradient: float32 [32, 2, 8192], P('groups', 'spot', 'vox'), parts along dimension 0
The draws below stay inside these ranges and needn't reach their ends.
There are 2 independent parts, one for each index of `groups`. The reference program is written for one: setup_inputs(seed, part) draws one part's arguments, and reference() takes and returns one part's arrays. A program takes and returns all parts, laid end to end along the dimension named above; each array names one. Nothing has to cross between parts.
Inputs may be any that keep to these rules, and one draw needn't show every extreme that they name: `block_cols`: within one block-row and spot range all 48 entries differ.
All inputs are finite; a program needn't handle non-finite values.
Results may differ from the reference program's by a relative error of at most 0.0075.
The reference program's roundings to bfloat16 on the way count: a program that leaves them out, or rounds other values in their place, can miss the bound.
Values may be sent and summed in bfloat16 or wider, within the bound.
No kernel may reach another device: no remote copies, remote signals or barrier semaphores. Data moves between devices by JAX's collectives and lax.ppermute only.
A program may use at most 64 MiB of HBM per device.

```python
import math
import jax
import jax.numpy as jnp
from jax import lax

BLK = 128
PLAN_WEIGHTINGS = 16
KPS = 48
NSTRUCT = 8
ITERS = 4
ROWB = 64
VOX = 8192
SPOTS_PER_RANGE = 8192
CBS = 64
N_SPOT = 2


def draw_block_cols(key, part):
    key = jax.random.fold_in(key, 7)
    scores = jax.random.randint(key, (ROWB, N_SPOT, CBS), 0, 2 ** 20) * CBS + jnp.arange(CBS, dtype=jnp.int32)
    order = jnp.argsort(scores, axis=-1, stable=True)
    return order[:, :, :KPS].astype(jnp.int32)


def plant(result, own_key, smallest, high):
    dims = result.shape
    index_at = [jax.random.randint(jax.random.fold_in(own_key, axis), (), 0, dims[axis]) for axis in range(len(dims))]
    result = result.at[tuple(index_at)].set(smallest)
    longest = dims.index(max(dims))
    index_at[longest] = (index_at[longest] + 1) % dims[longest]
    return result.at[tuple(index_at)].set(high)


def block_scale(own_key, dims, pieces, smallest, largest):
    def one(dim, shards_of):
        steps = jax.random.uniform(jax.random.fold_in(jax.random.fold_in(own_key, 6), dim), (shards_of,), jnp.float32, smallest / len(pieces), largest / len(pieces))
        return jnp.repeat(jnp.exp(steps), dims[dim] // shards_of).reshape((-1,) + (1,) * (len(dims) - dim - 1))

    gain = one(*pieces[0])
    for cut in pieces[1:]:
        gain = gain * one(*cut)
    return gain


def bell_draw(key, extent, deviation, limit, split=(), held_as=jnp.bfloat16):
    entries = jax.random.normal(key, extent, jnp.float32) * deviation
    if len(split) > 0:
        entries = block_scale(key, extent, split, -0.22, 0.18) * entries
    return jnp.clip(entries, min=-limit, max=limit).astype(held_as)


def setup_inputs(seed: int = 0, part: int = 0) -> dict:
    seeds = jax.random.split(jax.random.key(seed), 11)
    own_keys = jax.random.split(jax.random.fold_in(seeds[10], part), 11)
    return {
        "dose_blocks": bell_draw(own_keys[0], (ROWB, N_SPOT, KPS, BLK, BLK), (BLK * KPS * N_SPOT // 2) ** -0.5, 0.078125, ((0, 4), (1, 2), (2, 2))),
        "block_cols": draw_block_cols(jax.random.fold_in(jax.random.fold_in(seeds[10], part), 71), part),
        "block_exps": plant(jax.random.randint(own_keys[2], (ROWB, N_SPOT, KPS), -1, 2), jax.random.fold_in(own_keys[2], 1), -1, 1).astype(jnp.int32),
        "live_counts": plant(jax.random.randint(own_keys[3], (ROWB, N_SPOT), 1, KPS + 1), jax.random.fold_in(own_keys[3], 1), 1, KPS).astype(jnp.int32),
        "labels": plant(jax.random.randint(own_keys[4], (VOX,), 0, NSTRUCT), jax.random.fold_in(own_keys[4], 1), 0, NSTRUCT - 1).astype(jnp.int32),
        "upper_dose": jnp.clip(jax.random.uniform(own_keys[5], (NSTRUCT,), jnp.float32, -0.5, 1.0), -0.5, 1.0),
        "upper_weight": jnp.clip(jnp.exp(jax.random.uniform(own_keys[6], (NSTRUCT,), jnp.float32, math.log(0.5), math.log(2.0))), 0.5, 2.0),
        "lower_dose": jnp.clip(jax.random.uniform(own_keys[7], (NSTRUCT,), jnp.float32, -1.5, 0.0), -1.5, 0.0),
        "lower_weight": jnp.clip(jnp.exp(jax.random.uniform(own_keys[8], (NSTRUCT,), jnp.float32, math.log(0.5), math.log(2.0))), 0.5, 2.0),
        "initial_spot_weights": jnp.clip(jnp.exp(math.log(2.0) - 1.3862944 * jax.random.uniform(own_keys[9], (PLAN_WEIGHTINGS, N_SPOT, SPOTS_PER_RANGE), jnp.float32) ** block_scale(own_keys[9], (PLAN_WEIGHTINGS, N_SPOT, SPOTS_PER_RANGE), ((1, 2), (2, 4)), -0.2, 0.2)), 0.5, 2.0),
    }


def risk_slope(dose, labels, upper_dose, upper_weight, lower_dose, lower_weight):
    onehot = (labels[:, None] == jnp.arange(upper_dose.shape[0], dtype=jnp.int32)[None, :]).astype(jnp.float32)
    table = jnp.stack([upper_dose, upper_weight, lower_dose, lower_weight], axis=1)
    params = jnp.dot(onehot, table, precision=lax.Precision.HIGHEST)
    slope = params[:, 1] * jax.nn.sigmoid(4.0 * (dose - params[:, 0])) - params[:, 3] * jax.nn.sigmoid(4.0 * (params[:, 2] - dose))
    return slope.astype(jnp.bfloat16)


def reference(dose_blocks, block_cols, block_exps, live_counts, labels, upper_dose, upper_weight, lower_dose, lower_weight, initial_spot_weights):
    slots = jnp.arange(KPS, dtype=jnp.int32)
    factor = jnp.where(slots[None, None, :] < live_counts[:, :, None], jnp.exp2(block_exps.astype(jnp.float32)), jnp.float32(0.0))
    ranges = jnp.arange(N_SPOT, dtype=jnp.int32)[:, None]
    weights = initial_spot_weights
    objective_gradient = jnp.zeros_like(initial_spot_weights)
    for step in range(ITERS):
        rounded = weights.astype(jnp.bfloat16).astype(jnp.float32).reshape(PLAN_WEIGHTINGS, N_SPOT, CBS, BLK)

        def forward(items):
            matrix_tiles, cols, step_scale = items
            selected_spots = rounded[:, ranges, cols]
            dose_product = jnp.einsum('yibq,ibeq->ibye', selected_spots, matrix_tiles.astype(jnp.float32))
            return jnp.einsum('nkjv,nk->jv', dose_product, step_scale, precision=lax.Precision.HIGHEST)

        rows = lax.map(forward, (dose_blocks, block_cols, factor))
        dose = jnp.transpose(rows, (1, 0, 2)).reshape(PLAN_WEIGHTINGS, VOX)
        slope = risk_slope(dose, labels, upper_dose, upper_weight, lower_dose, lower_weight)
        slope_rows = jnp.transpose(slope.reshape(PLAN_WEIGHTINGS, ROWB, BLK), (1, 0, 2)).astype(jnp.float32)

        def backward(running_total, items):
            matrix_tiles, cols, step_scale, part = items
            risk_term = jnp.einsum('ix,rlxf->irlf', part, matrix_tiles.astype(jnp.float32)) * step_scale[None, :, :, None]
            return running_total.at[:, ranges, cols].add(risk_term), None

        start = jnp.zeros((PLAN_WEIGHTINGS, N_SPOT, CBS, BLK), jnp.float32)
        running_total, unused = lax.scan(backward, start, (dose_blocks, block_cols, factor, slope_rows))
        objective_gradient = running_total.reshape(PLAN_WEIGHTINGS, N_SPOT, SPOTS_PER_RANGE)
        weights = jnp.maximum(weights - 0.5 * objective_gradient, 0.0)
    return weights, objective_gradient
```

```python
import functools

import jax
import jax.numpy as jnp
from jax import lax
from jax.experimental import pallas as pl
from jax.experimental.pallas import tpu as pltpu
from jax.sharding import PartitionSpec as P

ITERS = 4
F32 = jnp.float32
BF16 = jnp.bfloat16
PARAMS = pltpu.CompilerParams(vmem_limit_bytes=20 * 2**20)


def in_vmem():
    return pl.BlockSpec(memory_space=pltpu.VMEM)


def in_smem():
    return pl.BlockSpec(memory_space=pltpu.SMEM)


def held(array):
    return pltpu.with_memory_space_constraint(array, pltpu.VMEM)


def load_kernel(pieces, stored, kept, turned, sems):
    size = stored.shape[0] // pieces
    copies = [
        pltpu.make_async_copy(
            stored.at[pl.ds(i * size, size)], kept.at[pl.ds(i * size, size)], sems.at[i]
        )
        for i in range(pieces)
    ]
    for copy in copies:
        copy.start()
    step = 8 if size % 8 == 0 else 1
    for i, copy in enumerate(copies):
        copy.wait()

        def turn(t, carry, i=i):
            for u in range(step):
                n = i * size + t * step + u
                turned[n] = kept[n].T
            return carry

        lax.fori_loop(0, size // step, turn, 0)


def load_matrix(tiles):
    pieces = 16 if tiles.shape[0] % 16 == 0 else 1
    return pl.pallas_call(
        functools.partial(load_kernel, pieces),
        in_specs=[pl.BlockSpec(memory_space=pltpu.HBM)],
        out_specs=[in_vmem(), in_vmem()],
        out_shape=[pltpu.VMEM(tiles.shape, tiles.dtype)] * 2,
        scratch_shapes=[pltpu.SemaphoreType.DMA((pieces,))],
        compiler_params=PARAMS,
        cost_estimate=pl.CostEstimate(
            flops=0, bytes_accessed=2 * tiles.size * 2, transcendentals=0
        ),
        name="load_matrix",
    )(tiles)


def forward_kernel(slots, index, *refs):
    pieces, turned, dose, scaled = refs[:-3], refs[-3], refs[-2], refs[-1]
    columns = (scaled.shape[0] - 1) // 3
    at = 0
    for piece in pieces:
        n = piece.shape[0]
        values = piece[...]
        scaled[at : at + n] = values * BF16(0.5)
        scaled[columns + at : columns + at + n] = values
        scaled[2 * columns + at : 2 * columns + at + n] = values * BF16(2.0)
        at += n
    scaled[3 * columns] = jnp.zeros(scaled.shape[1:], BF16)
    rows = dose.shape[0]
    unroll = 4 if rows % 4 == 0 else 1

    def some_rows(t, carry):
        for u in range(unroll):
            b = t * unroll + u
            left = jnp.concatenate([scaled[index[b * slots + k]] for k in range(slots)], axis=1)
            right = turned[pl.ds(b * slots, slots)]
            right = right.reshape(slots * right.shape[1], right.shape[2])
            dose[b] = jnp.dot(left, right, preferred_element_type=F32)
        return carry

    lax.fori_loop(0, rows // unroll, some_rows, 0)


def forward(index, pieces, turned, rows, slots):
    columns = sum(p.shape[0] for p in pieces)
    weightings, width = pieces[0].shape[1:]
    return pl.pallas_call(
        functools.partial(forward_kernel, slots),
        in_specs=[in_smem()] + [in_vmem()] * (len(pieces) + 1),
        out_specs=in_vmem(),
        out_shape=jax.ShapeDtypeStruct((rows, weightings, width), F32),
        scratch_shapes=[pltpu.VMEM((3 * columns + 1, weightings, width), BF16)],
        compiler_params=PARAMS,
        name="forward",
    )(index, *pieces, held(turned))


def backward_kernel(slots, index, factor, own, other, levels, kept, far, near, slope, total):
    dose = own[...] + other[...]
    upper_dose, upper_weight, lower_dose, lower_weight = (levels[i] for i in range(4))
    slope[...] = (
        upper_weight * jax.nn.sigmoid(4.0 * (dose - upper_dose))
        - lower_weight * jax.nn.sigmoid(4.0 * (lower_dose - dose))
    ).astype(BF16)
    total[...] = jnp.zeros_like(total)
    rows = own.shape[0]
    width = kept.shape[-1]
    unroll = 4 if rows % 4 == 0 else 1
    group = 12 if slots % 12 == 0 else 1

    def some_rows(t, carry):
        for u in range(unroll):
            b = t * unroll + u
            left = slope[b]
            for k0 in range(0, slots, group):
                places = [b * slots + k0 + k for k in range(group)]
                right = jnp.concatenate([kept[p] for p in places], axis=1)
                product = jnp.dot(left, right, preferred_element_type=F32)
                columns = [index[p] for p in places]
                old = [total[c] for c in columns]
                for k, p in enumerate(places):
                    part = product[:, k * width : (k + 1) * width]
                    total[columns[k]] = old[k] + part * factor[p]
        return carry

    lax.fori_loop(0, rows // unroll, some_rows, 0)
    half = near.shape[0]
    near[...] = total[:half]
    far[...] = total[half:]


def backward(index, factor, own, other, levels, kept, columns, slots):
    rows, weightings, width = own.shape
    half = (columns // 2, weightings, width)
    return pl.pallas_call(
        functools.partial(backward_kernel, slots),
        in_specs=[in_smem()] * 2 + [in_vmem()] * 4,
        out_specs=[in_vmem()] * 2,
        out_shape=[jax.ShapeDtypeStruct(half, F32)] * 2,
        scratch_shapes=[
            pltpu.VMEM((rows, weightings, width), BF16),
            pltpu.VMEM((columns, weightings, width), F32),
        ],
        compiler_params=PARAMS,
        name="slope_backward",
    )(index, factor, own, other, levels, held(kept))


def swap(array, axis, size, bit):
    return lax.ppermute(array, axis, [(i, i ^ bit) for i in range(size)])


def per_device(
    sizes,
    dose_blocks,
    block_cols,
    block_exps,
    live_counts,
    labels,
    upper_dose,
    upper_weight,
    lower_dose,
    lower_weight,
    initial_spot_weights,
):
    n_vox, n_spot, n_rep = sizes
    z, x, core = (lax.axis_index(a) for a in ("vox", "spot", "rep"))
    rows, _, slots, width, _ = dose_blocks.shape
    weightings, _, chunk_spots = initial_spot_weights.shape
    chunk = chunk_spots // width
    columns = chunk * n_vox
    vox_bits = n_vox.bit_length() - 1
    top = 1 << (vox_bits - 1)

    mine = core * top + z % top
    places = block_cols[:, 0] ^ (mine * chunk)
    position = core * slots + jnp.arange(slots, dtype=jnp.int32)
    live = position[None, :] < live_counts
    exps = block_exps[:, 0]
    factor = jnp.where(live, jnp.where(exps < 0, 0.5, jnp.where(exps > 0, 2.0, 1.0)), 0.0)
    factor = factor.astype(F32).reshape(-1)
    forward_index = jnp.where(live, (exps + 1) * columns + places, 3 * columns).reshape(-1)
    places = places.reshape(-1)

    weights = initial_spot_weights[:, 0].reshape(weightings, chunk, width).transpose(1, 0, 2)
    moves = []
    for to_z in range(n_vox):
        for to_core in range(2):
            from_z, from_core = to_core * top + to_z % top, to_z // top
            moves.append((from_z * 2 + from_core, to_z * 2 + to_core))
    weights = lax.ppermute(weights, ("vox", "rep"), moves)

    kept, turned = load_matrix(dose_blocks.reshape(rows * slots, width, width))

    all_labels = labels
    for axis, size, place in (("rep", n_rep, core), ("spot", n_spot, x)):
        bit = 1
        while bit < size:
            got = swap(all_labels, axis, size, bit)
            first = (place // bit) % 2 == 0
            all_labels = jnp.concatenate(
                [jnp.where(first, all_labels, got), jnp.where(first, got, all_labels)]
            )
            bit *= 2
    all_labels = all_labels.reshape(rows, 1, width)
    table = jnp.stack([upper_dose, upper_weight, lower_dose, lower_weight], axis=0)
    levels = jnp.zeros((4, rows, 1, width), F32)
    for c in range(table.shape[1]):
        levels = jnp.where(all_labels[None] == c, table[:, c][:, None, None, None], levels)

    for step in range(ITERS):
        piece = weights.astype(BF16)
        pieces = [piece]
        for bit in range(vox_bits - 1):
            whole = jnp.concatenate(pieces, axis=0) if len(pieces) > 1 else piece
            pieces = pieces + [swap(whole, "vox", n_vox, 1 << bit)]
        whole = jnp.concatenate(pieces, axis=0) if len(pieces) > 1 else piece
        pieces = [whole, swap(whole, "rep", n_rep, 1)]

        dose = forward(forward_index, pieces, turned, rows, slots)
        dose = dose + swap(dose, "rep", n_rep, 1)
        bit = 1
        while bit < n_spot // 2:
            dose = dose + swap(dose, "spot", n_spot, bit)
            bit *= 2
        other = swap(dose, "spot", n_spot, bit)

        far, near = backward(places, factor, dose, other, levels, kept, columns, slots)
        part = near + swap(far, "rep", n_rep, 1)
        for bit in reversed(range(vox_bits - 1)):
            half = part.shape[0] // 2
            part = part[:half] + swap(part[half:], "vox", n_vox, 1 << bit)
        gradient = part + swap(part, "vox", n_vox, top)
        weights = jnp.maximum(weights - 0.5 * gradient, 0.0)

    both = jnp.stack([weights, gradient])
    both = jnp.where(z // top == core, both, swap(both, "rep", n_rep, 1))
    both = both.transpose(0, 2, 1, 3).reshape(2, weightings, 1, chunk_spots)
    return both[0], both[1]


def solution(mesh):
    placed = (
        P(("groups", "vox"), "spot", "rep", None, None),
        P(("groups", "vox"), "spot", "rep"),
        P(("groups", "vox"), "spot", "rep"),
        P(("groups", "vox"), "spot"),
        P(("groups", "vox", "spot", "rep")),
        P("groups"),
        P("groups"),
        P("groups"),
        P("groups"),
        P("groups", "spot", "vox"),
    )
    sizes = tuple(mesh.shape[a] for a in ("vox", "spot", "rep"))
    return jax.shard_map(
        functools.partial(per_device, sizes),
        mesh=mesh,
        in_specs=placed,
        out_specs=(P("groups", "spot", "vox"), P("groups", "spot", "vox")),
        check_vma=False,
    )
```

```python
import functools

import jax
import jax.numpy as jnp
from jax import lax
from jax.experimental import pallas as pl
from jax.experimental.pallas import tpu as pltpu
from jax.sharding import PartitionSpec as P

ITERS = 4
F32 = jnp.float32
BF16 = jnp.bfloat16
PARAMS = pltpu.CompilerParams(vmem_limit_bytes=20 * 2**20)


def in_vmem():
    return pl.BlockSpec(memory_space=pltpu.VMEM)


def in_smem():
    return pl.BlockSpec(memory_space=pltpu.SMEM)


def held(array):
    return pltpu.with_memory_space_constraint(array, pltpu.VMEM)


def load_kernel(place, cols, exps, live, stored, kept, turned, index, places, factor, sems):
    z, core, n_vox = place[0], place[1], place[2]
    rows, _, slots = cols.shape
    columns = place[3]
    own = columns // (2 * n_vox)
    copies = [
        pltpu.make_async_copy(
            stored.at[pl.ds(b * slots, slots)], kept.at[pl.ds(b * slots, slots)], sems.at[b]
        )
        for b in range(rows)
    ]
    for copy in copies:
        copy.start()
    step = 8 if slots % 8 == 0 else 1
    for b, copy in enumerate(copies):
        copy.wait()

        def turn(t, carry, b=b):
            for u in range(step):
                k = t * step + u
                n = b * slots + k
                turned[n] = kept[n].T
                column, exponent = cols[b, 0, k], exps[b, 0, k]
                piece, within = lax.div(column, own), lax.rem(column, own)
                owner_core, owner_z = lax.rem(piece, 2), lax.div(piece, 2)
                at = ((owner_core ^ core) * n_vox + (owner_z ^ z)) * own + within
                used = core * slots + k < live[b, 0]
                scale = jnp.where(exponent < 0, 0.5, jnp.where(exponent > 0, 2.0, 1.0))
                places[n] = at
                index[n] = jnp.where(used, (exponent + 1) * columns + at, 3 * columns)
                factor[n] = jnp.where(used, scale, 0.0).astype(F32)
            return carry

        lax.fori_loop(0, slots // step, turn, 0)


def load_matrix(place, cols, exps, live, tiles):
    rows, _, slots = cols.shape
    return pl.pallas_call(
        load_kernel,
        in_specs=[in_smem()] * 4 + [pl.BlockSpec(memory_space=pltpu.HBM)],
        out_specs=[in_vmem()] * 2 + [in_smem()] * 3,
        out_shape=[pltpu.VMEM(tiles.shape, tiles.dtype)] * 2
        + [jax.ShapeDtypeStruct((rows * slots,), t) for t in (jnp.int32, jnp.int32, F32)],
        scratch_shapes=[pltpu.SemaphoreType.DMA((rows,))],
        compiler_params=PARAMS,
        cost_estimate=pl.CostEstimate(
            flops=0, bytes_accessed=2 * tiles.size * 2, transcendentals=0
        ),
        name="load_matrix",
    )(place, cols, exps, live, tiles)


def forward_kernel(slots, index, *refs):
    pieces, turned, dose, scaled = refs[:-3], refs[-3], refs[-2], refs[-1]
    columns = (scaled.shape[0] - 1) // 3
    at = 0
    for piece in pieces:
        n = piece.shape[0]
        values = piece[...]
        scaled[at : at + n] = values * BF16(0.5)
        scaled[columns + at : columns + at + n] = values
        scaled[2 * columns + at : 2 * columns + at + n] = values * BF16(2.0)
        at += n
    scaled[3 * columns] = jnp.zeros(scaled.shape[1:], BF16)
    rows = dose.shape[0]
    unroll = 4 if rows % 4 == 0 else 1

    def some_rows(t, carry):
        for u in range(unroll):
            b = t * unroll + u
            left = jnp.concatenate([scaled[index[b * slots + k]] for k in range(slots)], axis=1)
            right = turned[pl.ds(b * slots, slots)]
            right = right.reshape(slots * right.shape[1], right.shape[2])
            dose[b] = jnp.dot(left, right, preferred_element_type=F32)
        return carry

    lax.fori_loop(0, rows // unroll, some_rows, 0)


def forward(index, pieces, turned, rows, slots):
    columns = sum(p.shape[0] for p in pieces)
    weightings, width = pieces[0].shape[1:]
    return pl.pallas_call(
        functools.partial(forward_kernel, slots),
        in_specs=[in_smem()] + [in_vmem()] * (len(pieces) + 1),
        out_specs=in_vmem(),
        out_shape=jax.ShapeDtypeStruct((rows, weightings, width), F32),
        scratch_shapes=[pltpu.VMEM((3 * columns + 1, weightings, width), BF16)],
        compiler_params=PARAMS,
        name="forward",
    )(index, *pieces, held(turned))


def backward_kernel(slots, index, factor, own, other, levels, kept, far, near, slope, total):
    dose = own[...] + other[...]
    upper_dose, upper_weight, lower_dose, lower_weight = (levels[i] for i in range(4))
    slope[...] = (
        upper_weight * jax.nn.sigmoid(4.0 * (dose - upper_dose))
        - lower_weight * jax.nn.sigmoid(4.0 * (lower_dose - dose))
    ).astype(BF16)
    total[...] = jnp.zeros_like(total)
    rows = own.shape[0]
    width = kept.shape[-1]
    unroll = 4 if rows % 4 == 0 else 1
    group = 12 if slots % 12 == 0 else 1

    def some_rows(t, carry):
        for u in range(unroll):
            b = t * unroll + u
            left = slope[b]
            for k0 in range(0, slots, group):
                places = [b * slots + k0 + k for k in range(group)]
                right = jnp.concatenate([kept[p] for p in places], axis=1)
                product = jnp.dot(left, right, preferred_element_type=F32)
                columns = [index[p] for p in places]
                old = [total[c] for c in columns]
                for k, p in enumerate(places):
                    part = product[:, k * width : (k + 1) * width]
                    total[columns[k]] = old[k] + part * factor[p]
        return carry

    lax.fori_loop(0, rows // unroll, some_rows, 0)
    half = near.shape[0]
    near[...] = total[:half]
    far[...] = total[half:]


def backward(index, factor, own, other, levels, kept, columns, slots):
    rows, weightings, width = own.shape
    half = (columns // 2, weightings, width)
    return pl.pallas_call(
        functools.partial(backward_kernel, slots),
        in_specs=[in_smem()] * 2 + [in_vmem()] * 4,
        out_specs=[in_vmem()] * 2,
        out_shape=[jax.ShapeDtypeStruct(half, F32)] * 2,
        scratch_shapes=[
            pltpu.VMEM((rows, weightings, width), BF16),
            pltpu.VMEM((columns, weightings, width), F32),
        ],
        compiler_params=PARAMS,
        name="slope_backward",
    )(index, factor, own, other, levels, held(kept))


def per_device(
    sizes,
    dose_blocks,
    block_cols,
    block_exps,
    live_counts,
    labels,
    upper_dose,
    upper_weight,
    lower_dose,
    lower_weight,
    initial_spot_weights,
):
    n_vox, n_spot = sizes
    z, x, core = (lax.axis_index(a) for a in ("vox", "spot", "rep"))
    rows, _, slots, width, _ = dose_blocks.shape
    weightings, _, chunk_spots = initial_spot_weights.shape
    chunk = chunk_spots // width
    columns = chunk * n_vox
    own = chunk // 2
    initial = initial_spot_weights[:, 0].reshape(weightings, chunk, width)
    weights = lax.dynamic_slice_in_dim(initial, core * own, own, 1).transpose(1, 0, 2)

    def over_vox(arrays):
        return [
            lax.ppermute(a, "vox", [(i, i ^ d) for i in range(n_vox)])
            for d, a in enumerate(arrays, 1)
        ]

    def over_rep(array):
        return lax.ppermute(array, "rep", [(0, 1), (1, 0)])

    place = jnp.stack([z, core, n_vox, columns]).astype(jnp.int32)
    level_table = jnp.stack([upper_dose, upper_weight, lower_dose, lower_weight])
    known = labels.astype(F32).reshape(-1, width)

    def gather_weights(weights):
        piece = weights.astype(BF16)
        return [piece] + over_vox([piece] * (n_vox - 1))

    pieces = gather_weights(weights)
    kept, turned, index, places, factor = load_matrix(
        place, block_cols, block_exps, live_counts, dose_blocks.reshape(rows * slots, width, width)
    )

    for step in range(ITERS):
        near = jnp.concatenate(pieces, axis=0)
        dose = forward(index, [near, over_rep(near)], turned, rows, slots)

        exchanges = [("rep", 2, 1, core)]
        bit = 1
        while bit < n_spot:
            exchanges.append(("spot", n_spot, bit, x))
            bit *= 2
        for axis, size, bit, at in exchanges:
            sent = dose
            if step == 0:
                n = known.shape[0]
                tile = jnp.pad(known, ((0, weightings - n), (0, 0)))
                sent = jnp.concatenate([dose, tile[None]], axis=0)
            got = lax.ppermute(sent, axis, [(i, i ^ bit) for i in range(size)])
            if step == 0:
                theirs = got[rows, :n]
                first = (at // bit) % 2 == 0
                known = jnp.concatenate(
                    [jnp.where(first, known, theirs), jnp.where(first, theirs, known)]
                )
                got = got[:rows]
            if (axis, bit) != (exchanges[-1][0], exchanges[-1][2]):
                dose = dose + got
        if step == 0:
            levels = jnp.zeros((4, rows, 1, width), F32)
            for c in range(level_table.shape[1]):
                value = level_table[:, c][:, None, None, None]
                levels = jnp.where(known[None, :, None, :] == c, value, levels)

        far, near = backward(places, factor, dose, got, levels, kept, columns, slots)
        near = near + over_rep(far)
        parts = over_vox([near[d * own : (d + 1) * own] for d in range(1, n_vox)])
        gradient = near[:own]
        for part in parts:
            gradient = gradient + part
        weights = jnp.maximum(weights - 0.5 * gradient, 0.0)
        if step < ITERS - 1:
            pieces = gather_weights(weights)

    mine = jnp.stack([weights, gradient])
    other = over_rep(mine)
    both = jnp.concatenate(
        [jnp.where(core == 0, mine, other), jnp.where(core == 0, other, mine)], axis=1
    )
    both = both.transpose(0, 2, 1, 3).reshape(2, weightings, 1, chunk_spots)
    return both[0], both[1]


def solution(mesh):
    placed = (
        P(("groups", "vox"), "spot", "rep", None, None),
        P(("groups", "vox"), "spot", "rep"),
        P(("groups", "vox"), "spot", "rep"),
        P(("groups", "vox"), "spot"),
        P(("groups", "vox", "spot", "rep")),
        P("groups"),
        P("groups"),
        P("groups"),
        P("groups"),
        P("groups", "spot", "vox"),
    )
    sizes = tuple(mesh.shape[a] for a in ("vox", "spot"))
    return jax.shard_map(
        functools.partial(per_device, sizes),
        mesh=mesh,
        in_specs=placed,
        out_specs=(P("groups", "spot", "vox"), P("groups", "spot", "vox")),
        check_vma=False,
    )
```

```python
import functools

import jax
import jax.numpy as jnp
from jax import lax
from jax.experimental import pallas as pl
from jax.experimental.pallas import tpu as pltpu
from jax.sharding import PartitionSpec as P

ITERS = 4
F32 = jnp.float32
BF16 = jnp.bfloat16
PARAMS = pltpu.CompilerParams(vmem_limit_bytes=8 * 2**20)


def in_vmem():
    return pl.BlockSpec(memory_space=pltpu.VMEM)


def in_smem():
    return pl.BlockSpec(memory_space=pltpu.SMEM)


def held(array):
    return pltpu.with_memory_space_constraint(array, pltpu.VMEM)


def load_kernel(n_vox, columns, row0, me, cols, exps, live, stored, kept, turned, index, places, factor, sems):
    z, core = me[0], me[1]
    slots = cols.shape[2]
    rows = kept.shape[0] // slots
    own = columns // (2 * n_vox)
    copies = [
        pltpu.make_async_copy(
            stored.at[pl.ds((row0 + b) * slots, slots)], kept.at[pl.ds(b * slots, slots)], sems.at[b]
        )
        for b in range(rows)
    ]
    for copy in copies:
        copy.start()
    step = 8 if slots % 8 == 0 else 1
    for b, copy in enumerate(copies):
        copy.wait()
        used_slots = live[row0 + b, 0] - core * slots

        def turn(t, carry, b=b, used_slots=used_slots):
            for u in range(step):
                k = t * step + u
                n = b * slots + k
                turned[n] = kept[n].T
                column, exponent = cols[row0 + b, 0, k], exps[row0 + b, 0, k]
                piece, within = column // own, column % own
                at = (((piece % 2) ^ core) * n_vox + ((piece // 2) ^ z)) * own + within
                used = k < used_slots
                scale = jnp.where(exponent < 0, 0.5, jnp.where(exponent > 0, 2.0, 1.0))
                places[n] = at
                index[n] = jnp.where(used, (exponent + 1) * columns + at, 3 * columns)
                factor[n] = jnp.where(used, scale, 0.0).astype(F32)
            return carry

        lax.fori_loop(0, slots // step, turn, 0)


def load_matrix(n_vox, columns, row0, rows, me, cols, exps, live, tiles):
    slots = cols.shape[2]
    shape = (rows * slots,) + tiles.shape[1:]
    return pl.pallas_call(
        functools.partial(load_kernel, n_vox, columns, row0),
        in_specs=[in_smem()] * 4 + [pl.BlockSpec(memory_space=pltpu.HBM)],
        out_specs=[in_vmem()] * 2 + [in_smem()] * 3,
        out_shape=[pltpu.VMEM(shape, tiles.dtype)] * 2
        + [jax.ShapeDtypeStruct(shape[:1], t) for t in (jnp.int32, jnp.int32, F32)],
        scratch_shapes=[pltpu.SemaphoreType.DMA((rows,))],
        compiler_params=PARAMS,
        cost_estimate=pl.CostEstimate(
            flops=0, bytes_accessed=8 * rows * slots * tiles.shape[1] * tiles.shape[2], transcendentals=0
        ),
        name="load_matrix",
    )(me, *(pltpu.with_memory_space_constraint(a, pltpu.HBM) for a in (cols, exps, live, tiles)))


def forward_kernel(slots, index, *refs):
    pieces, turned, dose, scaled = refs[:-3], refs[-3], refs[-2], refs[-1]
    columns = (scaled.shape[0] - 1) // 3
    at = 0
    for piece in pieces:
        n = piece.shape[0]
        values = piece[...]
        scaled[at : at + n] = values * BF16(0.5)
        scaled[columns + at : columns + at + n] = values
        scaled[2 * columns + at : 2 * columns + at + n] = values * BF16(2.0)
        at += n
    scaled[3 * columns] = jnp.zeros(scaled.shape[1:], BF16)
    rows = dose.shape[0]
    unroll = 4 if rows % 4 == 0 else 1

    def some_rows(t, carry):
        for u in range(unroll):
            b = t * unroll + u
            left = jnp.concatenate([scaled[index[b * slots + k]] for k in range(slots)], axis=1)
            right = turned[pl.ds(b * slots, slots)]
            right = right.reshape(slots * right.shape[1], right.shape[2])
            dose[b] = jnp.dot(left, right, preferred_element_type=F32)
        return carry

    lax.fori_loop(0, rows // unroll, some_rows, 0)


def forward(index, pieces, turned, rows, slots):
    columns = sum(p.shape[0] for p in pieces)
    weightings, width = pieces[0].shape[1:]
    return pl.pallas_call(
        functools.partial(forward_kernel, slots),
        in_specs=[in_smem()] + [in_vmem()] * (len(pieces) + 1),
        out_specs=in_vmem(),
        out_shape=jax.ShapeDtypeStruct((rows, weightings, width), F32),
        scratch_shapes=[pltpu.VMEM((3 * columns + 1, weightings, width), BF16)],
        compiler_params=PARAMS,
        cost_estimate=pl.CostEstimate(
            flops=2 * rows * slots * weightings * width * width,
            bytes_accessed=2 * rows * slots * width * width,
            transcendentals=0,
        ),
        name="forward",
    )(index, *pieces, held(turned))


def backward_kernel(slots, first, last, index, factor, own, other, levels, kept, *refs):
    *before, slope, total = refs
    dose = own[...] + other[...]
    upper_dose, upper_weight, lower_dose, lower_weight = (levels[i] for i in range(4))
    slope[...] = (
        upper_weight * jax.nn.sigmoid(4.0 * (dose - upper_dose))
        - lower_weight * jax.nn.sigmoid(4.0 * (lower_dose - dose))
    ).astype(BF16)
    total[...] = jnp.zeros_like(total) if first else before.pop(0)[...]
    rows = own.shape[0]
    width = kept.shape[-1]
    unroll = 4 if rows % 4 == 0 else 1
    group = 12 if slots % 12 == 0 else 1

    def some_rows(t, carry):
        for u in range(unroll):
            b = t * unroll + u
            left = slope[b]
            for k0 in range(0, slots, group):
                places = [b * slots + k0 + k for k in range(group)]
                right = jnp.concatenate([kept[p] for p in places], axis=1)
                product = jnp.dot(left, right, preferred_element_type=F32)
                columns = [index[p] for p in places]
                old = [total[c] for c in columns]
                for k, p in enumerate(places):
                    part = product[:, k * width : (k + 1) * width]
                    total[columns[k]] = old[k] + part * factor[p]
        return carry

    lax.fori_loop(0, rows // unroll, some_rows, 0)
    if last:
        far, near = before
        half = near.shape[0]
        near[...] = total[:half]
        far[...] = total[half:]
    else:
        before[0][...] = total[...]


def backward(index, factor, own, other, levels, kept, columns, slots, total, last):
    rows, weightings, width = own.shape
    first = total is None
    out = [(columns // 2, weightings, width)] * 2 if last else [(columns, weightings, width)]
    return pl.pallas_call(
        functools.partial(backward_kernel, slots, first, last),
        in_specs=[in_smem()] * 2 + [in_vmem()] * (4 if first else 5),
        out_specs=[in_vmem()] * len(out),
        out_shape=[jax.ShapeDtypeStruct(shape, F32) for shape in out],
        scratch_shapes=[
            pltpu.VMEM((rows, weightings, width), BF16),
            pltpu.VMEM((columns, weightings, width), F32),
        ],
        compiler_params=PARAMS,
        cost_estimate=pl.CostEstimate(
            flops=2 * rows * slots * weightings * width * width,
            bytes_accessed=2 * rows * slots * width * width,
            transcendentals=0,
        ),
        name="slope_backward",
    )(index, factor, own, other, levels, held(kept), *([] if first else [total]))


def per_device(
    sizes,
    dose_blocks,
    block_cols,
    block_exps,
    live_counts,
    labels,
    upper_dose,
    upper_weight,
    lower_dose,
    lower_weight,
    initial_spot_weights,
):
    n_vox, n_spot = sizes
    z, x, core = (lax.axis_index(a) for a in ("vox", "spot", "rep"))
    rows, _, slots, width, _ = dose_blocks.shape
    weightings, _, chunk_spots = initial_spot_weights.shape
    chunk = chunk_spots // width
    columns = chunk * n_vox
    own = chunk // 2
    initial = initial_spot_weights[:, 0].reshape(weightings, chunk, width)
    weights = lax.dynamic_slice_in_dim(initial, core * own, own, 1).transpose(1, 0, 2)

    def over_vox(arrays):
        return [
            lax.ppermute(a, "vox", [(i, i ^ d) for i in range(n_vox)])
            for d, a in enumerate(arrays, 1)
        ]

    def over_rep(array):
        return lax.ppermute(array, "rep", [(0, 1), (1, 0)])

    me = jnp.stack([z, core]).astype(jnp.int32)
    level_table = jnp.stack([upper_dose, upper_weight, lower_dose, lower_weight])
    known = labels.astype(F32).reshape(-1, width)
    tiles = dose_blocks.reshape(rows * slots, width, width)
    halves = 2 if rows % 2 == 0 else 1
    some = rows // halves

    def load(h):
        return load_matrix(
            n_vox, columns, h * some, some, me, block_cols, block_exps, live_counts, tiles
        )

    def gather_weights(weights):
        piece = weights.astype(BF16)
        return [piece] + over_vox([piece] * (n_vox - 1))

    exchanges = [("rep", 2, 1, core)]
    bit = 1
    while bit < n_spot:
        exchanges.append(("spot", n_spot, bit, x))
        bit *= 2

    pieces = gather_weights(weights)
    parts = [load(0)]
    pieces, first_part = lax.optimization_barrier((pieces, parts[0][2:]))
    parts[0] = [*parts[0][:2], *first_part]
    parts += [load(h) for h in range(1, halves)]

    for step in range(ITERS):
        near = jnp.concatenate(pieces, axis=0)
        weight_halves = [near, over_rep(near)]
        doses = [forward(index, weight_halves, turned, some, slots) for _, turned, index, _, _ in parts]

        own_doses, other_doses = [], []
        for h, dose in enumerate(doses):
            with_labels = step == 0 and h == 0
            for axis, size, bit, at in exchanges:
                sent = dose
                if with_labels:
                    n = known.shape[0]
                    tile = jnp.pad(known, ((0, weightings - n), (0, 0)))
                    sent = jnp.concatenate([dose, tile[None]], axis=0)
                got = lax.ppermute(sent, axis, [(i, i ^ bit) for i in range(size)])
                if with_labels:
                    theirs = got[some, :n]
                    first = (at // bit) % 2 == 0
                    known = jnp.concatenate(
                        [jnp.where(first, known, theirs), jnp.where(first, theirs, known)]
                    )
                    got = got[:some]
                if (axis, bit) != (exchanges[-1][0], exchanges[-1][2]):
                    dose = dose + got
            own_doses.append(dose)
            other_doses.append(got)
        if step == 0:
            levels = jnp.zeros((4, rows, 1, width), F32)
            for c in range(level_table.shape[1]):
                value = level_table[:, c][:, None, None, None]
                levels = jnp.where(known[None, :, None, :] == c, value, levels)

        total = None
        for h, (kept, _, _, places, factor) in enumerate(parts):
            result = backward(
                places,
                factor,
                own_doses[h],
                other_doses[h],
                levels[:, h * some : (h + 1) * some],
                kept,
                columns,
                slots,
                total,
                h == halves - 1,
            )
            total = result[0]
        far, near = result
        near = near + over_rep(far)
        received = over_vox([near[d * own : (d + 1) * own] for d in range(1, n_vox)])
        gradient = near[:own]
        for part in received:
            gradient = gradient + part
        weights = jnp.maximum(weights - 0.5 * gradient, 0.0)
        if step < ITERS - 1:
            pieces = gather_weights(weights)

    mine = jnp.stack([weights, gradient])
    other = over_rep(mine)
    both = jnp.concatenate(
        [jnp.where(core == 0, mine, other), jnp.where(core == 0, other, mine)], axis=1
    )
    both = both.transpose(0, 2, 1, 3).reshape(2, weightings, 1, chunk_spots)
    return both[0], both[1]


def solution(mesh):
    placed = (
        P(("groups", "vox"), "spot", "rep", None, None),
        P(("groups", "vox"), "spot", "rep"),
        P(("groups", "vox"), "spot", "rep"),
        P(("groups", "vox"), "spot"),
        P(("groups", "vox", "spot", "rep")),
        P("groups"),
        P("groups"),
        P("groups"),
        P("groups"),
        P("groups", "spot", "vox"),
    )
    sizes = tuple(mesh.shape[a] for a in ("vox", "spot"))
    return jax.shard_map(
        functools.partial(per_device, sizes),
        mesh=mesh,
        in_specs=placed,
        out_specs=(P("groups", "spot", "vox"), P("groups", "spot", "vox")),
        check_vma=False,
    )
```

```python
import functools

import jax
import jax.numpy as jnp
from jax import lax
from jax.experimental import pallas as pl
from jax.experimental.pallas import tpu as pltpu
from jax.sharding import PartitionSpec as P

ITERS = 4
F32 = jnp.float32
BF16 = jnp.bfloat16
PARAMS = pltpu.CompilerParams(vmem_limit_bytes=16 * 2**20)


def in_vmem():
    return pl.BlockSpec(memory_space=pltpu.VMEM)


def in_smem():
    return pl.BlockSpec(memory_space=pltpu.SMEM)


def held(array):
    return pltpu.with_memory_space_constraint(array, pltpu.VMEM)


def index_kernel(n_vox, columns, steps, me, cols, exps, live, index, places, factor, sides):
    z, core = me[0], me[1]
    slots = cols.shape[2]
    own = columns // (2 * n_vox)
    column, exponent = cols[:, 0, :], exps[:, 0, :]
    piece, within = lax.div(column, own), lax.rem(column, own)
    place = ((lax.rem(piece, 2) ^ core) * n_vox + (lax.div(piece, 2) ^ z)) * own + within
    position = core * slots + lax.broadcasted_iota(jnp.int32, column.shape, 1)
    used = position < live[...]
    scale = jnp.where(exponent < 0, 0.5, jnp.where(exponent > 0, 2.0, 1.0))
    places[...] = place
    index[...] = jnp.where(used, (exponent + 1) * columns + place, 3 * columns)
    factor[...] = jnp.where(used, scale, 0.0).astype(F32)
    for e, (at, bit) in enumerate(steps):
        first = jnp.where((me[at] & bit) == 0, 1.0, 0.0).astype(F32)
        sides[e] = jnp.full(sides.shape[1:], first)


def indices(n_vox, columns, steps, me, cols, exps, live):
    rows, _, slots = cols.shape
    return pl.pallas_call(
        functools.partial(index_kernel, n_vox, columns, steps),
        in_specs=[in_smem()] + [in_vmem()] * 3,
        out_specs=[in_vmem()] * 4,
        out_shape=[jax.ShapeDtypeStruct((rows, slots), t) for t in (jnp.int32, jnp.int32, F32)]
        + [jax.ShapeDtypeStruct((len(steps), 8, 128), F32)],
        compiler_params=PARAMS,
        name="indices",
    )(me, cols, exps, live)


def load_kernel(first, stored, after, kept, turned, sems):
    pieces = sems.shape[0]
    size = kept.shape[0] // pieces
    copies = [
        pltpu.make_async_copy(
            stored.at[pl.ds(first + i * size, size)], kept.at[pl.ds(i * size, size)], sems.at[i]
        )
        for i in range(pieces)
    ]
    for copy in copies:
        copy.start()
    step = 8 if size % 8 == 0 else 1
    for i, copy in enumerate(copies):
        copy.wait()

        def turn(t, carry, i=i):
            for u in range(step):
                n = i * size + t * step + u
                turned[n] = kept[n].T
            return carry

        lax.fori_loop(0, size // step, turn, 0)


def load_matrix(first, count, pieces, tiles, after):
    shape = (count,) + tiles.shape[1:]
    return pl.pallas_call(
        functools.partial(load_kernel, first),
        in_specs=[pl.BlockSpec(memory_space=pltpu.HBM), in_vmem()],
        out_specs=[in_vmem()] * 2,
        out_shape=[pltpu.VMEM(shape, tiles.dtype)] * 2,
        scratch_shapes=[pltpu.SemaphoreType.DMA((pieces,))],
        compiler_params=PARAMS,
        cost_estimate=pl.CostEstimate(
            flops=0, bytes_accessed=8 * count * tiles.shape[1] * tiles.shape[2], transcendentals=0
        ),
        name="load_matrix",
    )(pltpu.with_memory_space_constraint(tiles, pltpu.HBM), after)


def forward_kernel(slots, index, *refs):
    pieces, turned, dose, scaled = refs[:-3], refs[-3], refs[-2], refs[-1]
    columns = (scaled.shape[0] - 1) // 3
    at = 0
    for piece in pieces:
        n = piece.shape[0]
        values = piece[...]
        scaled[at : at + n] = values * BF16(0.5)
        scaled[columns + at : columns + at + n] = values
        scaled[2 * columns + at : 2 * columns + at + n] = values * BF16(2.0)
        at += n
    scaled[3 * columns] = jnp.zeros(scaled.shape[1:], BF16)
    rows = dose.shape[0]
    unroll = 4 if rows % 4 == 0 else 1

    def some_rows(t, carry):
        for u in range(unroll):
            b = t * unroll + u
            left = jnp.concatenate([scaled[index[b, k]] for k in range(slots)], axis=1)
            right = turned[pl.ds(b * slots, slots)]
            right = right.reshape(slots * right.shape[1], right.shape[2])
            dose[b] = jnp.dot(left, right, preferred_element_type=F32)
        return carry

    lax.fori_loop(0, rows // unroll, some_rows, 0)


def forward(index, pieces, turned, rows, slots):
    columns = sum(p.shape[0] for p in pieces)
    weightings, width = pieces[0].shape[1:]
    return pl.pallas_call(
        functools.partial(forward_kernel, slots),
        in_specs=[in_smem()] + [in_vmem()] * (len(pieces) + 1),
        out_specs=in_vmem(),
        out_shape=jax.ShapeDtypeStruct((rows, weightings, width), F32),
        scratch_shapes=[pltpu.VMEM((3 * columns + 1, weightings, width), BF16)],
        compiler_params=PARAMS,
        cost_estimate=pl.CostEstimate(
            flops=2 * rows * slots * weightings * width * width,
            bytes_accessed=2 * rows * slots * width * width,
            transcendentals=0,
        ),
        name="forward",
    )(index, *pieces, held(turned))


def backward_kernel(slots, first, last, index, factor, own, other, levels, kept, *refs):
    *before, slope, total = refs
    dose = own[...] + other[...]
    upper_dose, upper_weight, lower_dose, lower_weight = (levels[i] for i in range(4))
    slope[...] = (
        upper_weight * jax.nn.sigmoid(4.0 * (dose - upper_dose))
        - lower_weight * jax.nn.sigmoid(4.0 * (lower_dose - dose))
    ).astype(BF16)
    total[...] = jnp.zeros_like(total) if first else before.pop(0)[...]
    rows = own.shape[0]
    width = kept.shape[-1]
    unroll = 4 if rows % 4 == 0 else 1
    group = 12 if slots % 12 == 0 else 1

    def some_rows(t, carry):
        for u in range(unroll):
            b = t * unroll + u
            left = slope[b]
            for k0 in range(0, slots, group):
                places = [b * slots + k0 + k for k in range(group)]
                right = jnp.concatenate([kept[p] for p in places], axis=1)
                product = jnp.dot(left, right, preferred_element_type=F32)
                columns = [index[b, k0 + k] for k in range(group)]
                old = [total[c] for c in columns]
                for k in range(group):
                    part = product[:, k * width : (k + 1) * width]
                    total[columns[k]] = old[k] + part * factor[b, k0 + k]
        return carry

    lax.fori_loop(0, rows // unroll, some_rows, 0)
    if last:
        far, near = before
        half = near.shape[0]
        near[...] = total[:half]
        far[...] = total[half:]
    else:
        before[0][...] = total[...]


def backward(index, factor, own, other, levels, kept, columns, slots, total, last):
    rows, weightings, width = own.shape
    first = total is None
    out = [(columns // 2, weightings, width)] * 2 if last else [(columns, weightings, width)]
    return pl.pallas_call(
        functools.partial(backward_kernel, slots, first, last),
        in_specs=[in_smem()] * 2 + [in_vmem()] * (4 if first else 5),
        out_specs=[in_vmem()] * len(out),
        out_shape=[jax.ShapeDtypeStruct(shape, F32) for shape in out],
        scratch_shapes=[
            pltpu.VMEM((rows, weightings, width), BF16),
            pltpu.VMEM((columns, weightings, width), F32),
        ],
        compiler_params=PARAMS,
        cost_estimate=pl.CostEstimate(
            flops=2 * rows * slots * weightings * width * width,
            bytes_accessed=2 * rows * slots * width * width,
            transcendentals=0,
        ),
        name="slope_backward",
    )(index, factor, own, other, levels, held(kept), *([] if first else [total]))


def per_device(
    sizes,
    dose_blocks,
    block_cols,
    block_exps,
    live_counts,
    labels,
    upper_dose,
    upper_weight,
    lower_dose,
    lower_weight,
    initial_spot_weights,
):
    n_vox, n_spot = sizes
    z, x, core = (lax.axis_index(a) for a in ("vox", "spot", "rep"))
    rows, _, slots, width, _ = dose_blocks.shape
    weightings, _, chunk_spots = initial_spot_weights.shape
    chunk = chunk_spots // width
    columns = chunk * n_vox
    own = chunk // 2
    initial = initial_spot_weights[:, 0].reshape(weightings, chunk, width)
    weights = lax.dynamic_slice_in_dim(initial, core * own, own, 1).transpose(1, 0, 2)

    def over_vox(arrays):
        return [
            lax.ppermute(a, "vox", [(i, i ^ d) for i in range(n_vox)])
            for d, a in enumerate(arrays, 1)
        ]

    def over_rep(array):
        return lax.ppermute(array, "rep", [(0, 1), (1, 0)])

    me = jnp.stack([z, core, x]).astype(jnp.int32)
    level_table = jnp.stack([upper_dose, upper_weight, lower_dose, lower_weight])
    known = labels.astype(F32).reshape(-1, width)
    tiles = dose_blocks.reshape(rows * slots, width, width)
    halves = 2 if rows % 2 == 0 else 1
    some = rows // halves

    def gather_weights(weights):
        piece = weights.astype(BF16)
        return [piece] + over_vox([piece] * (n_vox - 1))

    exchanges = [("rep", 2, 1)]
    bit = 1
    while bit < n_spot:
        exchanges.append(("spot", n_spot, bit))
        bit *= 2

    pieces = gather_weights(weights)
    steps = [(1 if axis == "rep" else 2, bit) for axis, _, bit in exchanges]
    index, places, factor, sides = indices(
        n_vox, columns, steps, me, block_cols, block_exps, live_counts
    )
    count = some * slots
    loaded = [load_matrix(0, count, some, tiles, index)]
    pieces, loaded[0] = lax.optimization_barrier((pieces, loaded[0]))
    loaded += [load_matrix(h * count, count, some, tiles, index) for h in range(1, halves)]
    parts = []
    for h, (kept, turned) in enumerate(loaded):
        parts.append((kept, turned, *(a[h * some : (h + 1) * some] for a in (index, places, factor))))

    for step in range(ITERS):
        near = jnp.concatenate(pieces, axis=0)
        weight_halves = [near, over_rep(near)]
        doses = [forward(index, weight_halves, turned, some, slots) for _, turned, index, _, _ in parts]

        own_doses, other_doses = [], []
        for h, dose in enumerate(doses):
            with_labels = step == 0 and h == 0
            for e, (axis, size, bit) in enumerate(exchanges):
                sent = dose
                if with_labels:
                    n = known.shape[0]
                    tile = jnp.pad(known, ((0, weightings - n), (0, 0)))
                    sent = jnp.concatenate([dose, tile[None]], axis=0)
                got = lax.ppermute(sent, axis, [(i, i ^ bit) for i in range(size)])
                if with_labels:
                    theirs = got[some, :n]
                    first = sides[e, :1] > 0
                    known = jnp.concatenate(
                        [jnp.where(first, known, theirs), jnp.where(first, theirs, known)]
                    )
                    got = got[:some]
                if e < len(exchanges) - 1:
                    dose = dose + got
            own_doses.append(dose)
            other_doses.append(got)
        if step == 0:
            levels = jnp.zeros((4, rows, 1, width), F32)
            for c in range(level_table.shape[1]):
                value = level_table[:, c][:, None, None, None]
                levels = jnp.where(known[None, :, None, :] == c, value, levels)

        total = None
        for h, (kept, _, _, places, factor) in enumerate(parts):
            result = backward(
                places,
                factor,
                own_doses[h],
                other_doses[h],
                levels[:, h * some : (h + 1) * some],
                kept,
                columns,
                slots,
                total,
                h == halves - 1,
            )
            total = result[0]
        far, near = result
        near = near + over_rep(far)
        received = over_vox([near[d * own : (d + 1) * own] for d in range(1, n_vox)])
        gradient = near[:own]
        for part in received:
            gradient = gradient + part
        weights = jnp.maximum(weights - 0.5 * gradient, 0.0)
        if step < ITERS - 1:
            pieces = gather_weights(weights)

    mine = jnp.stack([weights, gradient])
    other = over_rep(mine)
    first = sides[0, :1] > 0
    both = jnp.concatenate(
        [jnp.where(first, mine, other), jnp.where(first, other, mine)], axis=1
    )
    both = both.transpose(0, 2, 1, 3).reshape(2, weightings, 1, chunk_spots)
    return both[0], both[1]


def solution(mesh):
    placed = (
        P(("groups", "vox"), "spot", "rep", None, None),
        P(("groups", "vox"), "spot", "rep"),
        P(("groups", "vox"), "spot", "rep"),
        P(("groups", "vox"), "spot"),
        P(("groups", "vox", "spot", "rep")),
        P("groups"),
        P("groups"),
        P("groups"),
        P("groups"),
        P("groups", "spot", "vox"),
    )
    sizes = tuple(mesh.shape[a] for a in ("vox", "spot"))
    return jax.shard_map(
        functools.partial(per_device, sizes),
        mesh=mesh,
        in_specs=placed,
        out_specs=(P("groups", "spot", "vox"), P("groups", "spot", "vox")),
        check_vma=False,
    )
```

```python
import functools

import jax
import jax.numpy as jnp
from jax import lax
from jax.experimental import pallas as pl
from jax.experimental.pallas import tpu as pltpu
from jax.sharding import PartitionSpec as P

ITERS = 4
F32 = jnp.float32
BF16 = jnp.bfloat16
PARAMS = pltpu.CompilerParams(vmem_limit_bytes=16 * 2**20)


def in_vmem():
    return pl.BlockSpec(memory_space=pltpu.VMEM)


def in_smem():
    return pl.BlockSpec(memory_space=pltpu.SMEM)


def held(array):
    return pltpu.with_memory_space_constraint(array, pltpu.VMEM)


def index_kernel(n_vox, columns, runs, steps, me, cols, exps, live, *outs):
    z, core = me[0], me[1]
    rows, _, slots = cols.shape
    own = columns // (2 * n_vox)
    column, exponent = cols[:, 0, :], exps[:, 0, :]
    piece, within = lax.div(column, own), lax.rem(column, own)
    place = ((lax.rem(piece, 2) ^ core) * n_vox + (lax.div(piece, 2) ^ z)) * own + within
    scale = jnp.where(exponent < 0, 0.5, jnp.where(exponent > 0, 2.0, 1.0))
    scaled = (exponent + 1) * columns + place
    position = core * slots + lax.broadcasted_iota(jnp.int32, (1, slots), 1)
    n = rows // (2 * runs)
    for half in range(2):
        index, places, factor = outs[3 * half : 3 * half + 3]
        for r in range(rows // 2):
            first = 2 * n * (r // n) + r % n
            low, high = (first, first + n) if half == 0 else (first + n, first)

            def row(array):
                return jnp.where(core == 0, array[low : low + 1], array[high : high + 1])

            used = position < jnp.where(core == 0, live[low], live[high])
            places[r : r + 1] = row(place)
            index[r : r + 1] = jnp.where(used, row(scaled), 3 * columns)
            factor[r : r + 1] = jnp.where(used, row(scale), 0.0).astype(F32)
    sides = outs[-1]
    for e, (at, bit) in enumerate(steps):
        side = jnp.where((me[at] & bit) == 0, 1.0, 0.0).astype(F32)
        sides[e] = jnp.full(sides.shape[1:], side)


def indices(n_vox, columns, runs, steps, me, cols, exps, live):
    rows, _, slots = cols.shape
    out = [jax.ShapeDtypeStruct((rows // 2, slots), t) for t in (jnp.int32, jnp.int32, F32)] * 2
    out.append(jax.ShapeDtypeStruct((len(steps), 8, 128), F32))
    return pl.pallas_call(
        functools.partial(index_kernel, n_vox, columns, runs, steps),
        in_specs=[in_smem()] + [in_vmem()] * 2 + [in_smem()],
        out_specs=[in_vmem()] * len(out),
        out_shape=out,
        compiler_params=PARAMS,
        name="indices",
    )(me, *(pltpu.with_memory_space_constraint(a, pltpu.HBM) for a in (cols, exps)), live)


def turn_kernel(kept, after, turned):
    count = kept.shape[0]
    step = 8 if count % 8 == 0 else 1

    def some(t, carry):
        for u in range(step):
            turned[t * step + u] = kept[t * step + u].T
        return carry

    lax.fori_loop(0, count // step, some, 0)


def turn(kept, after):
    return pl.pallas_call(
        turn_kernel,
        in_specs=[in_vmem(), pl.BlockSpec(memory_space=pl.ANY)],
        out_specs=in_vmem(),
        out_shape=pltpu.VMEM(kept.shape, kept.dtype),
        compiler_params=PARAMS,
        cost_estimate=pl.CostEstimate(flops=0, bytes_accessed=4 * kept.size, transcendentals=0),
        name="turn",
    )(held(kept), after)


def scale_weights(pieces, scaled):
    columns = (scaled.shape[0] - 1) // 3
    at = 0
    for piece in pieces:
        n = piece.shape[0]
        values = piece[...]
        scaled[at : at + n] = values * BF16(0.5)
        scaled[columns + at : columns + at + n] = values
        scaled[2 * columns + at : 2 * columns + at + n] = values * BF16(2.0)
        at += n
    scaled[3 * columns] = jnp.zeros(scaled.shape[1:], BF16)


def row_copies(mine, runs, slots, me, stored, kept, sems):
    rows = sems.shape[0]
    n = rows // runs
    half = me[1] if mine else 1 - me[1]
    return [
        pltpu.make_async_copy(
            stored.at[pl.ds(((2 * (b // n) + half) * n + b % n) * slots, slots)],
            kept.at[pl.ds(b * slots, slots)],
            sems.at[b],
        )
        for b in range(rows)
    ]


def load_kernel(slots, runs, me, stored, after, kept, sems):
    copies = row_copies(False, runs, slots, me, stored, kept, sems)
    for copy in copies:
        copy.start()
    for copy in copies:
        copy.wait()


def load_others(rows, runs, me, tiles, after):
    shape = (tiles.shape[0] // 2,) + tiles.shape[1:]
    return pl.pallas_call(
        functools.partial(load_kernel, tiles.shape[0] // rows, runs),
        in_specs=[in_smem(), pl.BlockSpec(memory_space=pltpu.HBM), in_vmem()],
        out_specs=in_vmem(),
        out_shape=pltpu.VMEM(shape, tiles.dtype),
        scratch_shapes=[pltpu.SemaphoreType.DMA((rows // 2,))],
        compiler_params=PARAMS,
        cost_estimate=pl.CostEstimate(flops=0, bytes_accessed=2 * tiles.size, transcendentals=0),
        name="load_others",
    )(me, pltpu.with_memory_space_constraint(tiles, pltpu.HBM), after)


def first_forward_kernel(slots, runs, me, index_others, index_mine, *refs):
    pieces, (kept_others, stored, given, dose, kept_mine, scaled, sems) = refs[:-7], refs[-7:]
    copies = row_copies(True, runs, slots, me, stored, kept_mine, sems)
    for copy in copies:
        copy.start()
    scale_weights(pieces, scaled)
    rows = dose.shape[0]
    unroll = 4 if rows % 4 == 0 else 1
    for index, kept, out in ((index_others, kept_others, given), (index_mine, kept_mine, dose)):
        for t in range(rows // unroll):
            if kept is kept_mine:
                for u in range(unroll):
                    copies[t * unroll + u].wait()
            for u in range(unroll):
                b = t * unroll + u
                left = jnp.concatenate([scaled[index[b, k]] for k in range(slots)], axis=1)
                right = jnp.concatenate([kept[b * slots + k] for k in range(slots)], axis=1)
                out[b] = lax.dot_general(
                    left, right, (((1,), (1,)), ((), ())), preferred_element_type=F32
                )


def forward_kernel(slots, index, *refs):
    pieces, turned, dose, scaled = refs[:-3], refs[-3], refs[-2], refs[-1]
    scale_weights(pieces, scaled)
    rows = dose.shape[0]
    unroll = 4 if rows % 4 == 0 else 1

    def some_rows(t, carry):
        for u in range(unroll):
            b = t * unroll + u
            left = jnp.concatenate([scaled[index[b, k]] for k in range(slots)], axis=1)
            right = turned[pl.ds(b * slots, slots)]
            right = right.reshape(slots * right.shape[1], right.shape[2])
            dose[b] = jnp.dot(left, right, preferred_element_type=F32)
        return carry

    lax.fori_loop(0, rows // unroll, some_rows, 0)


def work_of(rows, slots, weightings, width):
    return pl.CostEstimate(
        flops=2 * rows * slots * weightings * width * width,
        bytes_accessed=2 * rows * slots * width * width,
        transcendentals=0,
    )


def forward(index, pieces, turned):
    columns = sum(p.shape[0] for p in pieces)
    weightings, width = pieces[0].shape[1:]
    rows, slots = index.shape
    return pl.pallas_call(
        functools.partial(forward_kernel, slots),
        in_specs=[in_smem()] + [in_vmem()] * (len(pieces) + 1),
        out_specs=in_vmem(),
        out_shape=jax.ShapeDtypeStruct((rows, weightings, width), F32),
        scratch_shapes=[pltpu.VMEM((3 * columns + 1, weightings, width), BF16)],
        compiler_params=PARAMS,
        cost_estimate=work_of(rows, slots, weightings, width),
        name="forward",
    )(index, *pieces, held(turned))


def first_forward(runs, me, index_others, index_mine, pieces, kept_others, tiles):
    columns = sum(p.shape[0] for p in pieces)
    weightings, width = pieces[0].shape[1:]
    rows, slots = index_mine.shape
    part = jax.ShapeDtypeStruct((rows, weightings, width), F32)
    return pl.pallas_call(
        functools.partial(first_forward_kernel, slots, runs),
        in_specs=[in_smem()] * 3
        + [in_vmem()] * (len(pieces) + 1)
        + [pl.BlockSpec(memory_space=pltpu.HBM)],
        out_specs=[in_vmem()] * 3,
        out_shape=[part, part, pltpu.VMEM((rows * slots, width, width), BF16)],
        scratch_shapes=[
            pltpu.VMEM((3 * columns + 1, weightings, width), BF16),
            pltpu.SemaphoreType.DMA((rows,)),
        ],
        compiler_params=PARAMS,
        cost_estimate=work_of(2 * rows, slots, weightings, width),
        name="first_forward",
    )(
        me,
        index_others,
        index_mine,
        *pieces,
        held(kept_others),
        pltpu.with_memory_space_constraint(tiles, pltpu.HBM),
    )


def backward_kernel(slots, mine, index, factor, slope, kept, *refs):
    *before, total = refs
    total[...] = jnp.zeros_like(total) if mine else before.pop(0)[...]
    width = kept.shape[-1]
    group = 12 if slots % 12 == 0 else 1
    rows = slope.shape[0]
    unroll = 4 if rows % 4 == 0 else 1

    def some_rows(t, carry):
        for u in range(unroll):
            b = t * unroll + u
            left = slope[b]
            for k0 in range(0, slots, group):
                right = jnp.concatenate([kept[b * slots + k0 + k] for k in range(group)], axis=1)
                product = jnp.dot(left, right, preferred_element_type=F32)
                columns = [index[b, k0 + k] for k in range(group)]
                old = [total[c] for c in columns]
                for k in range(group):
                    part = product[:, k * width : (k + 1) * width]
                    total[columns[k]] = old[k] + part * factor[b, k0 + k]
        return carry

    lax.fori_loop(0, rows // unroll, some_rows, 0)
    if mine:
        before[0][...] = total[...]
    else:
        far, near = before
        half = near.shape[0]
        near[...] = total[:half]
        far[...] = total[half:]


def backward(mine, index, factor, slope, kept, columns, *total):
    half_rows, weightings, width = slope.shape
    slots = index.shape[1]
    out = [(columns, weightings, width)] if mine else [(columns // 2, weightings, width)] * 2
    return pl.pallas_call(
        functools.partial(backward_kernel, slots, mine),
        in_specs=[in_smem()] * 2 + [in_vmem()] * (2 + len(total)),
        out_specs=[in_vmem()] * len(out),
        out_shape=[jax.ShapeDtypeStruct(shape, F32) for shape in out],
        scratch_shapes=[pltpu.VMEM((columns, weightings, width), F32)],
        compiler_params=PARAMS,
        cost_estimate=work_of(half_rows, slots, weightings, width),
        name="backward",
    )(index, factor, slope, held(kept), *total)


def per_device(
    sizes,
    dose_blocks,
    block_cols,
    block_exps,
    live_counts,
    labels,
    upper_dose,
    upper_weight,
    lower_dose,
    lower_weight,
    initial_spot_weights,
):
    n_vox, n_spot = sizes
    z, x, core = (lax.axis_index(a) for a in ("vox", "spot", "rep"))
    rows, _, slots, width, _ = dose_blocks.shape
    weightings, _, chunk_spots = initial_spot_weights.shape
    chunk = chunk_spots // width
    columns = chunk * n_vox
    own = chunk // 2
    initial = initial_spot_weights[:, 0].reshape(weightings, chunk, width)
    weights = lax.dynamic_slice_in_dim(initial, core * own, own, 1).transpose(1, 0, 2)

    def over_vox(arrays):
        return [
            lax.ppermute(a, "vox", [(i, i ^ d) for i in range(n_vox)])
            for d, a in enumerate(arrays, 1)
        ]

    def over_rep(array):
        return lax.ppermute(array, "rep", [(0, 1), (1, 0)])

    me = jnp.stack([z, core, x]).astype(jnp.int32)
    level_table = jnp.stack([upper_dose, upper_weight, lower_dose, lower_weight])
    known = labels.astype(F32).reshape(-1, width)
    tiles = dose_blocks.reshape(rows * slots, width, width)

    def gather_weights(weights):
        piece = weights.astype(BF16)
        return [piece] + over_vox([piece] * (n_vox - 1))

    bits = [1 << i for i in range(n_spot.bit_length() - 1)]
    *tables, sides = indices(
        n_vox,
        columns,
        n_spot,
        [(1, 1)] + [(2, bit) for bit in bits],
        me,
        block_cols,
        block_exps,
        live_counts.reshape(rows),
    )
    mine, others = tables[:3], tables[3:]
    pieces = gather_weights(weights)
    kept_others = load_others(rows, n_spot, me, tiles, sides)
    pieces, kept_others = lax.optimization_barrier((pieces, kept_others))

    for step in range(ITERS):
        near = jnp.concatenate(pieces, axis=0)
        weight_halves = [near, over_rep(near)]
        if step == 0:
            given, dose, kept_mine = first_forward(
                n_spot, me, others[0], mine[0], weight_halves, kept_others, tiles
            )
        else:
            given = forward(others[0], weight_halves, turned_others)
            dose = forward(mine[0], weight_halves, turned_mine)
        dose = dose + over_rep(given)
        for e, bit in enumerate(bits, 1):
            sent = dose
            if step == 0:
                n = known.shape[0]
                tile = jnp.pad(known, ((0, weightings - n), (0, 0)))
                sent = jnp.concatenate([dose, tile[None]], axis=0)
            got = lax.ppermute(sent, "spot", [(i, i ^ bit) for i in range(n_spot)])
            if step == 0:
                theirs = got[rows // 2, :n]
                first = sides[e, :1] > 0
                known = jnp.concatenate(
                    [jnp.where(first, known, theirs), jnp.where(first, theirs, known)]
                )
                got = got[: rows // 2]
            dose = dose + got
        if step == 0:
            levels = jnp.zeros((4, rows // 2, 1, width), F32)
            for c in range(level_table.shape[1]):
                value = level_table[:, c][:, None, None, None]
                levels = jnp.where(known[None, :, None, :] == c, value, levels)
        slope = (
            levels[1] * jax.nn.sigmoid(4.0 * (dose - levels[0]))
            - levels[3] * jax.nn.sigmoid(4.0 * (levels[2] - dose))
        ).astype(BF16)
        (total,) = backward(True, *mine[1:], slope, kept_mine, columns)
        far, near = backward(False, *others[1:], over_rep(slope), kept_others, columns, total)
        near = near + over_rep(far)
        received = over_vox([near[d * own : (d + 1) * own] for d in range(1, n_vox)])
        if step == 0:
            turned = [turn(kept_others, near), turn(kept_mine, near)]
            received, turned = lax.optimization_barrier((received, turned))
            turned_others, turned_mine = turned
        gradient = near[:own]
        for part in received:
            gradient = gradient + part
        weights = jnp.maximum(weights - 0.5 * gradient, 0.0)
        if step < ITERS - 1:
            pieces = gather_weights(weights)

    mine = jnp.stack([weights, gradient])
    other = over_rep(mine)
    first = sides[0, :1] > 0
    both = jnp.concatenate(
        [jnp.where(first, mine, other), jnp.where(first, other, mine)], axis=1
    )
    both = both.transpose(0, 2, 1, 3).reshape(2, weightings, 1, chunk_spots)
    return both[0], both[1]


def solution(mesh):
    placed = (
        P(("groups", "vox"), "spot", "rep", None, None),
        P(("groups", "vox"), "spot", "rep"),
        P(("groups", "vox"), "spot", "rep"),
        P(("groups", "vox"), "spot"),
        P(("groups", "vox", "spot", "rep")),
        P("groups"),
        P("groups"),
        P("groups"),
        P("groups"),
        P("groups", "spot", "vox"),
    )
    sizes = tuple(mesh.shape[a] for a in ("vox", "spot"))
    return jax.shard_map(
        functools.partial(per_device, sizes),
        mesh=mesh,
        in_specs=placed,
        out_specs=(P("groups", "spot", "vox"), P("groups", "spot", "vox")),
        check_vma=False,
    )
```

```python
import functools

import jax
import jax.numpy as jnp
from jax import lax
from jax.experimental import pallas as pl
from jax.experimental.pallas import tpu as pltpu
from jax.sharding import PartitionSpec as P

ITERS = 4
F32 = jnp.float32
BF16 = jnp.bfloat16
PARAMS = pltpu.CompilerParams(vmem_limit_bytes=16 * 2**20)


def in_vmem():
    return pl.BlockSpec(memory_space=pltpu.VMEM)


def in_smem():
    return pl.BlockSpec(memory_space=pltpu.SMEM)


def held(array):
    return pltpu.with_memory_space_constraint(array, pltpu.VMEM)


def index_kernel(n_vox, columns, runs, steps, me, cols, exps, live, *outs):
    z, core = me[0], me[1]
    rows, _, slots = cols.shape
    own = columns // (2 * n_vox)
    column, exponent = cols[:, 0, :], exps[:, 0, :]
    piece, within = lax.div(column, own), lax.rem(column, own)
    place = ((lax.rem(piece, 2) ^ core) * n_vox + (lax.div(piece, 2) ^ z)) * own + within
    scale = jnp.where(exponent < 0, 0.5, jnp.where(exponent > 0, 2.0, 1.0))
    scaled = (exponent + 1) * columns + place
    position = core * slots + lax.broadcasted_iota(jnp.int32, (1, slots), 1)
    n = rows // (2 * runs)
    index, places, factor = outs[:3]
    for r in range(rows):
        half, t = divmod(r, rows // 2)
        first = 2 * n * (t // n) + t % n
        low, high = (first, first + n) if half == 0 else (first + n, first)

        def row(array):
            return jnp.where(core == 0, array[low : low + 1], array[high : high + 1])

        used = position < jnp.where(core == 0, live[low], live[high])
        places[r : r + 1] = row(place)
        index[r : r + 1] = jnp.where(used, row(scaled), 3 * columns)
        factor[r : r + 1] = jnp.where(used, row(scale), 0.0).astype(F32)
    sides = outs[-1]
    for e, (at, bit) in enumerate(steps):
        side = jnp.where((me[at] & bit) == 0, 1.0, 0.0).astype(F32)
        sides[e] = jnp.full(sides.shape[1:], side)


def indices(n_vox, columns, runs, steps, me, cols, exps, live):
    rows, _, slots = cols.shape
    out = [jax.ShapeDtypeStruct((rows, slots), t) for t in (jnp.int32, jnp.int32, F32)]
    out.append(jax.ShapeDtypeStruct((len(steps), 8, 128), F32))
    return pl.pallas_call(
        functools.partial(index_kernel, n_vox, columns, runs, steps),
        in_specs=[in_smem()] + [in_vmem()] * 2 + [in_smem()],
        out_specs=[in_vmem()] * len(out),
        out_shape=out,
        compiler_params=PARAMS,
        name="indices",
    )(me, *(pltpu.with_memory_space_constraint(a, pltpu.HBM) for a in (cols, exps)), live)


RUN = 4


def cut_of(slots):
    return 2 * slots // 3


def sort_slots(index, places, factor, columns):
    rows, slots = index.shape
    here = jnp.arange(slots, dtype=jnp.int32)
    dead = factor == 0
    kind = jnp.where(dead, 2, jnp.where(places >= columns // 2, 0, 1))
    key = kind * slots + here
    rank = jnp.sum((key[:, None, :] < key[:, :, None]).astype(jnp.int32), axis=-1)
    chosen = rank[:, None, :] == here[None, :, None]

    def pick(array):
        return jnp.sum(jnp.where(chosen, array[:, None, :], 0), axis=-1)

    row = jnp.arange(rows, dtype=jnp.int32)[:, None] % (rows // 2)
    slot = pick(row * slots + here)
    places = pick(jnp.where(dead, columns + rank, places))
    others = jnp.sum((kind == 0).astype(jnp.int32), axis=1)
    over = jnp.max(others.reshape(-1, RUN), axis=1, keepdims=True) > cut_of(slots)
    over = jnp.broadcast_to(over.astype(jnp.int32), (rows // RUN, 128))
    return slot, pick(index), places, pick(factor), over


def turn_kernel(kept, after, turned):
    count = kept.shape[0]
    step = 8 if count % 8 == 0 else 1

    def some(t, carry):
        for u in range(step):
            turned[t * step + u] = kept[t * step + u].T
        return carry

    lax.fori_loop(0, count // step, some, 0)


def turn(kept, after):
    return pl.pallas_call(
        turn_kernel,
        in_specs=[in_vmem(), pl.BlockSpec(memory_space=pl.ANY)],
        out_specs=in_vmem(),
        out_shape=pltpu.VMEM(kept.shape, kept.dtype),
        compiler_params=PARAMS,
        cost_estimate=pl.CostEstimate(flops=0, bytes_accessed=4 * kept.size, transcendentals=0),
        name="turn",
    )(held(kept), after)


def scale_weights(pieces, scaled):
    columns = (scaled.shape[0] - 1) // 3
    at = 0
    for piece in pieces:
        n = piece.shape[0]
        values = piece[...]
        scaled[at : at + n] = values * BF16(0.5)
        scaled[columns + at : columns + at + n] = values
        scaled[2 * columns + at : 2 * columns + at + n] = values * BF16(2.0)
        at += n
    scaled[3 * columns] = jnp.zeros(scaled.shape[1:], BF16)


def row_operands(chosen, b, slot, index, scaled, blocks):
    left = jnp.concatenate([scaled[index[b, k]] for k in chosen], axis=1)
    return left, [blocks[slot[b, k]] for k in chosen]


def row_copies(mine, runs, slots, me, stored, kept, sems):
    rows = sems.shape[0]
    n = rows // runs
    half = me[1] if mine else 1 - me[1]
    return [
        pltpu.make_async_copy(
            stored.at[pl.ds(((2 * (b // n) + half) * n + b % n) * slots, slots)],
            kept.at[pl.ds(b * slots, slots)],
            sems.at[b],
        )
        for b in range(rows)
    ]


def load_kernel(runs, count, me, stored, *refs):
    tables, kept, me_out, outs, sems, table_sems = (
        refs[:count],
        refs[count],
        refs[count + 1],
        refs[count + 2 : 2 * count + 2],
        refs[-2],
        refs[-1],
    )
    slots = tables[0].shape[1]
    copies = row_copies(False, runs, slots, me, stored, kept, sems)
    copies += [
        pltpu.make_async_copy(table, out, table_sems.at[i])
        for i, (table, out) in enumerate(zip(tables, outs, strict=True))
    ]
    for copy in copies:
        copy.start()
    for i in range(me.shape[0]):
        me_out[i] = me[i]
    for copy in copies:
        copy.wait()


def load_others(runs, me, tables, tiles):
    rows = tables[0].shape[0]
    shape = (tiles.shape[0] // 2,) + tiles.shape[1:]
    return pl.pallas_call(
        functools.partial(load_kernel, runs, len(tables)),
        in_specs=[in_smem(), pl.BlockSpec(memory_space=pltpu.HBM)] + [in_vmem()] * len(tables),
        out_specs=[in_vmem()] + [in_smem()] * (len(tables) + 1),
        out_shape=[pltpu.VMEM(shape, tiles.dtype)]
        + [pltpu.SMEM(t.shape, t.dtype) for t in (me, *tables)],
        scratch_shapes=[
            pltpu.SemaphoreType.DMA((rows // 2,)),
            pltpu.SemaphoreType.DMA((len(tables),)),
        ],
        compiler_params=PARAMS,
        cost_estimate=pl.CostEstimate(flops=0, bytes_accessed=2 * tiles.size, transcendentals=0),
        name="load_others",
    )(me, pltpu.with_memory_space_constraint(tiles, pltpu.HBM), *tables)


def first_forward_kernel(runs, me, slot, index, *refs):
    pieces, (kept_others, stored, given, dose, kept_mine, scaled, sems) = refs[:-7], refs[-7:]
    slots = slot.shape[1]
    copies = row_copies(True, runs, slots, me, stored, kept_mine, sems)
    for copy in copies:
        copy.start()
    scale_weights(pieces, scaled)
    rows = dose.shape[0]
    for kept, out, row0 in ((kept_others, given, rows), (kept_mine, dose, 0)):
        for t in range(0, rows, RUN):
            if kept is kept_mine:
                for b in range(t, t + RUN):
                    copies[b].wait()
            for b in range(t, t + RUN):
                left, blocks = row_operands(range(slots), row0 + b, slot, index, scaled, kept)
                right = jnp.concatenate(blocks, axis=1)
                out[b] = lax.dot_general(
                    left, right, (((1,), (1,)), ((), ())), preferred_element_type=F32
                )


def row_dose(chosen, b, slot, index, scaled, turned):
    left, blocks = row_operands(chosen, b, slot, index, scaled, turned)
    return jnp.dot(left, jnp.concatenate(blocks, axis=0), preferred_element_type=F32)


def near_forward_kernel(slot, index, over, near, turned_mine, turned_others, dose, scaled):
    scale_weights([near], scaled)
    rows, slots = slot.shape
    last = range(cut_of(slots), slots)
    for turned, row0 in ((turned_mine, 0), (turned_others, rows // 2)):

        def run(t, carry, turned=turned, row0=row0):
            b0 = row0 + t * RUN
            skip = over[b0 // RUN, 0] > 0

            @pl.when(skip)
            def _():
                for u in range(RUN):
                    dose[b0 + u] = jnp.zeros(dose.shape[1:], F32)

            @pl.when(jnp.logical_not(skip))
            def _():
                for u in range(RUN):
                    dose[b0 + u] = row_dose(last, b0 + u, slot, index, scaled, turned)

            return carry

        lax.fori_loop(0, rows // 2 // RUN, run, 0)


def forward_kernel(row0, slot, index, over, near, far, turned, part, dose, scaled):
    scale_weights([near, far], scaled)
    slots = slot.shape[1]
    cut = cut_of(slots)

    def run(t, carry):
        b0 = row0 + t * RUN
        for u in range(RUN):
            value = row_dose(range(cut), b0 + u, slot, index, scaled, turned)
            dose[t * RUN + u] = part[b0 + u] + value

        @pl.when(over[b0 // RUN, 0] > 0)
        def _():
            for u in range(RUN):
                dose[t * RUN + u] += row_dose(
                    range(cut, slots), b0 + u, slot, index, scaled, turned
                )

        return carry

    lax.fori_loop(0, dose.shape[0] // RUN, run, 0)


def work_of(rows, slots, weightings, width):
    return pl.CostEstimate(
        flops=2 * rows * slots * weightings * width * width,
        bytes_accessed=2 * rows * slots * width * width,
        transcendentals=0,
    )


def near_forward(tables, near, turned_mine, turned_others):
    half, weightings, width = near.shape
    rows, slots = tables[0].shape
    return pl.pallas_call(
        near_forward_kernel,
        in_specs=[in_smem()] * 3 + [in_vmem()] * 3,
        out_specs=in_vmem(),
        out_shape=jax.ShapeDtypeStruct((rows, weightings, width), F32),
        scratch_shapes=[pltpu.VMEM((6 * half + 1, weightings, width), BF16)],
        compiler_params=PARAMS,
        cost_estimate=work_of(rows, slots - cut_of(slots), weightings, width),
        name="near_forward",
    )(*tables[:2], tables[4], near, held(turned_mine), held(turned_others))


def forward(row0, tables, near, far, turned, part):
    half, weightings, width = near.shape
    rows, slots = tables[0].shape
    return pl.pallas_call(
        functools.partial(forward_kernel, row0),
        in_specs=[in_smem()] * 3 + [in_vmem()] * 4,
        out_specs=in_vmem(),
        out_shape=jax.ShapeDtypeStruct((rows // 2, weightings, width), F32),
        scratch_shapes=[pltpu.VMEM((6 * half + 1, weightings, width), BF16)],
        compiler_params=PARAMS,
        cost_estimate=work_of(rows // 2, cut_of(slots), weightings, width),
        name="forward",
    )(*tables[:2], tables[4], near, far, held(turned), part)


def first_forward(runs, me, tables, pieces, kept_others, tiles):
    columns = sum(p.shape[0] for p in pieces)
    weightings, width = pieces[0].shape[1:]
    rows, slots = tables[0].shape
    rows //= 2
    part = jax.ShapeDtypeStruct((rows, weightings, width), F32)
    return pl.pallas_call(
        functools.partial(first_forward_kernel, runs),
        in_specs=[in_smem()] * 3
        + [in_vmem()] * (len(pieces) + 1)
        + [pl.BlockSpec(memory_space=pltpu.HBM)],
        out_specs=[in_vmem()] * 3,
        out_shape=[part, part, pltpu.VMEM((rows * slots, width, width), BF16)],
        scratch_shapes=[
            pltpu.VMEM((3 * columns + 1, weightings, width), BF16),
            pltpu.SemaphoreType.DMA((rows,)),
        ],
        compiler_params=PARAMS,
        cost_estimate=work_of(2 * rows, slots, weightings, width),
        name="first_forward",
    )(
        me,
        *tables[:2],
        *pieces,
        held(kept_others),
        pltpu.with_memory_space_constraint(tiles, pltpu.HBM),
    )


def add_row(chosen, b, tables, left, kept, total):
    slot, places, factor = tables
    width = kept.shape[-1]
    group = 8 if len(chosen) % 8 == 0 else 1
    for k0 in range(0, len(chosen), group):
        some = chosen[k0 : k0 + group]
        right = jnp.concatenate([kept[slot[b, k]] for k in some], axis=1)
        product = jnp.dot(left, right, preferred_element_type=F32)
        at = [places[b, k] for k in some]
        old = [total[p] for p in at]
        for i, k in enumerate(some):
            total[at[i]] = old[i] + product[:, i * width : (i + 1) * width] * factor[b, k]


def backward_kernel(mine, row0, slot, places, factor, over, slope, kept, *refs):
    *before, total = refs
    columns = total.shape[0] - slot.shape[1]
    total[columns:] = jnp.zeros_like(total[columns:])
    total[:columns] = jnp.zeros_like(total[:columns]) if mine else before.pop(0)[...]
    tables = (slot, places, factor)
    slots = slot.shape[1]
    cut = cut_of(slots)

    def run(t, carry):
        b0 = row0 + t * RUN
        for u in range(RUN):
            add_row(range(cut), b0 + u, tables, slope[t * RUN + u], kept, total)

        @pl.when(over[b0 // RUN, 0] > 0)
        def _():
            for u in range(RUN):
                add_row(range(cut, slots), b0 + u, tables, slope[t * RUN + u], kept, total)

        return carry

    lax.fori_loop(0, slope.shape[0] // RUN, run, 0)
    if mine:
        before[0][...] = total[:columns]
    else:
        far, near = before
        near[...] = total[: columns // 2]
        far[...] = total[columns // 2 : columns]


def near_backward_kernel(
    slot, places, factor, over, slope_mine, slope_others, kept_mine, kept_others, near, out, total
):
    half = near.shape[0]
    total[:half] = near[...]
    total[2 * half :] = jnp.zeros_like(total[2 * half :])
    tables = (slot, places, factor)
    rows, slots = slot.shape
    last = range(cut_of(slots), slots)
    for slope, kept, row0 in ((slope_mine, kept_mine, 0), (slope_others, kept_others, rows // 2)):

        def run(t, carry, slope=slope, kept=kept, row0=row0):
            b0 = row0 + t * RUN

            @pl.when(over[b0 // RUN, 0] == 0)
            def _():
                for u in range(RUN):
                    add_row(last, b0 + u, tables, slope[t * RUN + u], kept, total)

            return carry

        lax.fori_loop(0, rows // 2 // RUN, run, 0)
    out[...] = total[:half]


def backward(mine, row0, tables, slope, kept, columns, *total):
    half_rows, weightings, width = slope.shape
    slots = tables[0].shape[1]
    out = [(columns, weightings, width)] if mine else [(columns // 2, weightings, width)] * 2
    return pl.pallas_call(
        functools.partial(backward_kernel, mine, row0),
        in_specs=[in_smem()] * 4 + [in_vmem()] * (2 + len(total)),
        out_specs=[in_vmem()] * len(out),
        out_shape=[jax.ShapeDtypeStruct(shape, F32) for shape in out],
        scratch_shapes=[pltpu.VMEM((columns + slots, weightings, width), F32)],
        compiler_params=PARAMS,
        cost_estimate=work_of(half_rows, cut_of(slots), weightings, width),
        name="backward",
    )(tables[0], *tables[2:], slope, held(kept), *total)


def near_backward(tables, slope_mine, slope_others, kept_mine, kept_others, near):
    half, weightings, width = near.shape
    rows, slots = tables[0].shape
    return pl.pallas_call(
        near_backward_kernel,
        in_specs=[in_smem()] * 4 + [in_vmem()] * 5,
        out_specs=in_vmem(),
        out_shape=jax.ShapeDtypeStruct(near.shape, F32),
        scratch_shapes=[pltpu.VMEM((2 * half + slots, weightings, width), F32)],
        compiler_params=PARAMS,
        cost_estimate=work_of(rows, slots - cut_of(slots), weightings, width),
        name="near_backward",
    )(tables[0], *tables[2:], slope_mine, slope_others, held(kept_mine), held(kept_others), near)


def per_device(
    sizes,
    dose_blocks,
    block_cols,
    block_exps,
    live_counts,
    labels,
    upper_dose,
    upper_weight,
    lower_dose,
    lower_weight,
    initial_spot_weights,
):
    n_vox, n_spot = sizes
    z, x, core = (lax.axis_index(a) for a in ("vox", "spot", "rep"))
    rows, _, slots, width, _ = dose_blocks.shape
    weightings, _, chunk_spots = initial_spot_weights.shape
    chunk = chunk_spots // width
    columns = chunk * n_vox
    own = chunk // 2
    initial = initial_spot_weights[:, 0].reshape(weightings, chunk, width)
    weights = lax.dynamic_slice_in_dim(initial, core * own, own, 1).transpose(1, 0, 2)

    def over_vox(arrays):
        return [
            lax.ppermute(a, "vox", [(i, i ^ d) for i in range(n_vox)])
            for d, a in enumerate(arrays, 1)
        ]

    def over_rep(array):
        return lax.ppermute(array, "rep", [(0, 1), (1, 0)])

    me = jnp.stack([z, core, x]).astype(jnp.int32)
    level_table = jnp.stack([upper_dose, upper_weight, lower_dose, lower_weight])
    known = labels.astype(F32).reshape(-1, width)
    tiles = dose_blocks.reshape(rows * slots, width, width)

    def gather_weights(weights):
        piece = weights.astype(BF16)
        return [piece] + over_vox([piece] * (n_vox - 1))

    bits = [1 << i for i in range(n_spot.bit_length() - 1)]
    *unsorted, sides = indices(
        n_vox,
        columns,
        n_spot,
        [(1, 1)] + [(2, bit) for bit in bits],
        me,
        block_cols,
        block_exps,
        live_counts.reshape(rows),
    )
    tables = sort_slots(*unsorted, columns)
    pieces = gather_weights(weights)
    kept_others, me, *tables = load_others(n_spot, me, tables, tiles)
    pieces, kept_others = lax.optimization_barrier((pieces, kept_others))

    for step in range(ITERS):
        near = jnp.concatenate(pieces, axis=0)
        other_half = over_rep(near)
        if step == 0:
            given, dose, kept_mine = first_forward(
                n_spot, me, tables, [near, other_half], kept_others, tiles
            )
        else:
            part = near_forward(tables, near, turned_mine, turned_others)
            given = forward(rows // 2, tables, near, other_half, turned_others, part)
            dose = forward(0, tables, near, other_half, turned_mine, part)
        dose = dose + over_rep(given)
        for e, bit in enumerate(bits, 1):
            sent = dose
            if step == 0:
                n = known.shape[0]
                tile = jnp.pad(known, ((0, weightings - n), (0, 0)))
                sent = jnp.concatenate([dose, tile[None]], axis=0)
            got = lax.ppermute(sent, "spot", [(i, i ^ bit) for i in range(n_spot)])
            if step == 0:
                theirs = got[rows // 2, :n]
                first = sides[e, :1] > 0
                known = jnp.concatenate(
                    [jnp.where(first, known, theirs), jnp.where(first, theirs, known)]
                )
                got = got[: rows // 2]
            dose = dose + got
        if step == 0:
            levels = jnp.zeros((4, rows // 2, 1, width), F32)
            for c in range(level_table.shape[1]):
                value = level_table[:, c][:, None, None, None]
                levels = jnp.where(known[None, :, None, :] == c, value, levels)
        slope = (
            levels[1] * jax.nn.sigmoid(4.0 * (dose - levels[0]))
            - levels[3] * jax.nn.sigmoid(4.0 * (levels[2] - dose))
        ).astype(BF16)
        slope_others = over_rep(slope)
        (total,) = backward(True, 0, tables, slope, kept_mine, columns)
        far, near = backward(False, rows // 2, tables, slope_others, kept_others, columns, total)
        theirs = over_rep(far)
        near = near_backward(tables, slope, slope_others, kept_mine, kept_others, near) + theirs
        received = over_vox([near[d * own : (d + 1) * own] for d in range(1, n_vox)])
        if step == 0:
            turned = [turn(kept_others, near), turn(kept_mine, near)]
            received, turned = lax.optimization_barrier((received, turned))
            turned_others, turned_mine = turned
        gradient = near[:own]
        for part in received:
            gradient = gradient + part
        weights = jnp.maximum(weights - 0.5 * gradient, 0.0)
        if step < ITERS - 1:
            pieces = gather_weights(weights)

    mine = jnp.stack([weights, gradient])
    other = over_rep(mine)
    first = sides[0, :1] > 0
    both = jnp.concatenate(
        [jnp.where(first, mine, other), jnp.where(first, other, mine)], axis=1
    )
    both = both.transpose(0, 2, 1, 3).reshape(2, weightings, 1, chunk_spots)
    return both[0], both[1]


def solution(mesh):
    placed = (
        P(("groups", "vox"), "spot", "rep", None, None),
        P(("groups", "vox"), "spot", "rep"),
        P(("groups", "vox"), "spot", "rep"),
        P(("groups", "vox"), "spot"),
        P(("groups", "vox", "spot", "rep")),
        P("groups"),
        P("groups"),
        P("groups"),
        P("groups"),
        P("groups", "spot", "vox"),
    )
    sizes = tuple(mesh.shape[a] for a in ("vox", "spot"))
    return jax.shard_map(
        functools.partial(per_device, sizes),
        mesh=mesh,
        in_specs=placed,
        out_specs=(P("groups", "spot", "vox"), P("groups", "spot", "vox")),
        check_vma=False,
    )
```

```python
import functools

import jax
import jax.numpy as jnp
from jax import lax
from jax.experimental import pallas as pl
from jax.experimental.pallas import tpu as pltpu
from jax.sharding import PartitionSpec as P

ITERS = 4
F32 = jnp.float32
BF16 = jnp.bfloat16
PARAMS = pltpu.CompilerParams(vmem_limit_bytes=16 * 2**20)


def in_vmem():
    return pl.BlockSpec(memory_space=pltpu.VMEM)


def in_smem():
    return pl.BlockSpec(memory_space=pltpu.SMEM)


def held(array):
    return pltpu.with_memory_space_constraint(array, pltpu.VMEM)


RUN = 4


def cut_of(slots):
    return 2 * slots // 3


def index_kernel(n_vox, columns, runs, steps, me, cols, exps, live, after, *refs):
    outs, sides, packed, *tables, sems = refs[:5], *refs[5:]
    z, core = me[0], me[1]
    rows, _, slots = cols.shape
    own = columns // (2 * n_vox)
    column, exponent = cols[:, 0, :], exps[:, 0, :]
    piece, within = lax.div(column, own), lax.rem(column, own)
    place = ((lax.rem(piece, 2) ^ core) * n_vox + (lax.div(piece, 2) ^ z)) * own + within
    both = place * 4 + exponent + 1
    position = core * slots + lax.broadcasted_iota(jnp.int32, (1, slots), 1)
    n = rows // (2 * runs)
    for r in range(rows):
        half, t = divmod(r, rows // 2)
        first = 2 * n * (t // n) + t % n
        low, high = (first, first + n) if half == 0 else (first + n, first)
        row = jnp.where(core == 0, both[low : low + 1], both[high : high + 1])
        used = position < jnp.where(core == 0, live[low], live[high])
        packed[r : r + 1] = jnp.where(used, row, 3)

    both = packed[...]
    here = lax.broadcasted_iota(jnp.int32, (rows, slots), 1)
    dead = lax.rem(both, 4) == 3
    kind = jnp.where(dead, 2, jnp.where(both >= 2 * columns, 0, 1))
    key = kind * slots + here
    rank = jnp.zeros_like(key)
    for k in range(slots):
        rank = rank + jnp.where(key[:, k : k + 1] < key, 1, 0)
    both = jnp.where(dead, (columns + rank) * 4 + 3, both) * 64 + here
    ordered = jnp.zeros_like(key)
    for k in range(slots):
        ordered = ordered + jnp.where(rank[:, k : k + 1] == here, both[:, k : k + 1], 0)
    kind, place = lax.rem(lax.div(ordered, 64), 4), lax.div(ordered, 256)
    slot, index, places, factor, over = tables
    in_half = lax.rem(lax.broadcasted_iota(jnp.int32, (rows, slots), 0), rows // 2)
    slot[...] = in_half * slots + lax.rem(ordered, 64)
    index[...] = jnp.where(kind == 3, 3 * columns, kind * columns + place)
    places[...] = place
    factor[...] = jnp.where(
        kind == 3, 0.0, jnp.where(kind == 0, 0.5, jnp.where(kind == 2, 2.0, 1.0))
    ).astype(F32)
    others = jnp.where((kind != 3) & (place >= columns // 2), 1.0, 0.0).astype(F32)
    others = jnp.sum(others, axis=1, keepdims=True)
    for r in range(rows // RUN):
        most = jnp.max(others[r * RUN : (r + 1) * RUN], axis=0, keepdims=True)
        most = jnp.broadcast_to(most, (1, over.shape[1]))
        over[r : r + 1] = jnp.where(most > cut_of(slots), 1, 0)
    copies = [
        pltpu.make_async_copy(table, out, sems.at[i])
        for i, (table, out) in enumerate(zip(tables, outs, strict=True))
    ]
    for copy in copies:
        copy.start()
    for e, (at, bit) in enumerate(steps):
        side = jnp.where((me[at] & bit) == 0, 1.0, 0.0).astype(F32)
        sides[e] = jnp.full(sides.shape[1:], side)
    for copy in copies:
        copy.wait()


def indices(n_vox, columns, runs, steps, me, cols, exps, live, after):
    rows, _, slots = cols.shape
    shapes = [((rows, slots), t) for t in (jnp.int32, jnp.int32, jnp.int32, F32)]
    shapes.append(((rows // RUN, 128), jnp.int32))
    return pl.pallas_call(
        functools.partial(index_kernel, n_vox, columns, runs, steps),
        in_specs=[in_smem()] + [in_vmem()] * 2 + [in_smem(), pl.BlockSpec(memory_space=pl.ANY)],
        out_specs=[in_smem()] * 5 + [in_vmem()],
        out_shape=[pltpu.SMEM(*shape) for shape in shapes]
        + [jax.ShapeDtypeStruct((len(steps), 8, 128), F32)],
        scratch_shapes=[pltpu.VMEM((rows, slots), jnp.int32)]
        + [pltpu.VMEM(*shape) for shape in shapes]
        + [pltpu.SemaphoreType.DMA((len(shapes),))],
        compiler_params=PARAMS,
        cost_estimate=pl.CostEstimate(flops=0, bytes_accessed=2**21, transcendentals=0),
        name="indices",
    )(me, *(pltpu.with_memory_space_constraint(a, pltpu.HBM) for a in (cols, exps)), live, after)


def turn_kernel(kept, after, turned):
    count = kept.shape[0]
    step = 8 if count % 8 == 0 else 1

    def some(t, carry):
        for u in range(step):
            turned[t * step + u] = kept[t * step + u].T
        return carry

    lax.fori_loop(0, count // step, some, 0)


def turn(kept, after):
    return pl.pallas_call(
        turn_kernel,
        in_specs=[in_vmem(), pl.BlockSpec(memory_space=pl.ANY)],
        out_specs=in_vmem(),
        out_shape=pltpu.VMEM(kept.shape, kept.dtype),
        compiler_params=PARAMS,
        cost_estimate=pl.CostEstimate(flops=0, bytes_accessed=4 * kept.size, transcendentals=0),
        name="turn",
    )(held(kept), after)


def scale_weights(pieces, scaled):
    columns = (scaled.shape[0] - 1) // 3
    at = 0
    for piece in pieces:
        n = piece.shape[0]
        values = piece[...]
        scaled[at : at + n] = values * BF16(0.5)
        scaled[columns + at : columns + at + n] = values
        scaled[2 * columns + at : 2 * columns + at + n] = values * BF16(2.0)
        at += n
    scaled[3 * columns] = jnp.zeros(scaled.shape[1:], BF16)


def row_operands(chosen, b, slot, index, scaled, blocks):
    left = jnp.concatenate([scaled[index[b, k]] for k in chosen], axis=1)
    return left, [blocks[slot[b, k]] for k in chosen]


def row_copies(mine, runs, slots, me, stored, kept, sems):
    rows = sems.shape[0]
    n = rows // runs
    half = me[1] if mine else 1 - me[1]
    return [
        pltpu.make_async_copy(
            stored.at[pl.ds(((2 * (b // n) + half) * n + b % n) * slots, slots)],
            kept.at[pl.ds(b * slots, slots)],
            sems.at[b],
        )
        for b in range(rows)
    ]


def load_kernel(runs, slots, me, stored, kept, me_out, sems):
    copies = row_copies(False, runs, slots, me, stored, kept, sems)
    for copy in copies:
        copy.start()
    for i in range(me.shape[0]):
        me_out[i] = me[i]
    for copy in copies:
        copy.wait()


def load_others(runs, rows, me, tiles):
    shape = (tiles.shape[0] // 2,) + tiles.shape[1:]
    return pl.pallas_call(
        functools.partial(load_kernel, runs, tiles.shape[0] // rows),
        in_specs=[in_smem(), pl.BlockSpec(memory_space=pltpu.HBM)],
        out_specs=[in_vmem(), in_smem()],
        out_shape=[pltpu.VMEM(shape, tiles.dtype), pltpu.SMEM(me.shape, me.dtype)],
        scratch_shapes=[pltpu.SemaphoreType.DMA((rows // 2,))],
        compiler_params=PARAMS,
        cost_estimate=pl.CostEstimate(flops=0, bytes_accessed=2 * tiles.size, transcendentals=0),
        name="load_others",
    )(me, pltpu.with_memory_space_constraint(tiles, pltpu.HBM))


def first_forward_kernel(runs, me, slot, index, *refs):
    pieces, (kept_others, stored, given, dose, kept_mine, scaled, sems) = refs[:-7], refs[-7:]
    slots = slot.shape[1]
    copies = row_copies(True, runs, slots, me, stored, kept_mine, sems)
    for copy in copies:
        copy.start()
    scale_weights(pieces, scaled)
    rows = dose.shape[0]
    for kept, out, row0 in ((kept_others, given, rows), (kept_mine, dose, 0)):
        for t in range(0, rows, RUN):
            if kept is kept_mine:
                for b in range(t, t + RUN):
                    copies[b].wait()
            for b in range(t, t + RUN):
                left, blocks = row_operands(range(slots), row0 + b, slot, index, scaled, kept)
                right = jnp.concatenate(blocks, axis=1)
                out[b] = lax.dot_general(
                    left, right, (((1,), (1,)), ((), ())), preferred_element_type=F32
                )


def row_dose(chosen, b, slot, index, scaled, turned):
    left, blocks = row_operands(chosen, b, slot, index, scaled, turned)
    return jnp.dot(left, jnp.concatenate(blocks, axis=0), preferred_element_type=F32)


def near_forward_kernel(slot, index, over, near, turned_mine, turned_others, dose, scaled):
    scale_weights([near], scaled)
    rows, slots = slot.shape
    last = range(cut_of(slots), slots)
    for turned, row0 in ((turned_mine, 0), (turned_others, rows // 2)):

        def run(t, carry, turned=turned, row0=row0):
            b0 = row0 + t * RUN
            skip = over[b0 // RUN, 0] > 0

            @pl.when(skip)
            def _():
                for u in range(RUN):
                    dose[b0 + u] = jnp.zeros(dose.shape[1:], F32)

            @pl.when(jnp.logical_not(skip))
            def _():
                for u in range(RUN):
                    dose[b0 + u] = row_dose(last, b0 + u, slot, index, scaled, turned)

            return carry

        lax.fori_loop(0, rows // 2 // RUN, run, 0)


def forward_kernel(row0, slot, index, over, near, far, turned, part, dose, scaled):
    scale_weights([near, far], scaled)
    slots = slot.shape[1]
    cut = cut_of(slots)

    def run(t, carry):
        b0 = row0 + t * RUN
        for u in range(RUN):
            value = row_dose(range(cut), b0 + u, slot, index, scaled, turned)
            dose[t * RUN + u] = part[b0 + u] + value

        @pl.when(over[b0 // RUN, 0] > 0)
        def _():
            for u in range(RUN):
                dose[t * RUN + u] += row_dose(
                    range(cut, slots), b0 + u, slot, index, scaled, turned
                )

        return carry

    lax.fori_loop(0, dose.shape[0] // RUN, run, 0)


def work_of(rows, slots, weightings, width):
    return pl.CostEstimate(
        flops=2 * rows * slots * weightings * width * width,
        bytes_accessed=2 * rows * slots * width * width,
        transcendentals=0,
    )


def near_forward(tables, near, turned_mine, turned_others):
    half, weightings, width = near.shape
    rows, slots = tables[0].shape
    return pl.pallas_call(
        near_forward_kernel,
        in_specs=[in_smem()] * 3 + [in_vmem()] * 3,
        out_specs=in_vmem(),
        out_shape=jax.ShapeDtypeStruct((rows, weightings, width), F32),
        scratch_shapes=[pltpu.VMEM((6 * half + 1, weightings, width), BF16)],
        compiler_params=PARAMS,
        cost_estimate=work_of(rows, slots - cut_of(slots), weightings, width),
        name="near_forward",
    )(*tables[:2], tables[4], near, held(turned_mine), held(turned_others))


def forward(row0, tables, near, far, turned, part):
    half, weightings, width = near.shape
    rows, slots = tables[0].shape
    return pl.pallas_call(
        functools.partial(forward_kernel, row0),
        in_specs=[in_smem()] * 3 + [in_vmem()] * 4,
        out_specs=in_vmem(),
        out_shape=jax.ShapeDtypeStruct((rows // 2, weightings, width), F32),
        scratch_shapes=[pltpu.VMEM((6 * half + 1, weightings, width), BF16)],
        compiler_params=PARAMS,
        cost_estimate=work_of(rows // 2, cut_of(slots), weightings, width),
        name="forward",
    )(*tables[:2], tables[4], near, far, held(turned), part)


def first_forward(runs, me, tables, pieces, kept_others, tiles):
    columns = sum(p.shape[0] for p in pieces)
    weightings, width = pieces[0].shape[1:]
    rows, slots = tables[0].shape
    rows //= 2
    part = jax.ShapeDtypeStruct((rows, weightings, width), F32)
    return pl.pallas_call(
        functools.partial(first_forward_kernel, runs),
        in_specs=[in_smem()] * 3
        + [in_vmem()] * (len(pieces) + 1)
        + [pl.BlockSpec(memory_space=pltpu.HBM)],
        out_specs=[in_vmem()] * 3,
        out_shape=[part, part, pltpu.VMEM((rows * slots, width, width), BF16)],
        scratch_shapes=[
            pltpu.VMEM((3 * columns + 1, weightings, width), BF16),
            pltpu.SemaphoreType.DMA((rows,)),
        ],
        compiler_params=PARAMS,
        cost_estimate=work_of(2 * rows, slots, weightings, width),
        name="first_forward",
    )(
        me,
        *tables[:2],
        *pieces,
        held(kept_others),
        pltpu.with_memory_space_constraint(tiles, pltpu.HBM),
    )


def add_row(chosen, b, tables, left, kept, total):
    slot, places, factor = tables
    width = kept.shape[-1]
    group = 8 if len(chosen) % 8 == 0 else 1
    for k0 in range(0, len(chosen), group):
        some = chosen[k0 : k0 + group]
        right = jnp.concatenate([kept[slot[b, k]] for k in some], axis=1)
        product = jnp.dot(left, right, preferred_element_type=F32)
        at = [places[b, k] for k in some]
        old = [total[p] for p in at]
        for i, k in enumerate(some):
            total[at[i]] = old[i] + product[:, i * width : (i + 1) * width] * factor[b, k]


def backward_kernel(mine, row0, slot, places, factor, over, slope, kept, *refs):
    *before, total = refs
    columns = total.shape[0] - slot.shape[1]
    total[columns:] = jnp.zeros_like(total[columns:])
    total[:columns] = jnp.zeros_like(total[:columns]) if mine else before.pop(0)[...]
    tables = (slot, places, factor)
    slots = slot.shape[1]
    cut = cut_of(slots)

    def run(t, carry):
        b0 = row0 + t * RUN
        for u in range(RUN):
            add_row(range(cut), b0 + u, tables, slope[t * RUN + u], kept, total)

        @pl.when(over[b0 // RUN, 0] > 0)
        def _():
            for u in range(RUN):
                add_row(range(cut, slots), b0 + u, tables, slope[t * RUN + u], kept, total)

        return carry

    lax.fori_loop(0, slope.shape[0] // RUN, run, 0)
    if mine:
        before[0][...] = total[:columns]
    else:
        far, near = before
        near[...] = total[: columns // 2]
        far[...] = total[columns // 2 : columns]


def near_backward_kernel(
    slot, places, factor, over, slope_mine, slope_others, kept_mine, kept_others, near, out, total
):
    half = near.shape[0]
    total[:half] = near[...]
    total[2 * half :] = jnp.zeros_like(total[2 * half :])
    tables = (slot, places, factor)
    rows, slots = slot.shape
    last = range(cut_of(slots), slots)
    for slope, kept, row0 in ((slope_mine, kept_mine, 0), (slope_others, kept_others, rows // 2)):

        def run(t, carry, slope=slope, kept=kept, row0=row0):
            b0 = row0 + t * RUN

            @pl.when(over[b0 // RUN, 0] == 0)
            def _():
                for u in range(RUN):
                    add_row(last, b0 + u, tables, slope[t * RUN + u], kept, total)

            return carry

        lax.fori_loop(0, rows // 2 // RUN, run, 0)
    out[...] = total[:half]


def backward(mine, row0, tables, slope, kept, columns, *total):
    half_rows, weightings, width = slope.shape
    slots = tables[0].shape[1]
    out = [(columns, weightings, width)] if mine else [(columns // 2, weightings, width)] * 2
    return pl.pallas_call(
        functools.partial(backward_kernel, mine, row0),
        in_specs=[in_smem()] * 4 + [in_vmem()] * (2 + len(total)),
        out_specs=[in_vmem()] * len(out),
        out_shape=[jax.ShapeDtypeStruct(shape, F32) for shape in out],
        scratch_shapes=[pltpu.VMEM((columns + slots, weightings, width), F32)],
        compiler_params=PARAMS,
        cost_estimate=work_of(half_rows, cut_of(slots), weightings, width),
        name="backward",
    )(tables[0], *tables[2:], slope, held(kept), *total)


def near_backward(tables, slope_mine, slope_others, kept_mine, kept_others, near):
    half, weightings, width = near.shape
    rows, slots = tables[0].shape
    return pl.pallas_call(
        near_backward_kernel,
        in_specs=[in_smem()] * 4 + [in_vmem()] * 5,
        out_specs=in_vmem(),
        out_shape=jax.ShapeDtypeStruct(near.shape, F32),
        scratch_shapes=[pltpu.VMEM((2 * half + slots, weightings, width), F32)],
        compiler_params=PARAMS,
        cost_estimate=work_of(rows, slots - cut_of(slots), weightings, width),
        name="near_backward",
    )(tables[0], *tables[2:], slope_mine, slope_others, held(kept_mine), held(kept_others), near)


def per_device(
    sizes,
    dose_blocks,
    block_cols,
    block_exps,
    live_counts,
    labels,
    upper_dose,
    upper_weight,
    lower_dose,
    lower_weight,
    initial_spot_weights,
):
    n_vox, n_spot = sizes
    z, x, core = (lax.axis_index(a) for a in ("vox", "spot", "rep"))
    rows, _, slots, width, _ = dose_blocks.shape
    weightings, _, chunk_spots = initial_spot_weights.shape
    chunk = chunk_spots // width
    columns = chunk * n_vox
    own = chunk // 2
    initial = initial_spot_weights[:, 0].reshape(weightings, chunk, width)
    weights = lax.dynamic_slice_in_dim(initial, core * own, own, 1).transpose(1, 0, 2)

    def over_vox(arrays):
        return [
            lax.ppermute(a, "vox", [(i, i ^ d) for i in range(n_vox)])
            for d, a in enumerate(arrays, 1)
        ]

    def over_rep(array):
        return lax.ppermute(array, "rep", [(0, 1), (1, 0)])

    me = jnp.stack([z, core, x]).astype(jnp.int32)
    level_table = jnp.stack([upper_dose, upper_weight, lower_dose, lower_weight])
    tiles = dose_blocks.reshape(rows * slots, width, width)

    def gather_weights(weights):
        piece = weights.astype(BF16)
        return [piece] + over_vox([piece] * (n_vox - 1))

    bits = [1 << i for i in range(n_spot.bit_length() - 1)]
    pieces = gather_weights(weights)
    kept_others, me = load_others(n_spot, rows, me, tiles)
    pieces, kept_others = lax.optimization_barrier((pieces, kept_others))
    steps = [(1, 1)] + [(2, bit) for bit in bits]
    near = jnp.concatenate(pieces, axis=0)
    live = live_counts.reshape(rows)
    *tables, sides = indices(
        n_vox, columns, n_spot, steps, me, block_cols, block_exps, live, near
    )

    for step in range(ITERS):
        if step > 0:
            near = jnp.concatenate(pieces, axis=0)
        other_half = over_rep(near)
        if step == 0:
            given, dose, kept_mine = first_forward(
                n_spot, me, tables, [near, other_half], kept_others, tiles
            )
            labels, given = lax.optimization_barrier((labels, given))
            known = labels.astype(F32).reshape(-1, width)
        else:
            part = near_forward(tables, near, turned_mine, turned_others)
            given = forward(rows // 2, tables, near, other_half, turned_others, part)
            dose = forward(0, tables, near, other_half, turned_mine, part)
        dose = dose + over_rep(given)
        for e, bit in enumerate(bits, 1):
            sent = dose
            if step == 0:
                n = known.shape[0]
                tile = jnp.pad(known, ((0, weightings - n), (0, 0)))
                sent = jnp.concatenate([dose, tile[None]], axis=0)
            got = lax.ppermute(sent, "spot", [(i, i ^ bit) for i in range(n_spot)])
            if step == 0:
                theirs = got[rows // 2, :n]
                first = sides[e, :1] > 0
                known = jnp.concatenate(
                    [jnp.where(first, known, theirs), jnp.where(first, theirs, known)]
                )
                got = got[: rows // 2]
            dose = dose + got
        if step == 0:
            levels = jnp.zeros((4, rows // 2, 1, width), F32)
            for c in range(level_table.shape[1]):
                value = level_table[:, c][:, None, None, None]
                levels = jnp.where(known[None, :, None, :] == c, value, levels)
        slope = (
            levels[1] * jax.nn.sigmoid(4.0 * (dose - levels[0]))
            - levels[3] * jax.nn.sigmoid(4.0 * (levels[2] - dose))
        ).astype(BF16)
        slope_others = over_rep(slope)
        (total,) = backward(True, 0, tables, slope, kept_mine, columns)
        far, near = backward(False, rows // 2, tables, slope_others, kept_others, columns, total)
        theirs = over_rep(far)
        near = near_backward(tables, slope, slope_others, kept_mine, kept_others, near) + theirs
        received = over_vox([near[d * own : (d + 1) * own] for d in range(1, n_vox)])
        if step == 0:
            turned_mine = turn(kept_mine, near)
            received, turned_mine = lax.optimization_barrier((received, turned_mine))
        else:
            received = lax.optimization_barrier(received)
        gradient = near[:own]
        for part in received:
            gradient = gradient + part
        weights = jnp.maximum(weights - 0.5 * gradient, 0.0)
        if step < ITERS - 1:
            pieces = gather_weights(weights)
            if step == 0:
                turned_others = turn(kept_others, pieces[0])
                pieces, turned_others = lax.optimization_barrier((pieces, turned_others))

    mine = jnp.stack([weights, gradient])
    other = over_rep(mine)
    first = sides[0, :1] > 0
    both = jnp.concatenate(
        [jnp.where(first, mine, other), jnp.where(first, other, mine)], axis=1
    )
    both = both.transpose(0, 2, 1, 3).reshape(2, weightings, 1, chunk_spots)
    return both[0], both[1]


def solution(mesh):
    placed = (
        P(("groups", "vox"), "spot", "rep", None, None),
        P(("groups", "vox"), "spot", "rep"),
        P(("groups", "vox"), "spot", "rep"),
        P(("groups", "vox"), "spot"),
        P(("groups", "vox", "spot", "rep")),
        P("groups"),
        P("groups"),
        P("groups"),
        P("groups"),
        P("groups", "spot", "vox"),
    )
    sizes = tuple(mesh.shape[a] for a in ("vox", "spot"))
    return jax.shard_map(
        functools.partial(per_device, sizes),
        mesh=mesh,
        in_specs=placed,
        out_specs=(P("groups", "spot", "vox"), P("groups", "spot", "vox")),
        check_vma=False,
    )
```

```python
import functools

import jax
import jax.numpy as jnp
from jax import lax
from jax.experimental import pallas as pl
from jax.experimental.pallas import tpu as pltpu
from jax.sharding import PartitionSpec as P

ITERS = 4
F32 = jnp.float32
BF16 = jnp.bfloat16
PARAMS = pltpu.CompilerParams(vmem_limit_bytes=16 * 2**20)


def in_vmem():
    return pl.BlockSpec(memory_space=pltpu.VMEM)


def in_smem():
    return pl.BlockSpec(memory_space=pltpu.SMEM)


def held(array):
    return pltpu.with_memory_space_constraint(array, pltpu.VMEM)


RUN = 4


def cut_of(slots):
    return 2 * slots // 3


def prepare_kernel(n_vox, columns, runs, steps, me, cols, exps, live, stored, *refs):
    outs, kept, me_out, sides, packed, *tables, sems, load_sems = refs[:5], *refs[5:]
    loads = [
        row_copy(False, runs, cols.shape[2], me, stored, kept, load_sems, jnp.int32(b))
        for b in range(load_sems.shape[0])
    ]
    for load in loads:
        load.start()
    for i in range(me.shape[0]):
        me_out[i] = me[i]
    z, core = me[0], me[1]
    rows, _, slots = cols.shape
    own = columns // (2 * n_vox)
    column, exponent = cols[:, 0, :], exps[:, 0, :]
    piece, within = lax.div(column, own), lax.rem(column, own)
    place = ((lax.rem(piece, 2) ^ core) * n_vox + (lax.div(piece, 2) ^ z)) * own + within
    both = place * 4 + exponent + 1
    position = core * slots + lax.broadcasted_iota(jnp.int32, (1, slots), 1)
    n = rows // (2 * runs)
    for r in range(rows):
        half, t = divmod(r, rows // 2)
        first = 2 * n * (t // n) + t % n
        low, high = (first, first + n) if half == 0 else (first + n, first)
        row = jnp.where(core == 0, both[low : low + 1], both[high : high + 1])
        used = position < jnp.where(core == 0, live[low], live[high])
        packed[r : r + 1] = jnp.where(used, row, 3)

    both = packed[...]
    here = lax.broadcasted_iota(jnp.int32, (rows, slots), 1)
    dead = lax.rem(both, 4) == 3
    kind = jnp.where(dead, 2, jnp.where(both >= 2 * columns, 0, 1))
    key = kind * slots + here
    rank = jnp.zeros_like(key)
    for k in range(slots):
        rank = rank + jnp.where(key[:, k : k + 1] < key, 1, 0)
    both = jnp.where(dead, (columns + rank) * 4 + 3, both) * 64 + here
    ordered = jnp.zeros_like(key)
    for k in range(slots):
        ordered = ordered + jnp.where(rank[:, k : k + 1] == here, both[:, k : k + 1], 0)
    kind, place = lax.rem(lax.div(ordered, 64), 4), lax.div(ordered, 256)
    slot, index, places, factor, over = tables
    in_half = lax.rem(lax.broadcasted_iota(jnp.int32, (rows, slots), 0), rows // 2)
    slot[...] = in_half * slots + lax.rem(ordered, 64)
    index[...] = jnp.where(kind == 3, 3 * columns, kind * columns + place)
    places[...] = place
    factor[...] = jnp.where(
        kind == 3, 0.0, jnp.where(kind == 0, 0.5, jnp.where(kind == 2, 2.0, 1.0))
    ).astype(F32)
    others = jnp.where((kind != 3) & (place >= columns // 2), 1.0, 0.0).astype(F32)
    others = jnp.sum(others, axis=1, keepdims=True)
    for r in range(rows // RUN):
        most = jnp.max(others[r * RUN : (r + 1) * RUN], axis=0, keepdims=True)
        most = jnp.broadcast_to(most, (1, over.shape[1]))
        over[r : r + 1] = jnp.where(most > cut_of(slots), 1, 0)
    copies = [
        pltpu.make_async_copy(table, out, sems.at[i])
        for i, (table, out) in enumerate(zip(tables, outs, strict=True))
    ]
    for copy in copies:
        copy.start()
    for e, (at, bit) in enumerate(steps):
        side = jnp.where((me[at] & bit) == 0, 1.0, 0.0).astype(F32)
        sides[e] = jnp.full(sides.shape[1:], side)
    for copy in copies + loads:
        copy.wait()


def prepare(n_vox, columns, runs, steps, me, cols, exps, live, tiles):
    rows, _, slots = cols.shape
    shapes = [((rows, slots), t) for t in (jnp.int32, jnp.int32, jnp.int32, F32)]
    shapes.append(((rows // RUN, 128), jnp.int32))
    half = (tiles.shape[0] // 2,) + tiles.shape[1:]
    in_hbm = [pltpu.with_memory_space_constraint(a, pltpu.HBM) for a in (cols, exps, tiles)]
    *tables, kept, me, sides = pl.pallas_call(
        functools.partial(prepare_kernel, n_vox, columns, runs, steps),
        in_specs=[in_smem()]
        + [in_vmem()] * 2
        + [in_smem(), pl.BlockSpec(memory_space=pltpu.HBM)],
        out_specs=[in_smem()] * 5 + [in_vmem(), in_smem(), in_vmem()],
        out_shape=[pltpu.SMEM(*shape) for shape in shapes]
        + [pltpu.VMEM(half, tiles.dtype), pltpu.SMEM(me.shape, me.dtype)]
        + [jax.ShapeDtypeStruct((len(steps), 8, 128), F32)],
        scratch_shapes=[pltpu.VMEM((rows, slots), jnp.int32)]
        + [pltpu.VMEM(*shape) for shape in shapes]
        + [pltpu.SemaphoreType.DMA((len(shapes),)), pltpu.SemaphoreType.DMA((rows // 2,))],
        compiler_params=PARAMS,
        cost_estimate=pl.CostEstimate(flops=0, bytes_accessed=2 * tiles.size, transcendentals=0),
        name="prepare",
    )(me, *in_hbm[:2], live, in_hbm[2])
    return tables, kept, me, sides


def turn_kernel(kept, after, turned):
    count = kept.shape[0]
    step = 8 if count % 8 == 0 else 1

    def some(t, carry):
        for u in range(step):
            turned[t * step + u] = kept[t * step + u].T
        return carry

    lax.fori_loop(0, count // step, some, 0)


def turn(kept, after):
    return pl.pallas_call(
        turn_kernel,
        in_specs=[in_vmem(), pl.BlockSpec(memory_space=pl.ANY)],
        out_specs=in_vmem(),
        out_shape=pltpu.VMEM(kept.shape, kept.dtype),
        compiler_params=PARAMS,
        cost_estimate=pl.CostEstimate(flops=0, bytes_accessed=4 * kept.size, transcendentals=0),
        name="turn",
    )(held(kept), after)


def scale_weights(pieces, scaled):
    columns = (scaled.shape[0] - 1) // 3
    at = 0
    for piece in pieces:
        n = piece.shape[0]
        values = piece[...]
        scaled[at : at + n] = values * BF16(0.5)
        scaled[columns + at : columns + at + n] = values
        scaled[2 * columns + at : 2 * columns + at + n] = values * BF16(2.0)
        at += n
    scaled[3 * columns] = jnp.zeros(scaled.shape[1:], BF16)


def row_operands(chosen, b, slot, index, scaled, blocks):
    left = jnp.concatenate([scaled[index[b, k]] for k in chosen], axis=1)
    return left, [blocks[slot[b, k]] for k in chosen]


def row_copy(mine, runs, slots, me, stored, kept, sems, b):
    n = sems.shape[0] // runs
    half = me[1] if mine else 1 - me[1]
    return pltpu.make_async_copy(
        stored.at[pl.ds(((2 * lax.div(b, n) + half) * n + lax.rem(b, n)) * slots, slots)],
        kept.at[pl.ds(b * slots, slots)],
        sems.at[b],
    )


def first_forward_kernel(runs, me, slot, index, *refs):
    pieces, (kept_others, stored, given, dose, kept_mine, scaled, sems) = refs[:-7], refs[-7:]
    slots = slot.shape[1]
    rows = dose.shape[0]

    def copies(t):
        rows_of_run = [t * RUN + u for u in range(RUN)]
        return [row_copy(True, runs, slots, me, stored, kept_mine, sems, b) for b in rows_of_run]

    for copy in copies(jnp.int32(0)):
        copy.start()
    scale_weights(pieces, scaled)
    for kept, out, row0 in ((kept_others, given, rows), (kept_mine, dose, 0)):

        def run(t, carry, kept=kept, out=out, row0=row0):
            if kept is kept_mine:
                for copy in copies(t):
                    copy.wait()
            for u in range(RUN):
                b = t * RUN + u
                left, blocks = row_operands(range(slots), row0 + b, slot, index, scaled, kept)
                right = jnp.concatenate(blocks, axis=1)
                out[b] = lax.dot_general(
                    left, right, (((1,), (1,)), ((), ())), preferred_element_type=F32
                )
            if kept is kept_others:

                @pl.when(t + 1 < rows // RUN)
                def _():
                    for copy in copies(t + 1):
                        copy.start()

            return carry

        lax.fori_loop(0, rows // RUN, run, 0)


def row_dose(chosen, b, slot, index, scaled, turned):
    left, blocks = row_operands(chosen, b, slot, index, scaled, turned)
    return jnp.dot(left, jnp.concatenate(blocks, axis=0), preferred_element_type=F32)


def near_forward_kernel(slot, index, over, near, turned_mine, turned_others, dose, scaled):
    scale_weights([near], scaled)
    rows, slots = slot.shape
    last = range(cut_of(slots), slots)
    for turned, row0 in ((turned_mine, 0), (turned_others, rows // 2)):

        def run(t, carry, turned=turned, row0=row0):
            b0 = row0 + t * RUN
            skip = over[b0 // RUN, 0] > 0

            @pl.when(skip)
            def _():
                for u in range(RUN):
                    dose[b0 + u] = jnp.zeros(dose.shape[1:], F32)

            @pl.when(jnp.logical_not(skip))
            def _():
                for u in range(RUN):
                    dose[b0 + u] = row_dose(last, b0 + u, slot, index, scaled, turned)

            return carry

        lax.fori_loop(0, rows // 2 // RUN, run, 0)


def forward_kernel(row0, slot, index, over, near, far, turned, part, dose, scaled):
    scale_weights([near, far], scaled)
    slots = slot.shape[1]
    cut = cut_of(slots)

    def run(t, carry):
        b0 = row0 + t * RUN
        for u in range(RUN):
            value = row_dose(range(cut), b0 + u, slot, index, scaled, turned)
            dose[t * RUN + u] = part[b0 + u] + value

        @pl.when(over[b0 // RUN, 0] > 0)
        def _():
            def rest(u, carry):
                dose[t * RUN + u] += row_dose(
                    range(cut, slots), b0 + u, slot, index, scaled, turned
                )
                return carry

            lax.fori_loop(0, RUN, rest, 0)

        return carry

    lax.fori_loop(0, dose.shape[0] // RUN, run, 0)


def work_of(rows, slots, weightings, width):
    return pl.CostEstimate(
        flops=2 * rows * slots * weightings * width * width,
        bytes_accessed=2 * rows * slots * width * width,
        transcendentals=0,
    )


def near_forward(tables, near, turned_mine, turned_others):
    half, weightings, width = near.shape
    rows, slots = tables[0].shape
    return pl.pallas_call(
        near_forward_kernel,
        in_specs=[in_smem()] * 3 + [in_vmem()] * 3,
        out_specs=in_vmem(),
        out_shape=jax.ShapeDtypeStruct((rows, weightings, width), F32),
        scratch_shapes=[pltpu.VMEM((6 * half + 1, weightings, width), BF16)],
        compiler_params=PARAMS,
        cost_estimate=work_of(rows, slots - cut_of(slots), weightings, width),
        name="near_forward",
    )(*tables[:2], tables[4], near, held(turned_mine), held(turned_others))


def forward(row0, tables, near, far, turned, part):
    half, weightings, width = near.shape
    rows, slots = tables[0].shape
    return pl.pallas_call(
        functools.partial(forward_kernel, row0),
        in_specs=[in_smem()] * 3 + [in_vmem()] * 4,
        out_specs=in_vmem(),
        out_shape=jax.ShapeDtypeStruct((rows // 2, weightings, width), F32),
        scratch_shapes=[pltpu.VMEM((6 * half + 1, weightings, width), BF16)],
        compiler_params=PARAMS,
        cost_estimate=work_of(rows // 2, cut_of(slots), weightings, width),
        name="forward",
    )(*tables[:2], tables[4], near, far, held(turned), part)


def first_forward(runs, me, tables, pieces, kept_others, tiles):
    columns = sum(p.shape[0] for p in pieces)
    weightings, width = pieces[0].shape[1:]
    rows, slots = tables[0].shape
    rows //= 2
    part = jax.ShapeDtypeStruct((rows, weightings, width), F32)
    return pl.pallas_call(
        functools.partial(first_forward_kernel, runs),
        in_specs=[in_smem()] * 3
        + [in_vmem()] * (len(pieces) + 1)
        + [pl.BlockSpec(memory_space=pltpu.HBM)],
        out_specs=[in_vmem()] * 3,
        out_shape=[part, part, pltpu.VMEM((rows * slots, width, width), BF16)],
        scratch_shapes=[
            pltpu.VMEM((3 * columns + 1, weightings, width), BF16),
            pltpu.SemaphoreType.DMA((rows,)),
        ],
        compiler_params=PARAMS,
        cost_estimate=work_of(2 * rows, slots, weightings, width),
        name="first_forward",
    )(
        me,
        *tables[:2],
        *pieces,
        held(kept_others),
        pltpu.with_memory_space_constraint(tiles, pltpu.HBM),
    )


def add_row(chosen, b, tables, left, kept, total):
    slot, places, factor = tables
    width = kept.shape[-1]
    group = 8 if len(chosen) % 8 == 0 else 1
    for k0 in range(0, len(chosen), group):
        some = chosen[k0 : k0 + group]
        right = jnp.concatenate([kept[slot[b, k]] for k in some], axis=1)
        product = jnp.dot(left, right, preferred_element_type=F32)
        at = [places[b, k] for k in some]
        old = [total[p] for p in at]
        for i, k in enumerate(some):
            total[at[i]] = old[i] + product[:, i * width : (i + 1) * width] * factor[b, k]


def backward_kernel(mine, row0, slot, places, factor, over, slope, kept, *refs):
    *before, total = refs
    columns = total.shape[0] - slot.shape[1]
    total[columns:] = jnp.zeros_like(total[columns:])
    total[:columns] = jnp.zeros_like(total[:columns]) if mine else before.pop(0)[...]
    tables = (slot, places, factor)
    slots = slot.shape[1]
    cut = cut_of(slots)

    def run(t, carry):
        b0 = row0 + t * RUN
        for u in range(RUN):
            add_row(range(cut), b0 + u, tables, slope[t * RUN + u], kept, total)

        @pl.when(over[b0 // RUN, 0] > 0)
        def _():
            def rest(u, carry):
                add_row(range(cut, slots), b0 + u, tables, slope[t * RUN + u], kept, total)
                return carry

            lax.fori_loop(0, RUN, rest, 0)

        return carry

    lax.fori_loop(0, slope.shape[0] // RUN, run, 0)
    if mine:
        before[0][...] = total[:columns]
    else:
        far, near = before
        near[...] = total[: columns // 2]
        far[...] = total[columns // 2 : columns]


def near_backward_kernel(
    slot, places, factor, over, slope_mine, slope_others, kept_mine, kept_others, near, out, total
):
    half = near.shape[0]
    total[:half] = near[...]
    total[2 * half :] = jnp.zeros_like(total[2 * half :])
    tables = (slot, places, factor)
    rows, slots = slot.shape
    last = range(cut_of(slots), slots)
    for slope, kept, row0 in ((slope_mine, kept_mine, 0), (slope_others, kept_others, rows // 2)):

        def run(t, carry, slope=slope, kept=kept, row0=row0):
            b0 = row0 + t * RUN

            @pl.when(over[b0 // RUN, 0] == 0)
            def _():
                for u in range(RUN):
                    add_row(last, b0 + u, tables, slope[t * RUN + u], kept, total)

            return carry

        lax.fori_loop(0, rows // 2 // RUN, run, 0)
    out[...] = total[:half]


def backward(mine, row0, tables, slope, kept, columns, *total):
    half_rows, weightings, width = slope.shape
    slots = tables[0].shape[1]
    out = [(columns, weightings, width)] if mine else [(columns // 2, weightings, width)] * 2
    return pl.pallas_call(
        functools.partial(backward_kernel, mine, row0),
        in_specs=[in_smem()] * 4 + [in_vmem()] * (2 + len(total)),
        out_specs=[in_vmem()] * len(out),
        out_shape=[jax.ShapeDtypeStruct(shape, F32) for shape in out],
        scratch_shapes=[pltpu.VMEM((columns + slots, weightings, width), F32)],
        compiler_params=PARAMS,
        cost_estimate=work_of(half_rows, cut_of(slots), weightings, width),
        name="backward",
    )(tables[0], *tables[2:], slope, held(kept), *total)


def near_backward(tables, slope_mine, slope_others, kept_mine, kept_others, near):
    half, weightings, width = near.shape
    rows, slots = tables[0].shape
    return pl.pallas_call(
        near_backward_kernel,
        in_specs=[in_smem()] * 4 + [in_vmem()] * 5,
        out_specs=in_vmem(),
        out_shape=jax.ShapeDtypeStruct(near.shape, F32),
        scratch_shapes=[pltpu.VMEM((2 * half + slots, weightings, width), F32)],
        compiler_params=PARAMS,
        cost_estimate=work_of(rows, slots - cut_of(slots), weightings, width),
        name="near_backward",
    )(tables[0], *tables[2:], slope_mine, slope_others, held(kept_mine), held(kept_others), near)


def per_device(
    sizes,
    dose_blocks,
    block_cols,
    block_exps,
    live_counts,
    labels,
    upper_dose,
    upper_weight,
    lower_dose,
    lower_weight,
    initial_spot_weights,
):
    n_vox, n_spot = sizes
    z, x, core = (lax.axis_index(a) for a in ("vox", "spot", "rep"))
    rows, _, slots, width, _ = dose_blocks.shape
    weightings, _, chunk_spots = initial_spot_weights.shape
    chunk = chunk_spots // width
    columns = chunk * n_vox
    own = chunk // 2
    initial = initial_spot_weights[:, 0].reshape(weightings, chunk, width)
    weights = lax.dynamic_slice_in_dim(initial, core * own, own, 1).transpose(1, 0, 2)

    def over_vox(arrays):
        return [
            lax.ppermute(a, "vox", [(i, i ^ d) for i in range(n_vox)])
            for d, a in enumerate(arrays, 1)
        ]

    def over_rep(array):
        return lax.ppermute(array, "rep", [(0, 1), (1, 0)])

    me = jnp.stack([z, core, x]).astype(jnp.int32)
    level_table = jnp.stack([upper_dose, upper_weight, lower_dose, lower_weight])
    tiles = dose_blocks.reshape(rows * slots, width, width)

    def gather_weights(weights):
        piece = weights.astype(BF16)
        return [piece] + over_vox([piece] * (n_vox - 1))

    bits = [1 << i for i in range(n_spot.bit_length() - 1)]
    pieces = gather_weights(weights)
    steps = [(1, 1)] + [(2, bit) for bit in bits]
    live = live_counts.reshape(rows)
    tables, kept_others, me, sides = prepare(
        n_vox, columns, n_spot, steps, me, block_cols, block_exps, live, tiles
    )
    pieces, kept_others = lax.optimization_barrier((pieces, kept_others))

    for step in range(ITERS):
        near = jnp.concatenate(pieces, axis=0)
        other_half = over_rep(near)
        if step == 0:
            given, dose, kept_mine = first_forward(
                n_spot, me, tables, [near, other_half], kept_others, tiles
            )
            labels, given = lax.optimization_barrier((labels, given))
            known = labels.astype(F32).reshape(-1, width)
        else:
            part = near_forward(tables, near, turned_mine, turned_others)
            given = forward(rows // 2, tables, near, other_half, turned_others, part)
            dose = forward(0, tables, near, other_half, turned_mine, part)
        dose = dose + over_rep(given)
        for e, bit in enumerate(bits, 1):
            sent = dose
            if step == 0:
                n = known.shape[0]
                tile = jnp.pad(known, ((0, weightings - n), (0, 0)))
                sent = jnp.concatenate([dose, tile[None]], axis=0)
            got = lax.ppermute(sent, "spot", [(i, i ^ bit) for i in range(n_spot)])
            if step == 0:
                theirs = got[rows // 2, :n]
                first = sides[e, :1] > 0
                known = jnp.concatenate(
                    [jnp.where(first, known, theirs), jnp.where(first, theirs, known)]
                )
                got = got[: rows // 2]
            dose = dose + got
        if step == 0:
            levels = jnp.zeros((4, rows // 2, 1, width), F32)
            for c in range(level_table.shape[1]):
                value = level_table[:, c][:, None, None, None]
                levels = jnp.where(known[None, :, None, :] == c, value, levels)
        slope = (
            levels[1] * jax.nn.sigmoid(4.0 * (dose - levels[0]))
            - levels[3] * jax.nn.sigmoid(4.0 * (levels[2] - dose))
        ).astype(BF16)
        slope_others = over_rep(slope)
        (total,) = backward(True, 0, tables, slope, kept_mine, columns)
        far, near = backward(False, rows // 2, tables, slope_others, kept_others, columns, total)
        theirs = over_rep(far)
        near = near_backward(tables, slope, slope_others, kept_mine, kept_others, near) + theirs
        received = over_vox([near[d * own : (d + 1) * own] for d in range(1, n_vox)])
        if step == 0:
            turned_mine = turn(kept_mine, near)
            received, turned_mine = lax.optimization_barrier((received, turned_mine))
        else:
            received = lax.optimization_barrier(received)
        gradient = near[:own]
        for part in received:
            gradient = gradient + part
        weights = jnp.maximum(weights - 0.5 * gradient, 0.0)
        if step < ITERS - 1:
            pieces = gather_weights(weights)
            if step == 0:
                turned_others = turn(kept_others, pieces[0])
                pieces, turned_others = lax.optimization_barrier((pieces, turned_others))

    mine = jnp.stack([weights, gradient])
    other = over_rep(mine)
    first = sides[0, :1] > 0
    both = jnp.concatenate(
        [jnp.where(first, mine, other), jnp.where(first, other, mine)], axis=1
    )
    both = both.transpose(0, 2, 1, 3).reshape(2, weightings, 1, chunk_spots)
    return both[0], both[1]


def solution(mesh):
    placed = (
        P(("groups", "vox"), "spot", "rep", None, None),
        P(("groups", "vox"), "spot", "rep"),
        P(("groups", "vox"), "spot", "rep"),
        P(("groups", "vox"), "spot"),
        P(("groups", "vox", "spot", "rep")),
        P("groups"),
        P("groups"),
        P("groups"),
        P("groups"),
        P("groups", "spot", "vox"),
    )
    sizes = tuple(mesh.shape[a] for a in ("vox", "spot"))
    return jax.shard_map(
        functools.partial(per_device, sizes),
        mesh=mesh,
        in_specs=placed,
        out_specs=(P("groups", "spot", "vox"), P("groups", "spot", "vox")),
        check_vma=False,
    )
```

```python
import functools

import jax
import jax.numpy as jnp
from jax import lax
from jax.experimental import pallas as pl
from jax.experimental.pallas import tpu as pltpu
from jax.sharding import PartitionSpec as P

ITERS = 4
F32 = jnp.float32
BF16 = jnp.bfloat16
PARAMS = pltpu.CompilerParams(vmem_limit_bytes=16 * 2**20)


def in_vmem():
    return pl.BlockSpec(memory_space=pltpu.VMEM)


def in_smem():
    return pl.BlockSpec(memory_space=pltpu.SMEM)


def held(array):
    return pltpu.with_memory_space_constraint(array, pltpu.VMEM)


RUN = 4


def cut_of(slots):
    return 2 * slots // 3


def prepare_kernel(n_vox, columns, runs, steps, me, cols, exps, live, stored, *refs):
    outs, kept, me_out, sides, packed, *tables, sems, load_sems = refs[:5], *refs[5:]
    loads = [
        row_copy(False, runs, cols.shape[2], me, stored, kept, load_sems, jnp.int32(b))
        for b in range(load_sems.shape[0])
    ]
    for load in loads:
        load.start()
    for i in range(me.shape[0]):
        me_out[i] = me[i]
    z, core = me[0], me[1]
    rows, _, slots = cols.shape
    own = columns // (2 * n_vox)
    column, exponent = cols[:, 0, :], exps[:, 0, :]
    piece, within = lax.div(column, own), lax.rem(column, own)
    place = ((lax.rem(piece, 2) ^ core) * n_vox + (lax.div(piece, 2) ^ z)) * own + within
    both = place * 4 + exponent + 1
    position = core * slots + lax.broadcasted_iota(jnp.int32, (1, slots), 1)
    n = rows // (2 * runs)
    for r in range(rows):
        half, t = divmod(r, rows // 2)
        first = 2 * n * (t // n) + t % n
        low, high = (first, first + n) if half == 0 else (first + n, first)
        row = jnp.where(core == 0, both[low : low + 1], both[high : high + 1])
        used = position < jnp.where(core == 0, live[low], live[high])
        packed[r : r + 1] = jnp.where(used, row, 3)

    both = packed[...]
    here = lax.broadcasted_iota(jnp.int32, (rows, slots), 1)
    dead = lax.rem(both, 4) == 3
    kind = jnp.where(dead, 2, jnp.where(both >= 2 * columns, 0, 1))
    key = kind * slots + here
    rank = jnp.zeros_like(key)
    for k in range(slots):
        rank = rank + jnp.where(key[:, k : k + 1] < key, 1, 0)
    both = jnp.where(dead, (columns + rank) * 4 + 3, both) * 64 + here
    ordered = jnp.zeros_like(key)
    for k in range(slots):
        ordered = ordered + jnp.where(rank[:, k : k + 1] == here, both[:, k : k + 1], 0)
    kind, place = lax.rem(lax.div(ordered, 64), 4), lax.div(ordered, 256)
    slot, index, places, factor, over = tables
    in_half = lax.rem(lax.broadcasted_iota(jnp.int32, (rows, slots), 0), rows // 2)
    slot[...] = in_half * slots + lax.rem(ordered, 64)
    index[...] = jnp.where(kind == 3, 3 * columns, kind * columns + place)
    places[...] = place
    factor[...] = jnp.where(
        kind == 3, 0.0, jnp.where(kind == 0, 0.5, jnp.where(kind == 2, 2.0, 1.0))
    ).astype(F32)
    others = jnp.where((kind != 3) & (place >= columns // 2), 1.0, 0.0).astype(F32)
    others = jnp.sum(others, axis=1, keepdims=True)
    for r in range(rows // RUN):
        most = jnp.max(others[r * RUN : (r + 1) * RUN], axis=0, keepdims=True)
        most = jnp.broadcast_to(most, (1, over.shape[1]))
        over[r : r + 1] = jnp.where(most > cut_of(slots), 1, 0)
    copies = [
        pltpu.make_async_copy(table, out, sems.at[i])
        for i, (table, out) in enumerate(zip(tables, outs, strict=True))
    ]
    for copy in copies:
        copy.start()
    for e, (at, bit) in enumerate(steps):
        side = jnp.where((me[at] & bit) == 0, 1.0, 0.0).astype(F32)
        sides[e] = jnp.full(sides.shape[1:], side)
    for copy in copies + loads:
        copy.wait()


def prepare(n_vox, columns, runs, steps, me, cols, exps, live, tiles):
    rows, _, slots = cols.shape
    shapes = [((rows, slots), t) for t in (jnp.int32, jnp.int32, jnp.int32, F32)]
    shapes.append(((rows // RUN, 128), jnp.int32))
    half = (tiles.shape[0] // 2,) + tiles.shape[1:]
    in_hbm = [pltpu.with_memory_space_constraint(a, pltpu.HBM) for a in (cols, exps, live, tiles)]
    *tables, kept, me, sides = pl.pallas_call(
        functools.partial(prepare_kernel, n_vox, columns, runs, steps),
        in_specs=[in_smem()]
        + [in_vmem()] * 2
        + [in_smem(), pl.BlockSpec(memory_space=pltpu.HBM)],
        out_specs=[in_smem()] * 5 + [in_vmem(), in_smem(), in_vmem()],
        out_shape=[pltpu.SMEM(*shape) for shape in shapes]
        + [pltpu.VMEM(half, tiles.dtype), pltpu.SMEM(me.shape, me.dtype)]
        + [jax.ShapeDtypeStruct((len(steps), 8, 128), F32)],
        scratch_shapes=[pltpu.VMEM((rows, slots), jnp.int32)]
        + [pltpu.VMEM(*shape) for shape in shapes]
        + [pltpu.SemaphoreType.DMA((len(shapes),)), pltpu.SemaphoreType.DMA((rows // 2,))],
        compiler_params=PARAMS,
        cost_estimate=pl.CostEstimate(flops=0, bytes_accessed=2 * tiles.size, transcendentals=0),
        name="prepare",
    )(me, *in_hbm)
    return tables, kept, me, sides


def turn_kernel(kept, after, turned):
    count = kept.shape[0]
    step = 8 if count % 8 == 0 else 1

    def some(t, carry):
        for u in range(step):
            turned[t * step + u] = kept[t * step + u].T
        return carry

    lax.fori_loop(0, count // step, some, 0)


def turn(kept, after):
    return pl.pallas_call(
        turn_kernel,
        in_specs=[in_vmem(), pl.BlockSpec(memory_space=pl.ANY)],
        out_specs=in_vmem(),
        out_shape=pltpu.VMEM(kept.shape, kept.dtype),
        compiler_params=PARAMS,
        cost_estimate=pl.CostEstimate(flops=0, bytes_accessed=4 * kept.size, transcendentals=0),
        name="turn",
    )(held(kept), after)


def scale_weights(pieces, scaled):
    columns = (scaled.shape[0] - 1) // 3
    at = 0
    for piece in pieces:
        n = piece.shape[0]
        values = piece[...]
        scaled[at : at + n] = values * BF16(0.5)
        scaled[columns + at : columns + at + n] = values
        scaled[2 * columns + at : 2 * columns + at + n] = values * BF16(2.0)
        at += n
    scaled[3 * columns] = jnp.zeros(scaled.shape[1:], BF16)


def row_operands(chosen, b, slot, index, scaled, blocks):
    left = jnp.concatenate([scaled[index[b, k]] for k in chosen], axis=1)
    return left, [blocks[slot[b, k]] for k in chosen]


def row_copy(mine, runs, slots, me, stored, kept, sems, b):
    n = sems.shape[0] // runs
    half = me[1] if mine else 1 - me[1]
    return pltpu.make_async_copy(
        stored.at[pl.ds(((2 * lax.div(b, n) + half) * n + lax.rem(b, n)) * slots, slots)],
        kept.at[pl.ds(b * slots, slots)],
        sems.at[b],
    )


def first_forward_kernel(runs, me, slot, index, *refs):
    pieces, (kept_others, stored, given, dose, kept_mine, scaled, sems) = refs[:-7], refs[-7:]
    slots = slot.shape[1]
    rows = dose.shape[0]

    def copies(t):
        rows_of_run = [t * RUN + u for u in range(RUN)]
        return [row_copy(True, runs, slots, me, stored, kept_mine, sems, b) for b in rows_of_run]

    for copy in copies(jnp.int32(0)):
        copy.start()
    scale_weights(pieces, scaled)
    for kept, out, row0 in ((kept_others, given, rows), (kept_mine, dose, 0)):

        def run(t, carry, kept=kept, out=out, row0=row0):
            if kept is kept_mine:
                for copy in copies(t):
                    copy.wait()
            for u in range(RUN):
                b = t * RUN + u
                left, blocks = row_operands(range(slots), row0 + b, slot, index, scaled, kept)
                right = jnp.concatenate(blocks, axis=1)
                out[b] = lax.dot_general(
                    left, right, (((1,), (1,)), ((), ())), preferred_element_type=F32
                )
            if kept is kept_others:

                @pl.when(t + 1 < rows // RUN)
                def _():
                    for copy in copies(t + 1):
                        copy.start()

            return carry

        lax.fori_loop(0, rows // RUN, run, 0)


def row_dose(chosen, b, slot, index, scaled, turned):
    left, blocks = row_operands(chosen, b, slot, index, scaled, turned)
    return jnp.dot(left, jnp.concatenate(blocks, axis=0), preferred_element_type=F32)


def near_forward_kernel(slot, index, over, near, turned_mine, turned_others, dose, scaled):
    scale_weights([near], scaled)
    rows, slots = slot.shape
    last = range(cut_of(slots), slots)
    for turned, row0 in ((turned_mine, 0), (turned_others, rows // 2)):

        def run(t, carry, turned=turned, row0=row0):
            b0 = row0 + t * RUN
            skip = over[b0 // RUN, 0] > 0

            @pl.when(skip)
            def _():
                for u in range(RUN):
                    dose[b0 + u] = jnp.zeros(dose.shape[1:], F32)

            @pl.when(jnp.logical_not(skip))
            def _():
                for u in range(RUN):
                    dose[b0 + u] = row_dose(last, b0 + u, slot, index, scaled, turned)

            return carry

        lax.fori_loop(0, rows // 2 // RUN, run, 0)


def forward_kernel(row0, slot, index, over, near, far, turned, part, dose, scaled):
    scale_weights([near, far], scaled)
    slots = slot.shape[1]
    cut = cut_of(slots)

    def run(t, carry):
        b0 = row0 + t * RUN
        for u in range(RUN):
            value = row_dose(range(cut), b0 + u, slot, index, scaled, turned)
            dose[t * RUN + u] = part[b0 + u] + value

        @pl.when(over[b0 // RUN, 0] > 0)
        def _():
            for u in range(RUN):
                dose[t * RUN + u] += row_dose(
                    range(cut, slots), b0 + u, slot, index, scaled, turned
                )

        return carry

    lax.fori_loop(0, dose.shape[0] // RUN, run, 0)


def work_of(rows, slots, weightings, width):
    return pl.CostEstimate(
        flops=2 * rows * slots * weightings * width * width,
        bytes_accessed=2 * rows * slots * width * width,
        transcendentals=0,
    )


def near_forward(tables, near, turned_mine, turned_others):
    half, weightings, width = near.shape
    rows, slots = tables[0].shape
    return pl.pallas_call(
        near_forward_kernel,
        in_specs=[in_smem()] * 3 + [in_vmem()] * 3,
        out_specs=in_vmem(),
        out_shape=jax.ShapeDtypeStruct((rows, weightings, width), F32),
        scratch_shapes=[pltpu.VMEM((6 * half + 1, weightings, width), BF16)],
        compiler_params=PARAMS,
        cost_estimate=work_of(rows, slots - cut_of(slots), weightings, width),
        name="near_forward",
    )(*tables[:2], tables[4], near, held(turned_mine), held(turned_others))


def forward(row0, tables, near, far, turned, part):
    half, weightings, width = near.shape
    rows, slots = tables[0].shape
    return pl.pallas_call(
        functools.partial(forward_kernel, row0),
        in_specs=[in_smem()] * 3 + [in_vmem()] * 4,
        out_specs=in_vmem(),
        out_shape=jax.ShapeDtypeStruct((rows // 2, weightings, width), F32),
        scratch_shapes=[pltpu.VMEM((6 * half + 1, weightings, width), BF16)],
        compiler_params=PARAMS,
        cost_estimate=work_of(rows // 2, cut_of(slots), weightings, width),
        name="forward",
    )(*tables[:2], tables[4], near, far, held(turned), part)


def first_forward(runs, me, tables, pieces, kept_others, tiles):
    columns = sum(p.shape[0] for p in pieces)
    weightings, width = pieces[0].shape[1:]
    rows, slots = tables[0].shape
    rows //= 2
    part = jax.ShapeDtypeStruct((rows, weightings, width), F32)
    return pl.pallas_call(
        functools.partial(first_forward_kernel, runs),
        in_specs=[in_smem()] * 3
        + [in_vmem()] * (len(pieces) + 1)
        + [pl.BlockSpec(memory_space=pltpu.HBM)],
        out_specs=[in_vmem()] * 3,
        out_shape=[part, part, pltpu.VMEM((rows * slots, width, width), BF16)],
        scratch_shapes=[
            pltpu.VMEM((3 * columns + 1, weightings, width), BF16),
            pltpu.SemaphoreType.DMA((rows,)),
        ],
        compiler_params=PARAMS,
        cost_estimate=work_of(2 * rows, slots, weightings, width),
        name="first_forward",
    )(
        me,
        *tables[:2],
        *pieces,
        held(kept_others),
        pltpu.with_memory_space_constraint(tiles, pltpu.HBM),
    )


def add_row(chosen, b, tables, left, kept, total):
    slot, places, factor = tables
    width = kept.shape[-1]
    group = 8 if len(chosen) % 8 == 0 else 1
    for k0 in range(0, len(chosen), group):
        some = chosen[k0 : k0 + group]
        right = jnp.concatenate([kept[slot[b, k]] for k in some], axis=1)
        product = jnp.dot(left, right, preferred_element_type=F32)
        at = [places[b, k] for k in some]
        old = [total[p] for p in at]
        for i, k in enumerate(some):
            total[at[i]] = old[i] + product[:, i * width : (i + 1) * width] * factor[b, k]


def backward_kernel(mine, row0, slot, places, factor, over, slope, kept, *refs):
    *before, total = refs
    columns = total.shape[0] - slot.shape[1]
    total[columns:] = jnp.zeros_like(total[columns:])
    total[:columns] = jnp.zeros_like(total[:columns]) if mine else before.pop(0)[...]
    tables = (slot, places, factor)
    slots = slot.shape[1]
    cut = cut_of(slots)

    def run(t, carry):
        b0 = row0 + t * RUN
        for u in range(RUN):
            add_row(range(cut), b0 + u, tables, slope[t * RUN + u], kept, total)

        @pl.when(over[b0 // RUN, 0] > 0)
        def _():
            for u in range(RUN):
                add_row(range(cut, slots), b0 + u, tables, slope[t * RUN + u], kept, total)

        return carry

    lax.fori_loop(0, slope.shape[0] // RUN, run, 0)
    if mine:
        before[0][...] = total[:columns]
    else:
        far, near = before
        near[...] = total[: columns // 2]
        far[...] = total[columns // 2 : columns]


def near_backward_kernel(
    slot, places, factor, over, slope_mine, slope_others, kept_mine, kept_others, near, out, total
):
    half = near.shape[0]
    total[:half] = near[...]
    total[2 * half :] = jnp.zeros_like(total[2 * half :])
    tables = (slot, places, factor)
    rows, slots = slot.shape
    last = range(cut_of(slots), slots)
    for slope, kept, row0 in ((slope_mine, kept_mine, 0), (slope_others, kept_others, rows // 2)):

        def run(t, carry, slope=slope, kept=kept, row0=row0):
            b0 = row0 + t * RUN

            @pl.when(over[b0 // RUN, 0] == 0)
            def _():
                for u in range(RUN):
                    add_row(last, b0 + u, tables, slope[t * RUN + u], kept, total)

            return carry

        lax.fori_loop(0, rows // 2 // RUN, run, 0)
    out[...] = total[:half]


def backward(mine, row0, tables, slope, kept, columns, *total):
    half_rows, weightings, width = slope.shape
    slots = tables[0].shape[1]
    out = [(columns, weightings, width)] if mine else [(columns // 2, weightings, width)] * 2
    return pl.pallas_call(
        functools.partial(backward_kernel, mine, row0),
        in_specs=[in_smem()] * 4 + [in_vmem()] * (2 + len(total)),
        out_specs=[in_vmem()] * len(out),
        out_shape=[jax.ShapeDtypeStruct(shape, F32) for shape in out],
        scratch_shapes=[pltpu.VMEM((columns + slots, weightings, width), F32)],
        compiler_params=PARAMS,
        cost_estimate=work_of(half_rows, cut_of(slots), weightings, width),
        name="backward",
    )(tables[0], *tables[2:], slope, held(kept), *total)


def near_backward(tables, slope_mine, slope_others, kept_mine, kept_others, near):
    half, weightings, width = near.shape
    rows, slots = tables[0].shape
    return pl.pallas_call(
        near_backward_kernel,
        in_specs=[in_smem()] * 4 + [in_vmem()] * 5,
        out_specs=in_vmem(),
        out_shape=jax.ShapeDtypeStruct(near.shape, F32),
        scratch_shapes=[pltpu.VMEM((2 * half + slots, weightings, width), F32)],
        compiler_params=PARAMS,
        cost_estimate=work_of(rows, slots - cut_of(slots), weightings, width),
        name="near_backward",
    )(tables[0], *tables[2:], slope_mine, slope_others, held(kept_mine), held(kept_others), near)


def finish_kernel(me, mine, other, weights, gradient):
    own, _, width = mine.shape[1:]
    for out, i in ((weights, 0), (gradient, 1)):
        for c in range(2 * own):
            held_here = me[1] == c // own
            tile = jnp.where(held_here, mine[i, c % own], other[i, c % own])
            out[:, 0, c * width : (c + 1) * width] = tile


def finish(me, mine, other):
    _, own, weightings, width = mine.shape
    out = jax.ShapeDtypeStruct((weightings, 1, 2 * own * width), F32)
    return pl.pallas_call(
        finish_kernel,
        in_specs=[in_smem(), in_vmem(), in_vmem()],
        out_specs=[in_vmem()] * 2,
        out_shape=[out] * 2,
        compiler_params=PARAMS,
        name="finish",
    )(me, mine, other)


def per_device(
    sizes,
    dose_blocks,
    block_cols,
    block_exps,
    live_counts,
    labels,
    upper_dose,
    upper_weight,
    lower_dose,
    lower_weight,
    initial_spot_weights,
):
    n_vox, n_spot = sizes
    z, x, core = (lax.axis_index(a) for a in ("vox", "spot", "rep"))
    rows, _, slots, width, _ = dose_blocks.shape
    weightings, _, chunk_spots = initial_spot_weights.shape
    chunk = chunk_spots // width
    columns = chunk * n_vox
    own = chunk // 2
    initial = initial_spot_weights[:, 0].reshape(weightings, chunk, width)
    weights = lax.dynamic_slice_in_dim(initial, core * own, own, 1).transpose(1, 0, 2)

    def over_vox(arrays):
        return [
            lax.ppermute(a, "vox", [(i, i ^ d) for i in range(n_vox)])
            for d, a in enumerate(arrays, 1)
        ]

    def over_rep(array):
        return lax.ppermute(array, "rep", [(0, 1), (1, 0)])

    me = jnp.stack([z, core, x]).astype(jnp.int32)
    level_table = jnp.stack([upper_dose, upper_weight, lower_dose, lower_weight])
    tiles = dose_blocks.reshape(rows * slots, width, width)

    def gather_weights(weights):
        piece = weights.astype(BF16)
        return [piece] + over_vox([piece] * (n_vox - 1))

    bits = [1 << i for i in range(n_spot.bit_length() - 1)]
    pieces = gather_weights(weights)
    steps = [(1, 1)] + [(2, bit) for bit in bits]
    live = live_counts.reshape(rows)
    tables, kept_others, me, sides = prepare(
        n_vox, columns, n_spot, steps, me, block_cols, block_exps, live, tiles
    )
    pieces, kept_others = lax.optimization_barrier((pieces, kept_others))

    for step in range(ITERS):
        near = jnp.concatenate(pieces, axis=0)
        other_half = over_rep(near)
        if step == 0:
            given, dose, kept_mine = first_forward(
                n_spot, me, tables, [near, other_half], kept_others, tiles
            )
            labels, given = lax.optimization_barrier((labels, given))
            known = labels.astype(F32).reshape(-1, width)
        else:
            part = near_forward(tables, near, turned_mine, turned_others)
            given = forward(rows // 2, tables, near, other_half, turned_others, part)
            dose = forward(0, tables, near, other_half, turned_mine, part)
        dose = dose + over_rep(given)
        for e, bit in enumerate(bits, 1):
            sent = dose
            if step == 0:
                n = known.shape[0]
                tile = jnp.pad(known, ((0, weightings - n), (0, 0)))
                sent = jnp.concatenate([dose, tile[None]], axis=0)
            got = lax.ppermute(sent, "spot", [(i, i ^ bit) for i in range(n_spot)])
            if step == 0:
                theirs = got[rows // 2, :n]
                first = sides[e, :1] > 0
                known = jnp.concatenate(
                    [jnp.where(first, known, theirs), jnp.where(first, theirs, known)]
                )
                got = got[: rows // 2]
            dose = dose + got
        if step == 0:
            levels = jnp.zeros((4, rows // 2, 1, width), F32)
            for c in range(level_table.shape[1]):
                value = level_table[:, c][:, None, None, None]
                levels = jnp.where(known[None, :, None, :] == c, value, levels)
        slope = (
            levels[1] * jax.nn.sigmoid(4.0 * (dose - levels[0]))
            - levels[3] * jax.nn.sigmoid(4.0 * (levels[2] - dose))
        ).astype(BF16)
        slope_others = over_rep(slope)
        (total,) = backward(True, 0, tables, slope, kept_mine, columns)
        far, near = backward(False, rows // 2, tables, slope_others, kept_others, columns, total)
        theirs = over_rep(far)
        near = near_backward(tables, slope, slope_others, kept_mine, kept_others, near) + theirs
        received = over_vox([near[d * own : (d + 1) * own] for d in range(1, n_vox)])
        if step == 0:
            turned_mine = turn(kept_mine, near)
            received, turned_mine = lax.optimization_barrier((received, turned_mine))
        else:
            received = lax.optimization_barrier(received)
        gradient = near[:own]
        for part in received:
            gradient = gradient + part
        weights = jnp.maximum(weights - 0.5 * gradient, 0.0)
        if step < ITERS - 1:
            pieces = gather_weights(weights)
            if step == 0:
                turned_others = turn(kept_others, pieces[0])
                pieces, turned_others = lax.optimization_barrier((pieces, turned_others))

    mine = jnp.stack([weights, gradient])
    return tuple(finish(me, mine, over_rep(mine)))


def solution(mesh):
    placed = (
        P(("groups", "vox"), "spot", "rep", None, None),
        P(("groups", "vox"), "spot", "rep"),
        P(("groups", "vox"), "spot", "rep"),
        P(("groups", "vox"), "spot"),
        P(("groups", "vox", "spot", "rep")),
        P("groups"),
        P("groups"),
        P("groups"),
        P("groups"),
        P("groups", "spot", "vox"),
    )
    sizes = tuple(mesh.shape[a] for a in ("vox", "spot"))
    return jax.shard_map(
        functools.partial(per_device, sizes),
        mesh=mesh,
        in_specs=placed,
        out_specs=(P("groups", "spot", "vox"), P("groups", "spot", "vox")),
        check_vma=False,
    )
```

```python
import functools

import jax
import jax.numpy as jnp
from jax import lax
from jax.experimental import pallas as pl
from jax.experimental.pallas import tpu as pltpu
from jax.sharding import PartitionSpec as P

ITERS = 4
F32 = jnp.float32
BF16 = jnp.bfloat16
PARAMS = pltpu.CompilerParams(vmem_limit_bytes=16 * 2**20)


def in_vmem():
    return pl.BlockSpec(memory_space=pltpu.VMEM)


def in_smem():
    return pl.BlockSpec(memory_space=pltpu.SMEM)


def held(array):
    return pltpu.with_memory_space_constraint(array, pltpu.VMEM)


RUN = 4
LONG_RUN = 8


def cut_of(slots):
    return 2 * slots // 3


def prepare_kernel(n_vox, columns, runs, steps, me, cols, exps, live, stored, *refs):
    outs, kept, me_out, sides, packed, *tables, sems, load_sems = refs[:5], *refs[5:]
    loads = [
        row_copy(False, runs, cols.shape[2], me, stored, kept, load_sems, jnp.int32(b))
        for b in range(load_sems.shape[0])
    ]
    for load in loads:
        load.start()
    for i in range(me.shape[0]):
        me_out[i] = me[i]
    z, core = me[0], me[1]
    rows, _, slots = cols.shape
    own = columns // (2 * n_vox)
    column, exponent = cols[:, 0, :], exps[:, 0, :]
    piece, within = lax.div(column, own), lax.rem(column, own)
    place = ((lax.rem(piece, 2) ^ core) * n_vox + (lax.div(piece, 2) ^ z)) * own + within
    both = place * 4 + exponent + 1
    position = core * slots + lax.broadcasted_iota(jnp.int32, (1, slots), 1)
    n = rows // (2 * runs)
    for r in range(rows):
        half, t = divmod(r, rows // 2)
        first = 2 * n * (t // n) + t % n
        low, high = (first, first + n) if half == 0 else (first + n, first)
        row = jnp.where(core == 0, both[low : low + 1], both[high : high + 1])
        used = position < jnp.where(core == 0, live[low], live[high])
        packed[r : r + 1] = jnp.where(used, row, 3)

    both = packed[...]
    here = lax.broadcasted_iota(jnp.int32, (rows, slots), 1)
    dead = lax.rem(both, 4) == 3
    kind = jnp.where(dead, 2, jnp.where(both >= 2 * columns, 0, 1))
    key = kind * slots + here
    rank = jnp.zeros_like(key)
    for k in range(slots):
        rank = rank + jnp.where(key[:, k : k + 1] < key, 1, 0)
    both = jnp.where(dead, (columns + rank) * 4 + 3, both) * 64 + here
    ordered = jnp.zeros_like(key)
    for k in range(slots):
        ordered = ordered + jnp.where(rank[:, k : k + 1] == here, both[:, k : k + 1], 0)
    kind, place = lax.rem(lax.div(ordered, 64), 4), lax.div(ordered, 256)
    slot, index, places, factor, over = tables
    in_half = lax.rem(lax.broadcasted_iota(jnp.int32, (rows, slots), 0), rows // 2)
    slot[...] = in_half * slots + lax.rem(ordered, 64)
    index[...] = jnp.where(kind == 3, 3 * columns, kind * columns + place)
    places[...] = place
    factor[...] = jnp.where(
        kind == 3, 0.0, jnp.where(kind == 0, 0.5, jnp.where(kind == 2, 2.0, 1.0))
    ).astype(F32)
    others = jnp.where((kind != 3) & (place >= columns // 2), 1.0, 0.0).astype(F32)
    others = jnp.sum(others, axis=1, keepdims=True)
    for r in range(rows // RUN):
        most = jnp.max(others[r * RUN : (r + 1) * RUN], axis=0, keepdims=True)
        most = jnp.broadcast_to(most, (1, over.shape[1]))
        over[r : r + 1] = jnp.where(most > cut_of(slots), 1, 0)
    copies = [
        pltpu.make_async_copy(table, out, sems.at[i])
        for i, (table, out) in enumerate(zip(tables, outs, strict=True))
    ]
    for copy in copies:
        copy.start()
    for e, (at, bit) in enumerate(steps):
        side = jnp.where((me[at] & bit) == 0, 1.0, 0.0).astype(F32)
        sides[e] = jnp.full(sides.shape[1:], side)
    for copy in copies + loads:
        copy.wait()


def prepare(n_vox, columns, runs, steps, me, cols, exps, live, tiles):
    rows, _, slots = cols.shape
    shapes = [((rows, slots), t) for t in (jnp.int32, jnp.int32, jnp.int32, F32)]
    shapes.append(((rows // RUN, 128), jnp.int32))
    half = (tiles.shape[0] // 2,) + tiles.shape[1:]
    in_hbm = [pltpu.with_memory_space_constraint(a, pltpu.HBM) for a in (cols, exps, live, tiles)]
    *tables, kept, me, sides = pl.pallas_call(
        functools.partial(prepare_kernel, n_vox, columns, runs, steps),
        in_specs=[in_smem()]
        + [in_vmem()] * 2
        + [in_smem(), pl.BlockSpec(memory_space=pltpu.HBM)],
        out_specs=[in_smem()] * 5 + [in_vmem(), in_smem(), in_vmem()],
        out_shape=[pltpu.SMEM(*shape) for shape in shapes]
        + [pltpu.VMEM(half, tiles.dtype), pltpu.SMEM(me.shape, me.dtype)]
        + [jax.ShapeDtypeStruct((len(steps), 8, 128), F32)],
        scratch_shapes=[pltpu.VMEM((rows, slots), jnp.int32)]
        + [pltpu.VMEM(*shape) for shape in shapes]
        + [pltpu.SemaphoreType.DMA((len(shapes),)), pltpu.SemaphoreType.DMA((rows // 2,))],
        compiler_params=PARAMS,
        cost_estimate=pl.CostEstimate(flops=0, bytes_accessed=2 * tiles.size, transcendentals=0),
        name="prepare",
    )(me, *in_hbm)
    return tables, kept, me, sides


def turn_kernel(kept, after, turned):
    count = kept.shape[0]
    step = 8 if count % 8 == 0 else 1

    def some(t, carry):
        for u in range(step):
            turned[t * step + u] = kept[t * step + u].T
        return carry

    lax.fori_loop(0, count // step, some, 0)


def turn(kept, after):
    return pl.pallas_call(
        turn_kernel,
        in_specs=[in_vmem(), pl.BlockSpec(memory_space=pl.ANY)],
        out_specs=in_vmem(),
        out_shape=pltpu.VMEM(kept.shape, kept.dtype),
        compiler_params=PARAMS,
        cost_estimate=pl.CostEstimate(flops=0, bytes_accessed=4 * kept.size, transcendentals=0),
        name="turn",
    )(held(kept), after)


def scale_weights(pieces, scaled):
    columns = (scaled.shape[0] - 1) // 3
    at = 0
    for piece in pieces:
        n = piece.shape[0]
        values = piece[...]
        scaled[at : at + n] = values * BF16(0.5)
        scaled[columns + at : columns + at + n] = values
        scaled[2 * columns + at : 2 * columns + at + n] = values * BF16(2.0)
        at += n
    scaled[3 * columns] = jnp.zeros(scaled.shape[1:], BF16)


def row_operands(chosen, b, slot, index, scaled, blocks):
    left = jnp.concatenate([scaled[index[b, k]] for k in chosen], axis=1)
    return left, [blocks[slot[b, k]] for k in chosen]


def row_copy(mine, runs, slots, me, stored, kept, sems, b):
    n = sems.shape[0] // runs
    half = me[1] if mine else 1 - me[1]
    return pltpu.make_async_copy(
        stored.at[pl.ds(((2 * lax.div(b, n) + half) * n + lax.rem(b, n)) * slots, slots)],
        kept.at[pl.ds(b * slots, slots)],
        sems.at[b],
    )


def first_forward_kernel(runs, me, slot, index, *refs):
    pieces, (kept_others, stored, given, dose, kept_mine, scaled, sems) = refs[:-7], refs[-7:]
    slots = slot.shape[1]
    rows = dose.shape[0]

    def copies(t):
        rows_of_run = [t * RUN + u for u in range(RUN)]
        return [row_copy(True, runs, slots, me, stored, kept_mine, sems, b) for b in rows_of_run]

    for copy in copies(jnp.int32(0)):
        copy.start()
    scale_weights(pieces, scaled)
    for kept, out, row0 in ((kept_others, given, rows), (kept_mine, dose, 0)):

        def run(t, carry, kept=kept, out=out, row0=row0):
            if kept is kept_mine:
                for copy in copies(t):
                    copy.wait()
            for u in range(RUN):
                b = t * RUN + u
                left, blocks = row_operands(range(slots), row0 + b, slot, index, scaled, kept)
                right = jnp.concatenate(blocks, axis=1)
                out[b] = lax.dot_general(
                    left, right, (((1,), (1,)), ((), ())), preferred_element_type=F32
                )
            if kept is kept_others:

                @pl.when(t + 1 < rows // RUN)
                def _():
                    for copy in copies(t + 1):
                        copy.start()

            return carry

        lax.fori_loop(0, rows // RUN, run, 0)


def row_dose(chosen, b, slot, index, scaled, turned):
    left, blocks = row_operands(chosen, b, slot, index, scaled, turned)
    return jnp.dot(left, jnp.concatenate(blocks, axis=0), preferred_element_type=F32)


def near_forward_kernel(slot, index, over, near, turned_mine, turned_others, dose, scaled):
    scale_weights([near], scaled)
    rows, slots = slot.shape
    last = range(cut_of(slots), slots)
    for turned, row0 in ((turned_mine, 0), (turned_others, rows // 2)):

        def run(t, carry, turned=turned, row0=row0):
            b0 = row0 + t * RUN
            skip = over[b0 // RUN, 0] > 0

            @pl.when(skip)
            def _():
                for u in range(RUN):
                    dose[b0 + u] = jnp.zeros(dose.shape[1:], F32)

            @pl.when(jnp.logical_not(skip))
            def _():
                for u in range(RUN):
                    dose[b0 + u] = row_dose(last, b0 + u, slot, index, scaled, turned)

            return carry

        lax.fori_loop(0, rows // 2 // RUN, run, 0)


def forward_kernel(row0, slot, index, over, near, far, turned, part, dose, scaled):
    scale_weights([near, far], scaled)
    slots = slot.shape[1]
    cut = cut_of(slots)
    rows = dose.shape[0]
    step = LONG_RUN if rows % LONG_RUN == 0 else RUN

    def some_rows(t, carry):
        for u in range(step):
            b = t * step + u
            value = row_dose(range(cut), row0 + b, slot, index, scaled, turned)
            dose[b] = part[row0 + b] + value
        return carry

    lax.fori_loop(0, rows // step, some_rows, 0)

    def rest(t, carry):
        @pl.when(over[row0 // RUN + t, 0] > 0)
        def _():
            for u in range(RUN):
                b = t * RUN + u
                dose[b] += row_dose(range(cut, slots), row0 + b, slot, index, scaled, turned)

        return carry

    lax.fori_loop(0, rows // RUN, rest, 0)


def work_of(rows, slots, weightings, width):
    return pl.CostEstimate(
        flops=2 * rows * slots * weightings * width * width,
        bytes_accessed=2 * rows * slots * width * width,
        transcendentals=0,
    )


def near_forward(tables, near, turned_mine, turned_others):
    half, weightings, width = near.shape
    rows, slots = tables[0].shape
    return pl.pallas_call(
        near_forward_kernel,
        in_specs=[in_smem()] * 3 + [in_vmem()] * 3,
        out_specs=in_vmem(),
        out_shape=jax.ShapeDtypeStruct((rows, weightings, width), F32),
        scratch_shapes=[pltpu.VMEM((6 * half + 1, weightings, width), BF16)],
        compiler_params=PARAMS,
        cost_estimate=work_of(rows, slots - cut_of(slots), weightings, width),
        name="near_forward",
    )(*tables[:2], tables[4], near, held(turned_mine), held(turned_others))


def forward(row0, tables, near, far, turned, part):
    half, weightings, width = near.shape
    rows, slots = tables[0].shape
    return pl.pallas_call(
        functools.partial(forward_kernel, row0),
        in_specs=[in_smem()] * 3 + [in_vmem()] * 4,
        out_specs=in_vmem(),
        out_shape=jax.ShapeDtypeStruct((rows // 2, weightings, width), F32),
        scratch_shapes=[pltpu.VMEM((6 * half + 1, weightings, width), BF16)],
        compiler_params=PARAMS,
        cost_estimate=work_of(rows // 2, cut_of(slots), weightings, width),
        name="forward",
    )(*tables[:2], tables[4], near, far, held(turned), part)


def first_forward(runs, me, tables, pieces, kept_others, tiles):
    columns = sum(p.shape[0] for p in pieces)
    weightings, width = pieces[0].shape[1:]
    rows, slots = tables[0].shape
    rows //= 2
    part = jax.ShapeDtypeStruct((rows, weightings, width), F32)
    return pl.pallas_call(
        functools.partial(first_forward_kernel, runs),
        in_specs=[in_smem()] * 3
        + [in_vmem()] * (len(pieces) + 1)
        + [pl.BlockSpec(memory_space=pltpu.HBM)],
        out_specs=[in_vmem()] * 3,
        out_shape=[part, part, pltpu.VMEM((rows * slots, width, width), BF16)],
        scratch_shapes=[
            pltpu.VMEM((3 * columns + 1, weightings, width), BF16),
            pltpu.SemaphoreType.DMA((rows,)),
        ],
        compiler_params=PARAMS,
        cost_estimate=work_of(2 * rows, slots, weightings, width),
        name="first_forward",
    )(
        me,
        *tables[:2],
        *pieces,
        held(kept_others),
        pltpu.with_memory_space_constraint(tiles, pltpu.HBM),
    )


def add_row(chosen, b, tables, left, kept, total):
    slot, places, factor = tables
    width = kept.shape[-1]
    group = 8 if len(chosen) % 8 == 0 else 1
    for k0 in range(0, len(chosen), group):
        some = chosen[k0 : k0 + group]
        right = jnp.concatenate([kept[slot[b, k]] for k in some], axis=1)
        product = jnp.dot(left, right, preferred_element_type=F32)
        at = [places[b, k] for k in some]
        old = [total[p] for p in at]
        for i, k in enumerate(some):
            total[at[i]] = old[i] + product[:, i * width : (i + 1) * width] * factor[b, k]


def backward_kernel(mine, row0, slot, places, factor, over, slope, kept, *refs):
    *before, total = refs
    columns = total.shape[0] - slot.shape[1]
    total[columns:] = jnp.zeros_like(total[columns:])
    total[:columns] = jnp.zeros_like(total[:columns]) if mine else before.pop(0)[...]
    tables = (slot, places, factor)
    slots = slot.shape[1]
    cut = cut_of(slots)

    rows = slope.shape[0]
    step = LONG_RUN if rows % LONG_RUN == 0 else RUN

    def some_rows(t, carry):
        for u in range(step):
            b = t * step + u
            add_row(range(cut), row0 + b, tables, slope[b], kept, total)
        return carry

    lax.fori_loop(0, rows // step, some_rows, 0)

    def rest(t, carry):
        @pl.when(over[row0 // RUN + t, 0] > 0)
        def _():
            for u in range(RUN):
                b = t * RUN + u
                add_row(range(cut, slots), row0 + b, tables, slope[b], kept, total)

        return carry

    lax.fori_loop(0, rows // RUN, rest, 0)
    if mine:
        before[0][...] = total[:columns]
    else:
        far, near = before
        near[...] = total[: columns // 2]
        far[...] = total[columns // 2 : columns]


def near_backward_kernel(
    slot, places, factor, over, slope_mine, slope_others, kept_mine, kept_others, near, out, total
):
    half = near.shape[0]
    total[:half] = near[...]
    total[2 * half :] = jnp.zeros_like(total[2 * half :])
    tables = (slot, places, factor)
    rows, slots = slot.shape
    last = range(cut_of(slots), slots)
    for slope, kept, row0 in ((slope_mine, kept_mine, 0), (slope_others, kept_others, rows // 2)):

        def run(t, carry, slope=slope, kept=kept, row0=row0):
            b0 = row0 + t * RUN

            @pl.when(over[b0 // RUN, 0] == 0)
            def _():
                for u in range(RUN):
                    add_row(last, b0 + u, tables, slope[t * RUN + u], kept, total)

            return carry

        lax.fori_loop(0, rows // 2 // RUN, run, 0)
    out[...] = total[:half]


def backward(mine, row0, tables, slope, kept, columns, *total):
    half_rows, weightings, width = slope.shape
    slots = tables[0].shape[1]
    out = [(columns, weightings, width)] if mine else [(columns // 2, weightings, width)] * 2
    return pl.pallas_call(
        functools.partial(backward_kernel, mine, row0),
        in_specs=[in_smem()] * 4 + [in_vmem()] * (2 + len(total)),
        out_specs=[in_vmem()] * len(out),
        out_shape=[jax.ShapeDtypeStruct(shape, F32) for shape in out],
        scratch_shapes=[pltpu.VMEM((columns + slots, weightings, width), F32)],
        compiler_params=PARAMS,
        cost_estimate=work_of(half_rows, cut_of(slots), weightings, width),
        name="backward",
    )(tables[0], *tables[2:], slope, held(kept), *total)


def near_backward(tables, slope_mine, slope_others, kept_mine, kept_others, near):
    half, weightings, width = near.shape
    rows, slots = tables[0].shape
    return pl.pallas_call(
        near_backward_kernel,
        in_specs=[in_smem()] * 4 + [in_vmem()] * 5,
        out_specs=in_vmem(),
        out_shape=jax.ShapeDtypeStruct(near.shape, F32),
        scratch_shapes=[pltpu.VMEM((2 * half + slots, weightings, width), F32)],
        compiler_params=PARAMS,
        cost_estimate=work_of(rows, slots - cut_of(slots), weightings, width),
        name="near_backward",
    )(tables[0], *tables[2:], slope_mine, slope_others, held(kept_mine), held(kept_others), near)


def finish_kernel(me, mine, other, weights, gradient):
    own, _, width = mine.shape[1:]
    for out, i in ((weights, 0), (gradient, 1)):
        for c in range(2 * own):
            held_here = me[1] == c // own
            tile = jnp.where(held_here, mine[i, c % own], other[i, c % own])
            out[:, 0, c * width : (c + 1) * width] = tile


def finish(me, mine, other):
    _, own, weightings, width = mine.shape
    out = jax.ShapeDtypeStruct((weightings, 1, 2 * own * width), F32)
    return pl.pallas_call(
        finish_kernel,
        in_specs=[in_smem(), in_vmem(), in_vmem()],
        out_specs=[in_vmem()] * 2,
        out_shape=[out] * 2,
        compiler_params=PARAMS,
        name="finish",
    )(me, mine, other)


def per_device(
    sizes,
    dose_blocks,
    block_cols,
    block_exps,
    live_counts,
    labels,
    upper_dose,
    upper_weight,
    lower_dose,
    lower_weight,
    initial_spot_weights,
):
    n_vox, n_spot = sizes
    z, x, core = (lax.axis_index(a) for a in ("vox", "spot", "rep"))
    rows, _, slots, width, _ = dose_blocks.shape
    weightings, _, chunk_spots = initial_spot_weights.shape
    chunk = chunk_spots // width
    columns = chunk * n_vox
    own = chunk // 2
    initial = initial_spot_weights[:, 0].reshape(weightings, chunk, width)
    weights = lax.dynamic_slice_in_dim(initial, core * own, own, 1).transpose(1, 0, 2)

    def over_vox(arrays):
        return [
            lax.ppermute(a, "vox", [(i, i ^ d) for i in range(n_vox)])
            for d, a in enumerate(arrays, 1)
        ]

    def over_rep(array):
        return lax.ppermute(array, "rep", [(0, 1), (1, 0)])

    me = jnp.stack([z, core, x]).astype(jnp.int32)
    level_table = jnp.stack([upper_dose, upper_weight, lower_dose, lower_weight])
    tiles = dose_blocks.reshape(rows * slots, width, width)

    def gather_weights(weights):
        piece = weights.astype(BF16)
        return [piece] + over_vox([piece] * (n_vox - 1))

    bits = [1 << i for i in range(n_spot.bit_length() - 1)]
    pieces = gather_weights(weights)
    steps = [(1, 1)] + [(2, bit) for bit in bits]
    live = live_counts.reshape(rows)
    tables, kept_others, me, sides = prepare(
        n_vox, columns, n_spot, steps, me, block_cols, block_exps, live, tiles
    )
    pieces, kept_others = lax.optimization_barrier((pieces, kept_others))

    for step in range(ITERS):
        near = jnp.concatenate(pieces, axis=0)
        other_half = over_rep(near)
        if step == 0:
            given, dose, kept_mine = first_forward(
                n_spot, me, tables, [near, other_half], kept_others, tiles
            )
            labels, given = lax.optimization_barrier((labels, given))
            known = labels.astype(F32).reshape(-1, width)
        else:
            part = near_forward(tables, near, turned_mine, turned_others)
            given = forward(rows // 2, tables, near, other_half, turned_others, part)
            dose = forward(0, tables, near, other_half, turned_mine, part)
        dose = dose + over_rep(given)
        for e, bit in enumerate(bits, 1):
            sent = dose
            if step == 0:
                n = known.shape[0]
                tile = jnp.pad(known, ((0, weightings - n), (0, 0)))
                sent = jnp.concatenate([dose, tile[None]], axis=0)
            got = lax.ppermute(sent, "spot", [(i, i ^ bit) for i in range(n_spot)])
            if step == 0:
                theirs = got[rows // 2, :n]
                first = sides[e, :1] > 0
                known = jnp.concatenate(
                    [jnp.where(first, known, theirs), jnp.where(first, theirs, known)]
                )
                got = got[: rows // 2]
            dose = dose + got
        if step == 0:
            levels = jnp.zeros((4, rows // 2, 1, width), F32)
            for c in range(level_table.shape[1]):
                value = level_table[:, c][:, None, None, None]
                levels = jnp.where(known[None, :, None, :] == c, value, levels)
        slope = (
            levels[1] * jax.nn.sigmoid(4.0 * (dose - levels[0]))
            - levels[3] * jax.nn.sigmoid(4.0 * (levels[2] - dose))
        ).astype(BF16)
        slope_others = over_rep(slope)
        (total,) = backward(True, 0, tables, slope, kept_mine, columns)
        far, near = backward(False, rows // 2, tables, slope_others, kept_others, columns, total)
        theirs = over_rep(far)
        near = near_backward(tables, slope, slope_others, kept_mine, kept_others, near) + theirs
        received = over_vox([near[d * own : (d + 1) * own] for d in range(1, n_vox)])
        if step == 0:
            turned_mine = turn(kept_mine, near)
            received, turned_mine = lax.optimization_barrier((received, turned_mine))
        else:
            received = lax.optimization_barrier(received)
        gradient = near[:own]
        for part in received:
            gradient = gradient + part
        weights = jnp.maximum(weights - 0.5 * gradient, 0.0)
        if step < ITERS - 1:
            pieces = gather_weights(weights)
            if step == 0:
                turned_others = turn(kept_others, pieces[0])
                pieces, turned_others = lax.optimization_barrier((pieces, turned_others))

    mine = jnp.stack([weights, gradient])
    return tuple(finish(me, mine, over_rep(mine)))


def solution(mesh):
    placed = (
        P(("groups", "vox"), "spot", "rep", None, None),
        P(("groups", "vox"), "spot", "rep"),
        P(("groups", "vox"), "spot", "rep"),
        P(("groups", "vox"), "spot"),
        P(("groups", "vox", "spot", "rep")),
        P("groups"),
        P("groups"),
        P("groups"),
        P("groups"),
        P("groups", "spot", "vox"),
    )
    sizes = tuple(mesh.shape[a] for a in ("vox", "spot"))
    return jax.shard_map(
        functools.partial(per_device, sizes),
        mesh=mesh,
        in_specs=placed,
        out_specs=(P("groups", "spot", "vox"), P("groups", "spot", "vox")),
        check_vma=False,
    )
```

```python
import functools

import jax
import jax.numpy as jnp
from jax import lax
from jax.experimental import pallas as pl
from jax.experimental.pallas import tpu as pltpu
from jax.sharding import PartitionSpec as P

ITERS = 4
F32 = jnp.float32
BF16 = jnp.bfloat16
PARAMS = pltpu.CompilerParams(vmem_limit_bytes=16 * 2**20)


def in_vmem():
    return pl.BlockSpec(memory_space=pltpu.VMEM)


def in_smem():
    return pl.BlockSpec(memory_space=pltpu.SMEM)


def held(array):
    return pltpu.with_memory_space_constraint(array, pltpu.VMEM)


RUN = 4
LONG_RUN = 8


def cut_of(slots):
    return 17 * slots // 24


def prepare_kernel(n_vox, columns, runs, steps, me, cols, exps, live, stored, *refs):
    outs, kept, me_out, sides, packed, *tables, sems, load_sems = refs[:5], *refs[5:]
    loads = [
        row_copy(False, runs, cols.shape[2], me, stored, kept, load_sems, jnp.int32(b))
        for b in range(load_sems.shape[0])
    ]
    for load in loads:
        load.start()
    for i in range(me.shape[0]):
        me_out[i] = me[i]
    z, core = me[0], me[1]
    rows, _, slots = cols.shape
    own = columns // (2 * n_vox)
    column, exponent = cols[:, 0, :], exps[:, 0, :]
    piece, within = lax.div(column, own), lax.rem(column, own)
    place = ((lax.rem(piece, 2) ^ core) * n_vox + (lax.div(piece, 2) ^ z)) * own + within
    both = place * 4 + exponent + 1
    position = core * slots + lax.broadcasted_iota(jnp.int32, (1, slots), 1)
    n = rows // (2 * runs)
    for r in range(rows):
        half, t = divmod(r, rows // 2)
        first = 2 * n * (t // n) + t % n
        low, high = (first, first + n) if half == 0 else (first + n, first)
        row = jnp.where(core == 0, both[low : low + 1], both[high : high + 1])
        used = position < jnp.where(core == 0, live[low], live[high])
        packed[r : r + 1] = jnp.where(used, row, 3)

    both = packed[...]
    here = lax.broadcasted_iota(jnp.int32, (rows, slots), 1)
    dead = lax.rem(both, 4) == 3
    kind = jnp.where(dead, 2, jnp.where(both >= 2 * columns, 0, 1))
    key = kind * slots + here
    rank = jnp.zeros_like(key)
    for k in range(slots):
        rank = rank + jnp.where(key[:, k : k + 1] < key, 1, 0)
    both = jnp.where(dead, (columns + rank) * 4 + 3, both) * 64 + here
    ordered = jnp.zeros_like(key)
    for k in range(slots):
        ordered = ordered + jnp.where(rank[:, k : k + 1] == here, both[:, k : k + 1], 0)
    kind, place = lax.rem(lax.div(ordered, 64), 4), lax.div(ordered, 256)
    slot, index, places, factor, over = tables
    in_half = lax.rem(lax.broadcasted_iota(jnp.int32, (rows, slots), 0), rows // 2)
    slot[...] = in_half * slots + lax.rem(ordered, 64)
    index[...] = jnp.where(kind == 3, 3 * columns, kind * columns + place)
    places[...] = place
    factor[...] = jnp.where(
        kind == 3, 0.0, jnp.where(kind == 0, 0.5, jnp.where(kind == 2, 2.0, 1.0))
    ).astype(F32)
    others = jnp.where((kind != 3) & (place >= columns // 2), 1.0, 0.0).astype(F32)
    others = jnp.sum(others, axis=1, keepdims=True)
    for r in range(rows // RUN):
        most = jnp.max(others[r * RUN : (r + 1) * RUN], axis=0, keepdims=True)
        most = jnp.broadcast_to(most, (1, over.shape[1]))
        over[r : r + 1] = jnp.where(most > cut_of(slots), 1, 0)
    copies = [
        pltpu.make_async_copy(table, out, sems.at[i])
        for i, (table, out) in enumerate(zip(tables, outs, strict=True))
    ]
    for copy in copies:
        copy.start()
    for e, (at, bit) in enumerate(steps):
        side = jnp.where((me[at] & bit) == 0, 1.0, 0.0).astype(F32)
        sides[e] = jnp.full(sides.shape[1:], side)
    for copy in copies + loads:
        copy.wait()


def prepare(n_vox, columns, runs, steps, me, cols, exps, live, tiles):
    rows, _, slots = cols.shape
    shapes = [((rows, slots), t) for t in (jnp.int32, jnp.int32, jnp.int32, F32)]
    shapes.append(((rows // RUN, 128), jnp.int32))
    half = (tiles.shape[0] // 2,) + tiles.shape[1:]
    in_hbm = [pltpu.with_memory_space_constraint(a, pltpu.HBM) for a in (cols, exps, live, tiles)]
    *tables, kept, me, sides = pl.pallas_call(
        functools.partial(prepare_kernel, n_vox, columns, runs, steps),
        in_specs=[in_smem()]
        + [in_vmem()] * 2
        + [in_smem(), pl.BlockSpec(memory_space=pltpu.HBM)],
        out_specs=[in_smem()] * 5 + [in_vmem(), in_smem(), in_vmem()],
        out_shape=[pltpu.SMEM(*shape) for shape in shapes]
        + [pltpu.VMEM(half, tiles.dtype), pltpu.SMEM(me.shape, me.dtype)]
        + [jax.ShapeDtypeStruct((len(steps), 8, 128), F32)],
        scratch_shapes=[pltpu.VMEM((rows, slots), jnp.int32)]
        + [pltpu.VMEM(*shape) for shape in shapes]
        + [pltpu.SemaphoreType.DMA((len(shapes),)), pltpu.SemaphoreType.DMA((rows // 2,))],
        compiler_params=PARAMS,
        cost_estimate=pl.CostEstimate(flops=0, bytes_accessed=2 * tiles.size, transcendentals=0),
        name="prepare",
    )(me, *in_hbm)
    return tables, kept, me, sides


def turn_kernel(kept, after, turned):
    count = kept.shape[0]
    step = 8 if count % 8 == 0 else 1

    def some(t, carry):
        for u in range(step):
            turned[t * step + u] = kept[t * step + u].T
        return carry

    lax.fori_loop(0, count // step, some, 0)


def turn(kept, after):
    return pl.pallas_call(
        turn_kernel,
        in_specs=[in_vmem(), pl.BlockSpec(memory_space=pl.ANY)],
        out_specs=in_vmem(),
        out_shape=pltpu.VMEM(kept.shape, kept.dtype),
        compiler_params=PARAMS,
        cost_estimate=pl.CostEstimate(flops=0, bytes_accessed=4 * kept.size, transcendentals=0),
        name="turn",
    )(held(kept), after)


def scale_weights(pieces, scaled):
    columns = (scaled.shape[0] - 1) // 3
    at = 0
    for piece in pieces:
        n = piece.shape[0]
        values = piece[...]
        scaled[at : at + n] = values * BF16(0.5)
        scaled[columns + at : columns + at + n] = values
        scaled[2 * columns + at : 2 * columns + at + n] = values * BF16(2.0)
        at += n
    scaled[3 * columns] = jnp.zeros(scaled.shape[1:], BF16)


def row_operands(chosen, b, slot, index, scaled, blocks):
    left = jnp.concatenate([scaled[index[b, k]] for k in chosen], axis=1)
    return left, [blocks[slot[b, k]] for k in chosen]


def row_copy(mine, runs, slots, me, stored, kept, sems, b):
    n = sems.shape[0] // runs
    half = me[1] if mine else 1 - me[1]
    return pltpu.make_async_copy(
        stored.at[pl.ds(((2 * lax.div(b, n) + half) * n + lax.rem(b, n)) * slots, slots)],
        kept.at[pl.ds(b * slots, slots)],
        sems.at[b],
    )


def first_forward_kernel(runs, me, slot, index, *refs):
    pieces, (kept_others, stored, given, dose, kept_mine, scaled, sems) = refs[:-7], refs[-7:]
    slots = slot.shape[1]
    rows = dose.shape[0]

    def copies(t):
        rows_of_run = [t * RUN + u for u in range(RUN)]
        return [row_copy(True, runs, slots, me, stored, kept_mine, sems, b) for b in rows_of_run]

    for copy in copies(jnp.int32(0)):
        copy.start()
    scale_weights(pieces, scaled)
    for kept, out, row0 in ((kept_others, given, rows), (kept_mine, dose, 0)):

        def run(t, carry, kept=kept, out=out, row0=row0):
            if kept is kept_mine:
                for copy in copies(t):
                    copy.wait()
            for u in range(RUN):
                b = t * RUN + u
                left, blocks = row_operands(range(slots), row0 + b, slot, index, scaled, kept)
                right = jnp.concatenate(blocks, axis=1)
                out[b] = lax.dot_general(
                    left, right, (((1,), (1,)), ((), ())), preferred_element_type=F32
                )
            if kept is kept_others:

                @pl.when(t + 1 < rows // RUN)
                def _():
                    for copy in copies(t + 1):
                        copy.start()

            return carry

        lax.fori_loop(0, rows // RUN, run, 0)


def row_dose(chosen, b, slot, index, scaled, turned):
    left, blocks = row_operands(chosen, b, slot, index, scaled, turned)
    return jnp.dot(left, jnp.concatenate(blocks, axis=0), preferred_element_type=F32)


def near_forward_kernel(slot, index, over, near, turned_mine, turned_others, dose, scaled):
    scale_weights([near], scaled)
    rows, slots = slot.shape
    last = range(cut_of(slots), slots)
    for turned, row0 in ((turned_mine, 0), (turned_others, rows // 2)):

        def run(t, carry, turned=turned, row0=row0):
            b0 = row0 + t * RUN
            skip = over[b0 // RUN, 0] > 0

            @pl.when(skip)
            def _():
                for u in range(RUN):
                    dose[b0 + u] = jnp.zeros(dose.shape[1:], F32)

            @pl.when(jnp.logical_not(skip))
            def _():
                for u in range(RUN):
                    dose[b0 + u] = row_dose(last, b0 + u, slot, index, scaled, turned)

            return carry

        lax.fori_loop(0, rows // 2 // RUN, run, 0)


def forward_kernel(row0, slot, index, over, near, far, turned, part, dose, scaled):
    scale_weights([near, far], scaled)
    slots = slot.shape[1]
    cut = cut_of(slots)
    rows = dose.shape[0]
    step = LONG_RUN if rows % LONG_RUN == 0 else RUN

    def some_rows(t, carry):
        for u in range(step):
            b = t * step + u
            value = row_dose(range(cut), row0 + b, slot, index, scaled, turned)
            dose[b] = part[row0 + b] + value
        return carry

    lax.fori_loop(0, rows // step, some_rows, 0)

    def rest(t, carry):
        @pl.when(over[row0 // RUN + t, 0] > 0)
        def _():
            for u in range(RUN):
                b = t * RUN + u
                dose[b] += row_dose(range(cut, slots), row0 + b, slot, index, scaled, turned)

        return carry

    lax.fori_loop(0, rows // RUN, rest, 0)


def work_of(rows, slots, weightings, width):
    return pl.CostEstimate(
        flops=2 * rows * slots * weightings * width * width,
        bytes_accessed=2 * rows * slots * width * width,
        transcendentals=0,
    )


def near_forward(tables, near, turned_mine, turned_others):
    half, weightings, width = near.shape
    rows, slots = tables[0].shape
    return pl.pallas_call(
        near_forward_kernel,
        in_specs=[in_smem()] * 3 + [in_vmem()] * 3,
        out_specs=in_vmem(),
        out_shape=jax.ShapeDtypeStruct((rows, weightings, width), F32),
        scratch_shapes=[pltpu.VMEM((6 * half + 1, weightings, width), BF16)],
        compiler_params=PARAMS,
        cost_estimate=work_of(rows, slots - cut_of(slots), weightings, width),
        name="near_forward",
    )(*tables[:2], tables[4], near, held(turned_mine), held(turned_others))


def forward(row0, tables, near, far, turned, part):
    half, weightings, width = near.shape
    rows, slots = tables[0].shape
    return pl.pallas_call(
        functools.partial(forward_kernel, row0),
        in_specs=[in_smem()] * 3 + [in_vmem()] * 4,
        out_specs=in_vmem(),
        out_shape=jax.ShapeDtypeStruct((rows // 2, weightings, width), F32),
        scratch_shapes=[pltpu.VMEM((6 * half + 1, weightings, width), BF16)],
        compiler_params=PARAMS,
        cost_estimate=work_of(rows // 2, cut_of(slots), weightings, width),
        name="forward",
    )(*tables[:2], tables[4], near, far, held(turned), part)


def first_forward(runs, me, tables, pieces, kept_others, tiles):
    columns = sum(p.shape[0] for p in pieces)
    weightings, width = pieces[0].shape[1:]
    rows, slots = tables[0].shape
    rows //= 2
    part = jax.ShapeDtypeStruct((rows, weightings, width), F32)
    return pl.pallas_call(
        functools.partial(first_forward_kernel, runs),
        in_specs=[in_smem()] * 3
        + [in_vmem()] * (len(pieces) + 1)
        + [pl.BlockSpec(memory_space=pltpu.HBM)],
        out_specs=[in_vmem()] * 3,
        out_shape=[part, part, pltpu.VMEM((rows * slots, width, width), BF16)],
        scratch_shapes=[
            pltpu.VMEM((3 * columns + 1, weightings, width), BF16),
            pltpu.SemaphoreType.DMA((rows,)),
        ],
        compiler_params=PARAMS,
        cost_estimate=work_of(2 * rows, slots, weightings, width),
        name="first_forward",
    )(
        me,
        *tables[:2],
        *pieces,
        held(kept_others),
        pltpu.with_memory_space_constraint(tiles, pltpu.HBM),
    )


def add_row(chosen, b, tables, left, kept, total):
    slot, places, factor = tables
    width = kept.shape[-1]
    size = -(-len(chosen) // max(1, len(chosen) // 8))
    for k0 in range(0, len(chosen), size):
        some = chosen[k0 : k0 + size]
        right = jnp.concatenate([kept[slot[b, k]] for k in some], axis=1)
        product = jnp.dot(left, right, preferred_element_type=F32)
        at = [places[b, k] for k in some]
        old = [total[p] for p in at]
        for i, k in enumerate(some):
            total[at[i]] = old[i] + product[:, i * width : (i + 1) * width] * factor[b, k]


def backward_kernel(mine, row0, slot, places, factor, over, slope, kept, *refs):
    *before, total = refs
    columns = total.shape[0] - slot.shape[1]
    total[columns:] = jnp.zeros_like(total[columns:])
    total[:columns] = jnp.zeros_like(total[:columns]) if mine else before.pop(0)[...]
    tables = (slot, places, factor)
    slots = slot.shape[1]
    cut = cut_of(slots)

    rows = slope.shape[0]
    step = LONG_RUN if rows % LONG_RUN == 0 else RUN

    def some_rows(t, carry):
        for u in range(step):
            b = t * step + u
            add_row(range(cut), row0 + b, tables, slope[b], kept, total)
        return carry

    lax.fori_loop(0, rows // step, some_rows, 0)

    def rest(t, carry):
        @pl.when(over[row0 // RUN + t, 0] > 0)
        def _():
            for u in range(RUN):
                b = t * RUN + u
                add_row(range(cut, slots), row0 + b, tables, slope[b], kept, total)

        return carry

    lax.fori_loop(0, rows // RUN, rest, 0)
    if mine:
        before[0][...] = total[:columns]
    else:
        far, near = before
        near[...] = total[: columns // 2]
        far[...] = total[columns // 2 : columns]


def near_backward_kernel(
    slot, places, factor, over, slope_mine, slope_others, kept_mine, kept_others, near, out, total
):
    half = near.shape[0]
    total[:half] = near[...]
    total[2 * half :] = jnp.zeros_like(total[2 * half :])
    tables = (slot, places, factor)
    rows, slots = slot.shape
    last = range(cut_of(slots), slots)
    for slope, kept, row0 in ((slope_mine, kept_mine, 0), (slope_others, kept_others, rows // 2)):

        def run(t, carry, slope=slope, kept=kept, row0=row0):
            b0 = row0 + t * RUN

            @pl.when(over[b0 // RUN, 0] == 0)
            def _():
                for u in range(RUN):
                    add_row(last, b0 + u, tables, slope[t * RUN + u], kept, total)

            return carry

        lax.fori_loop(0, rows // 2 // RUN, run, 0)
    out[...] = total[:half]


def backward(mine, row0, tables, slope, kept, columns, *total):
    half_rows, weightings, width = slope.shape
    slots = tables[0].shape[1]
    out = [(columns, weightings, width)] if mine else [(columns // 2, weightings, width)] * 2
    return pl.pallas_call(
        functools.partial(backward_kernel, mine, row0),
        in_specs=[in_smem()] * 4 + [in_vmem()] * (2 + len(total)),
        out_specs=[in_vmem()] * len(out),
        out_shape=[jax.ShapeDtypeStruct(shape, F32) for shape in out],
        scratch_shapes=[pltpu.VMEM((columns + slots, weightings, width), F32)],
        compiler_params=PARAMS,
        cost_estimate=work_of(half_rows, cut_of(slots), weightings, width),
        name="backward",
    )(tables[0], *tables[2:], slope, held(kept), *total)


def near_backward(tables, slope_mine, slope_others, kept_mine, kept_others, near):
    half, weightings, width = near.shape
    rows, slots = tables[0].shape
    return pl.pallas_call(
        near_backward_kernel,
        in_specs=[in_smem()] * 4 + [in_vmem()] * 5,
        out_specs=in_vmem(),
        out_shape=jax.ShapeDtypeStruct(near.shape, F32),
        scratch_shapes=[pltpu.VMEM((2 * half + slots, weightings, width), F32)],
        compiler_params=PARAMS,
        cost_estimate=work_of(rows, slots - cut_of(slots), weightings, width),
        name="near_backward",
    )(tables[0], *tables[2:], slope_mine, slope_others, held(kept_mine), held(kept_others), near)


def finish_kernel(me, mine, other, weights, gradient):
    own, _, width = mine.shape[1:]
    for out, i in ((weights, 0), (gradient, 1)):
        for c in range(2 * own):
            held_here = me[1] == c // own
            tile = jnp.where(held_here, mine[i, c % own], other[i, c % own])
            out[:, 0, c * width : (c + 1) * width] = tile


def finish(me, mine, other):
    _, own, weightings, width = mine.shape
    out = jax.ShapeDtypeStruct((weightings, 1, 2 * own * width), F32)
    return pl.pallas_call(
        finish_kernel,
        in_specs=[in_smem(), in_vmem(), in_vmem()],
        out_specs=[in_vmem()] * 2,
        out_shape=[out] * 2,
        compiler_params=PARAMS,
        name="finish",
    )(me, mine, other)


def per_device(
    sizes,
    dose_blocks,
    block_cols,
    block_exps,
    live_counts,
    labels,
    upper_dose,
    upper_weight,
    lower_dose,
    lower_weight,
    initial_spot_weights,
):
    n_vox, n_spot = sizes
    z, x, core = (lax.axis_index(a) for a in ("vox", "spot", "rep"))
    rows, _, slots, width, _ = dose_blocks.shape
    weightings, _, chunk_spots = initial_spot_weights.shape
    chunk = chunk_spots // width
    columns = chunk * n_vox
    own = chunk // 2
    initial = initial_spot_weights[:, 0].reshape(weightings, chunk, width)
    weights = lax.dynamic_slice_in_dim(initial, core * own, own, 1).transpose(1, 0, 2)

    def over_vox(arrays):
        return [
            lax.ppermute(a, "vox", [(i, i ^ d) for i in range(n_vox)])
            for d, a in enumerate(arrays, 1)
        ]

    def over_rep(array):
        return lax.ppermute(array, "rep", [(0, 1), (1, 0)])

    me = jnp.stack([z, core, x]).astype(jnp.int32)
    level_table = jnp.stack([upper_dose, upper_weight, lower_dose, lower_weight])
    tiles = dose_blocks.reshape(rows * slots, width, width)

    def gather_weights(weights):
        piece = weights.astype(BF16)
        return [piece] + over_vox([piece] * (n_vox - 1))

    bits = [1 << i for i in range(n_spot.bit_length() - 1)]
    pieces = gather_weights(weights)
    steps = [(1, 1)] + [(2, bit) for bit in bits]
    live = live_counts.reshape(rows)
    tables, kept_others, me, sides = prepare(
        n_vox, columns, n_spot, steps, me, block_cols, block_exps, live, tiles
    )
    pieces, kept_others = lax.optimization_barrier((pieces, kept_others))

    for step in range(ITERS):
        near = jnp.concatenate(pieces, axis=0)
        other_half = over_rep(near)
        if step == 0:
            given, dose, kept_mine = first_forward(
                n_spot, me, tables, [near, other_half], kept_others, tiles
            )
            labels, given = lax.optimization_barrier((labels, given))
            known = labels.astype(F32).reshape(-1, width)
        else:
            part = near_forward(tables, near, turned_mine, turned_others)
            given = forward(rows // 2, tables, near, other_half, turned_others, part)
            dose = forward(0, tables, near, other_half, turned_mine, part)
        dose = dose + over_rep(given)
        for e, bit in enumerate(bits, 1):
            sent = dose
            if step == 0:
                n = known.shape[0]
                tile = jnp.pad(known, ((0, weightings - n), (0, 0)))
                sent = jnp.concatenate([dose, tile[None]], axis=0)
            got = lax.ppermute(sent, "spot", [(i, i ^ bit) for i in range(n_spot)])
            if step == 0:
                theirs = got[rows // 2, :n]
                first = sides[e, :1] > 0
                known = jnp.concatenate(
                    [jnp.where(first, known, theirs), jnp.where(first, theirs, known)]
                )
                got = got[: rows // 2]
            dose = dose + got
        if step == 0:
            levels = jnp.zeros((4, rows // 2, 1, width), F32)
            for c in range(level_table.shape[1]):
                value = level_table[:, c][:, None, None, None]
                levels = jnp.where(known[None, :, None, :] == c, value, levels)
        slope = (
            levels[1] * jax.nn.sigmoid(4.0 * (dose - levels[0]))
            - levels[3] * jax.nn.sigmoid(4.0 * (levels[2] - dose))
        ).astype(BF16)
        slope_others = over_rep(slope)
        (total,) = backward(True, 0, tables, slope, kept_mine, columns)
        far, near = backward(False, rows // 2, tables, slope_others, kept_others, columns, total)
        theirs = over_rep(far)
        near = near_backward(tables, slope, slope_others, kept_mine, kept_others, near) + theirs
        received = over_vox([near[d * own : (d + 1) * own] for d in range(1, n_vox)])
        if step == 0:
            turned_mine = turn(kept_mine, near)
            received, turned_mine = lax.optimization_barrier((received, turned_mine))
        else:
            received = lax.optimization_barrier(received)
        gradient = near[:own]
        for part in received:
            gradient = gradient + part
        weights = jnp.maximum(weights - 0.5 * gradient, 0.0)
        if step < ITERS - 1:
            pieces = gather_weights(weights)
            if step == 0:
                turned_others = turn(kept_others, pieces[0])
                pieces, turned_others = lax.optimization_barrier((pieces, turned_others))

    mine = jnp.stack([weights, gradient])
    return tuple(finish(me, mine, over_rep(mine)))


def solution(mesh):
    placed = (
        P(("groups", "vox"), "spot", "rep", None, None),
        P(("groups", "vox"), "spot", "rep"),
        P(("groups", "vox"), "spot", "rep"),
        P(("groups", "vox"), "spot"),
        P(("groups", "vox", "spot", "rep")),
        P("groups"),
        P("groups"),
        P("groups"),
        P("groups"),
        P("groups", "spot", "vox"),
    )
    sizes = tuple(mesh.shape[a] for a in ("vox", "spot"))
    return jax.shard_map(
        functools.partial(per_device, sizes),
        mesh=mesh,
        in_specs=placed,
        out_specs=(P("groups", "spot", "vox"), P("groups", "spot", "vox")),
        check_vma=False,
    )
```

```python
import functools

import jax
import jax.numpy as jnp
from jax import lax
from jax.experimental import pallas as pl
from jax.experimental.pallas import tpu as pltpu
from jax.sharding import PartitionSpec as P

ITERS = 4
F32 = jnp.float32
BF16 = jnp.bfloat16
PARAMS = pltpu.CompilerParams(vmem_limit_bytes=16 * 2**20)


def in_vmem():
    return pl.BlockSpec(memory_space=pltpu.VMEM)


def in_smem():
    return pl.BlockSpec(memory_space=pltpu.SMEM)


def held(array):
    return pltpu.with_memory_space_constraint(array, pltpu.VMEM)


RUN = 4
LONG_RUN = 8


def cut_of(slots, mine):
    return (18 if mine else 17) * slots // 24


def prepare_kernel(n_vox, columns, runs, steps, me, cols, exps, live, stored, *refs):
    outs, kept, me_out, sides, packed, *tables, sems, load_sems = refs[:5], *refs[5:]
    loads = [
        row_copy(False, runs, cols.shape[2], me, stored, kept, load_sems, jnp.int32(b))
        for b in range(load_sems.shape[0])
    ]
    for load in loads:
        load.start()
    for i in range(me.shape[0]):
        me_out[i] = me[i]
    z, core = me[0], me[1]
    rows, _, slots = cols.shape
    own = columns // (2 * n_vox)
    column, exponent = cols[:, 0, :], exps[:, 0, :]
    piece, within = lax.div(column, own), lax.rem(column, own)
    place = ((lax.rem(piece, 2) ^ core) * n_vox + (lax.div(piece, 2) ^ z)) * own + within
    both = place * 4 + exponent + 1
    position = core * slots + lax.broadcasted_iota(jnp.int32, (1, slots), 1)
    n = rows // (2 * runs)
    for r in range(rows):
        half, t = divmod(r, rows // 2)
        first = 2 * n * (t // n) + t % n
        low, high = (first, first + n) if half == 0 else (first + n, first)
        row = jnp.where(core == 0, both[low : low + 1], both[high : high + 1])
        used = position < jnp.where(core == 0, live[low], live[high])
        packed[r : r + 1] = jnp.where(used, row, 3)

    both = packed[...]
    here = lax.broadcasted_iota(jnp.int32, (rows, slots), 1)
    dead = lax.rem(both, 4) == 3
    kind = jnp.where(dead, 2, jnp.where(both >= 2 * columns, 0, 1))
    key = kind * slots + here
    rank = jnp.zeros_like(key)
    for k in range(slots):
        rank = rank + jnp.where(key[:, k : k + 1] < key, 1, 0)
    both = jnp.where(dead, (columns + rank) * 4 + 3, both) * 64 + here
    ordered = jnp.zeros_like(key)
    for k in range(slots):
        ordered = ordered + jnp.where(rank[:, k : k + 1] == here, both[:, k : k + 1], 0)
    kind, place = lax.rem(lax.div(ordered, 64), 4), lax.div(ordered, 256)
    slot, index, places, factor, over = tables
    in_half = lax.rem(lax.broadcasted_iota(jnp.int32, (rows, slots), 0), rows // 2)
    slot[...] = in_half * slots + lax.rem(ordered, 64)
    index[...] = jnp.where(kind == 3, 3 * columns, kind * columns + place)
    places[...] = place
    factor[...] = jnp.where(
        kind == 3, 0.0, jnp.where(kind == 0, 0.5, jnp.where(kind == 2, 2.0, 1.0))
    ).astype(F32)
    others = jnp.where((kind != 3) & (place >= columns // 2), 1.0, 0.0).astype(F32)
    others = jnp.sum(others, axis=1, keepdims=True)
    for r in range(rows // RUN):
        most = jnp.max(others[r * RUN : (r + 1) * RUN], axis=0, keepdims=True)
        most = jnp.broadcast_to(most, (1, over.shape[1]))
        over[r : r + 1] = jnp.where(most > cut_of(slots, 2 * r * RUN < rows), 1, 0)
    copies = [
        pltpu.make_async_copy(table, out, sems.at[i])
        for i, (table, out) in enumerate(zip(tables, outs, strict=True))
    ]
    for copy in copies:
        copy.start()
    for e, (at, bit) in enumerate(steps):
        side = jnp.where((me[at] & bit) == 0, 1.0, 0.0).astype(F32)
        sides[e] = jnp.full(sides.shape[1:], side)
    for copy in copies + loads:
        copy.wait()


def prepare(n_vox, columns, runs, steps, me, cols, exps, live, tiles):
    rows, _, slots = cols.shape
    shapes = [((rows, slots), t) for t in (jnp.int32, jnp.int32, jnp.int32, F32)]
    shapes.append(((rows // RUN, 128), jnp.int32))
    half = (tiles.shape[0] // 2,) + tiles.shape[1:]
    in_hbm = [pltpu.with_memory_space_constraint(a, pltpu.HBM) for a in (cols, exps, live, tiles)]
    *tables, kept, me, sides = pl.pallas_call(
        functools.partial(prepare_kernel, n_vox, columns, runs, steps),
        in_specs=[in_smem()]
        + [in_vmem()] * 2
        + [in_smem(), pl.BlockSpec(memory_space=pltpu.HBM)],
        out_specs=[in_smem()] * 5 + [in_vmem(), in_smem(), in_vmem()],
        out_shape=[pltpu.SMEM(*shape) for shape in shapes]
        + [pltpu.VMEM(half, tiles.dtype), pltpu.SMEM(me.shape, me.dtype)]
        + [jax.ShapeDtypeStruct((len(steps), 8, 128), F32)],
        scratch_shapes=[pltpu.VMEM((rows, slots), jnp.int32)]
        + [pltpu.VMEM(*shape) for shape in shapes]
        + [pltpu.SemaphoreType.DMA((len(shapes),)), pltpu.SemaphoreType.DMA((rows // 2,))],
        compiler_params=PARAMS,
        cost_estimate=pl.CostEstimate(flops=0, bytes_accessed=2 * tiles.size, transcendentals=0),
        name="prepare",
    )(me, *in_hbm)
    return tables, kept, me, sides


def turn_kernel(kept, after, turned):
    count = kept.shape[0]
    step = 8 if count % 8 == 0 else 1

    def some(t, carry):
        for u in range(step):
            turned[t * step + u] = kept[t * step + u].T
        return carry

    lax.fori_loop(0, count // step, some, 0)


def turn(kept, after):
    return pl.pallas_call(
        turn_kernel,
        in_specs=[in_vmem(), pl.BlockSpec(memory_space=pl.ANY)],
        out_specs=in_vmem(),
        out_shape=pltpu.VMEM(kept.shape, kept.dtype),
        compiler_params=PARAMS,
        cost_estimate=pl.CostEstimate(flops=0, bytes_accessed=4 * kept.size, transcendentals=0),
        name="turn",
    )(held(kept), after)


def scale_weights(pieces, scaled):
    columns = (scaled.shape[0] - 1) // 3
    at = 0
    for piece in pieces:
        n = piece.shape[0]
        values = piece[...]
        scaled[at : at + n] = values * BF16(0.5)
        scaled[columns + at : columns + at + n] = values
        scaled[2 * columns + at : 2 * columns + at + n] = values * BF16(2.0)
        at += n
    scaled[3 * columns] = jnp.zeros(scaled.shape[1:], BF16)


def row_operands(chosen, b, slot, index, scaled, blocks):
    left = jnp.concatenate([scaled[index[b, k]] for k in chosen], axis=1)
    return left, [blocks[slot[b, k]] for k in chosen]


def row_copy(mine, runs, slots, me, stored, kept, sems, b):
    n = sems.shape[0] // runs
    half = me[1] if mine else 1 - me[1]
    return pltpu.make_async_copy(
        stored.at[pl.ds(((2 * lax.div(b, n) + half) * n + lax.rem(b, n)) * slots, slots)],
        kept.at[pl.ds(b * slots, slots)],
        sems.at[b],
    )


def first_forward_kernel(runs, me, slot, index, *refs):
    pieces, (kept_others, stored, given, dose, kept_mine, scaled, sems) = refs[:-7], refs[-7:]
    slots = slot.shape[1]
    rows = dose.shape[0]

    def copies(t):
        rows_of_run = [t * RUN + u for u in range(RUN)]
        return [row_copy(True, runs, slots, me, stored, kept_mine, sems, b) for b in rows_of_run]

    for copy in copies(jnp.int32(0)):
        copy.start()
    scale_weights(pieces, scaled)
    for kept, out, row0 in ((kept_others, given, rows), (kept_mine, dose, 0)):

        def run(t, carry, kept=kept, out=out, row0=row0):
            if kept is kept_mine:
                for copy in copies(t):
                    copy.wait()
            for u in range(RUN):
                b = t * RUN + u
                left, blocks = row_operands(range(slots), row0 + b, slot, index, scaled, kept)
                right = jnp.concatenate(blocks, axis=1)
                out[b] = lax.dot_general(
                    left, right, (((1,), (1,)), ((), ())), preferred_element_type=F32
                )
            if kept is kept_others:

                @pl.when(t + 1 < rows // RUN)
                def _():
                    for copy in copies(t + 1):
                        copy.start()

            return carry

        lax.fori_loop(0, rows // RUN, run, 0)


def row_dose(chosen, b, slot, index, scaled, turned):
    left, blocks = row_operands(chosen, b, slot, index, scaled, turned)
    return jnp.dot(left, jnp.concatenate(blocks, axis=0), preferred_element_type=F32)


def near_forward_kernel(slot, index, over, near, turned_mine, turned_others, dose, scaled):
    scale_weights([near], scaled)
    rows, slots = slot.shape
    for turned, row0 in ((turned_mine, 0), (turned_others, rows // 2)):

        last = range(cut_of(slots, row0 == 0), slots)

        def run(t, carry, turned=turned, row0=row0, last=last):
            b0 = row0 + t * RUN
            skip = over[b0 // RUN, 0] > 0

            @pl.when(skip)
            def _():
                for u in range(RUN):
                    dose[b0 + u] = jnp.zeros(dose.shape[1:], F32)

            @pl.when(jnp.logical_not(skip))
            def _():
                for u in range(RUN):
                    dose[b0 + u] = row_dose(last, b0 + u, slot, index, scaled, turned)

            return carry

        lax.fori_loop(0, rows // 2 // RUN, run, 0)


def forward_kernel(row0, slot, index, over, near, far, turned, part, dose, scaled):
    scale_weights([near, far], scaled)
    slots = slot.shape[1]
    cut = cut_of(slots, row0 == 0)
    rows = dose.shape[0]
    step = LONG_RUN if rows % LONG_RUN == 0 else RUN

    def some_rows(t, carry):
        for u in range(step):
            b = t * step + u
            value = row_dose(range(cut), row0 + b, slot, index, scaled, turned)
            dose[b] = part[row0 + b] + value
        return carry

    lax.fori_loop(0, rows // step, some_rows, 0)

    def rest(t, carry):
        @pl.when(over[row0 // RUN + t, 0] > 0)
        def _():
            for u in range(RUN):
                b = t * RUN + u
                dose[b] += row_dose(range(cut, slots), row0 + b, slot, index, scaled, turned)

        return carry

    lax.fori_loop(0, rows // RUN, rest, 0)


def work_of(rows, slots, weightings, width):
    return pl.CostEstimate(
        flops=2 * rows * slots * weightings * width * width,
        bytes_accessed=2 * rows * slots * width * width,
        transcendentals=0,
    )


def near_forward(tables, near, turned_mine, turned_others):
    half, weightings, width = near.shape
    rows, slots = tables[0].shape
    return pl.pallas_call(
        near_forward_kernel,
        in_specs=[in_smem()] * 3 + [in_vmem()] * 3,
        out_specs=in_vmem(),
        out_shape=jax.ShapeDtypeStruct((rows, weightings, width), F32),
        scratch_shapes=[pltpu.VMEM((6 * half + 1, weightings, width), BF16)],
        compiler_params=PARAMS,
        cost_estimate=work_of(rows, slots - cut_of(slots, True), weightings, width),
        name="near_forward",
    )(*tables[:2], tables[4], near, held(turned_mine), held(turned_others))


def forward(row0, tables, near, far, turned, part):
    half, weightings, width = near.shape
    rows, slots = tables[0].shape
    return pl.pallas_call(
        functools.partial(forward_kernel, row0),
        in_specs=[in_smem()] * 3 + [in_vmem()] * 4,
        out_specs=in_vmem(),
        out_shape=jax.ShapeDtypeStruct((rows // 2, weightings, width), F32),
        scratch_shapes=[pltpu.VMEM((6 * half + 1, weightings, width), BF16)],
        compiler_params=PARAMS,
        cost_estimate=work_of(rows // 2, cut_of(slots, True), weightings, width),
        name="forward",
    )(*tables[:2], tables[4], near, far, held(turned), part)


def first_forward(runs, me, tables, pieces, kept_others, tiles):
    columns = sum(p.shape[0] for p in pieces)
    weightings, width = pieces[0].shape[1:]
    rows, slots = tables[0].shape
    rows //= 2
    part = jax.ShapeDtypeStruct((rows, weightings, width), F32)
    return pl.pallas_call(
        functools.partial(first_forward_kernel, runs),
        in_specs=[in_smem()] * 3
        + [in_vmem()] * (len(pieces) + 1)
        + [pl.BlockSpec(memory_space=pltpu.HBM)],
        out_specs=[in_vmem()] * 3,
        out_shape=[part, part, pltpu.VMEM((rows * slots, width, width), BF16)],
        scratch_shapes=[
            pltpu.VMEM((3 * columns + 1, weightings, width), BF16),
            pltpu.SemaphoreType.DMA((rows,)),
        ],
        compiler_params=PARAMS,
        cost_estimate=work_of(2 * rows, slots, weightings, width),
        name="first_forward",
    )(
        me,
        *tables[:2],
        *pieces,
        held(kept_others),
        pltpu.with_memory_space_constraint(tiles, pltpu.HBM),
    )


def add_row(chosen, b, tables, left, kept, total):
    slot, places, factor = tables
    width = kept.shape[-1]
    size = -(-len(chosen) // max(1, len(chosen) // 8))
    for k0 in range(0, len(chosen), size):
        some = chosen[k0 : k0 + size]
        right = jnp.concatenate([kept[slot[b, k]] for k in some], axis=1)
        product = jnp.dot(left, right, preferred_element_type=F32)
        at = [places[b, k] for k in some]
        old = [total[p] for p in at]
        for i, k in enumerate(some):
            total[at[i]] = old[i] + product[:, i * width : (i + 1) * width] * factor[b, k]


def backward_kernel(mine, row0, slot, places, factor, over, slope, kept, *refs):
    *before, total = refs
    columns = total.shape[0] - slot.shape[1]
    total[columns:] = jnp.zeros_like(total[columns:])
    total[:columns] = jnp.zeros_like(total[:columns]) if mine else before.pop(0)[...]
    tables = (slot, places, factor)
    slots = slot.shape[1]
    cut = cut_of(slots, mine)

    rows = slope.shape[0]
    step = LONG_RUN if rows % LONG_RUN == 0 else RUN

    def some_rows(t, carry):
        for u in range(step):
            b = t * step + u
            add_row(range(cut), row0 + b, tables, slope[b], kept, total)
        return carry

    lax.fori_loop(0, rows // step, some_rows, 0)

    def rest(t, carry):
        @pl.when(over[row0 // RUN + t, 0] > 0)
        def _():
            for u in range(RUN):
                b = t * RUN + u
                add_row(range(cut, slots), row0 + b, tables, slope[b], kept, total)

        return carry

    lax.fori_loop(0, rows // RUN, rest, 0)
    if mine:
        before[0][...] = total[:columns]
    else:
        far, near = before
        near[...] = total[: columns // 2]
        far[...] = total[columns // 2 : columns]


def near_backward_kernel(
    slot, places, factor, over, slope_mine, slope_others, kept_mine, kept_others, near, out, total
):
    half = near.shape[0]
    total[:half] = near[...]
    total[2 * half :] = jnp.zeros_like(total[2 * half :])
    tables = (slot, places, factor)
    rows, slots = slot.shape
    for slope, kept, row0 in ((slope_mine, kept_mine, 0), (slope_others, kept_others, rows // 2)):

        last = range(cut_of(slots, row0 == 0), slots)

        def run(t, carry, slope=slope, kept=kept, row0=row0, last=last):
            b0 = row0 + t * RUN

            @pl.when(over[b0 // RUN, 0] == 0)
            def _():
                for u in range(RUN):
                    add_row(last, b0 + u, tables, slope[t * RUN + u], kept, total)

            return carry

        lax.fori_loop(0, rows // 2 // RUN, run, 0)
    out[...] = total[:half]


def backward(mine, row0, tables, slope, kept, columns, *total):
    half_rows, weightings, width = slope.shape
    slots = tables[0].shape[1]
    out = [(columns, weightings, width)] if mine else [(columns // 2, weightings, width)] * 2
    return pl.pallas_call(
        functools.partial(backward_kernel, mine, row0),
        in_specs=[in_smem()] * 4 + [in_vmem()] * (2 + len(total)),
        out_specs=[in_vmem()] * len(out),
        out_shape=[jax.ShapeDtypeStruct(shape, F32) for shape in out],
        scratch_shapes=[pltpu.VMEM((columns + slots, weightings, width), F32)],
        compiler_params=PARAMS,
        cost_estimate=work_of(half_rows, cut_of(slots, True), weightings, width),
        name="backward",
    )(tables[0], *tables[2:], slope, held(kept), *total)


def near_backward(tables, slope_mine, slope_others, kept_mine, kept_others, near):
    half, weightings, width = near.shape
    rows, slots = tables[0].shape
    return pl.pallas_call(
        near_backward_kernel,
        in_specs=[in_smem()] * 4 + [in_vmem()] * 5,
        out_specs=in_vmem(),
        out_shape=jax.ShapeDtypeStruct(near.shape, F32),
        scratch_shapes=[pltpu.VMEM((2 * half + slots, weightings, width), F32)],
        compiler_params=PARAMS,
        cost_estimate=work_of(rows, slots - cut_of(slots, True), weightings, width),
        name="near_backward",
    )(tables[0], *tables[2:], slope_mine, slope_others, held(kept_mine), held(kept_others), near)


def finish_kernel(me, mine, other, weights, gradient):
    own, _, width = mine.shape[1:]
    for out, i in ((weights, 0), (gradient, 1)):
        for c in range(2 * own):
            held_here = me[1] == c // own
            tile = jnp.where(held_here, mine[i, c % own], other[i, c % own])
            out[:, 0, c * width : (c + 1) * width] = tile


def finish(me, mine, other):
    _, own, weightings, width = mine.shape
    out = jax.ShapeDtypeStruct((weightings, 1, 2 * own * width), F32)
    return pl.pallas_call(
        finish_kernel,
        in_specs=[in_smem(), in_vmem(), in_vmem()],
        out_specs=[in_vmem()] * 2,
        out_shape=[out] * 2,
        compiler_params=PARAMS,
        name="finish",
    )(me, mine, other)


def per_device(
    sizes,
    dose_blocks,
    block_cols,
    block_exps,
    live_counts,
    labels,
    upper_dose,
    upper_weight,
    lower_dose,
    lower_weight,
    initial_spot_weights,
):
    n_vox, n_spot = sizes
    z, x, core = (lax.axis_index(a) for a in ("vox", "spot", "rep"))
    rows, _, slots, width, _ = dose_blocks.shape
    weightings, _, chunk_spots = initial_spot_weights.shape
    chunk = chunk_spots // width
    columns = chunk * n_vox
    own = chunk // 2
    initial = initial_spot_weights[:, 0].reshape(weightings, chunk, width)
    weights = lax.dynamic_slice_in_dim(initial, core * own, own, 1).transpose(1, 0, 2)

    def over_vox(arrays):
        return [
            lax.ppermute(a, "vox", [(i, i ^ d) for i in range(n_vox)])
            for d, a in enumerate(arrays, 1)
        ]

    def over_rep(array):
        return lax.ppermute(array, "rep", [(0, 1), (1, 0)])

    me = jnp.stack([z, core, x]).astype(jnp.int32)
    level_table = jnp.stack([upper_dose, upper_weight, lower_dose, lower_weight])
    tiles = dose_blocks.reshape(rows * slots, width, width)

    def gather_weights(weights):
        piece = weights.astype(BF16)
        return [piece] + over_vox([piece] * (n_vox - 1))

    bits = [1 << i for i in range(n_spot.bit_length() - 1)]
    pieces = gather_weights(weights)
    steps = [(1, 1)] + [(2, bit) for bit in bits]
    live = live_counts.reshape(rows)
    tables, kept_others, me, sides = prepare(
        n_vox, columns, n_spot, steps, me, block_cols, block_exps, live, tiles
    )
    pieces, kept_others = lax.optimization_barrier((pieces, kept_others))

    for step in range(ITERS):
        near = jnp.concatenate(pieces, axis=0)
        other_half = over_rep(near)
        if step == 0:
            given, dose, kept_mine = first_forward(
                n_spot, me, tables, [near, other_half], kept_others, tiles
            )
            labels, given = lax.optimization_barrier((labels, given))
            known = labels.astype(F32).reshape(-1, width)
        else:
            part = near_forward(tables, near, turned_mine, turned_others)
            given = forward(rows // 2, tables, near, other_half, turned_others, part)
            dose = forward(0, tables, near, other_half, turned_mine, part)
        dose = dose + over_rep(given)
        for e, bit in enumerate(bits, 1):
            sent = dose
            if step == 0:
                n = known.shape[0]
                tile = jnp.pad(known, ((0, weightings - n), (0, 0)))
                sent = jnp.concatenate([dose, tile[None]], axis=0)
            got = lax.ppermute(sent, "spot", [(i, i ^ bit) for i in range(n_spot)])
            if step == 0:
                theirs = got[rows // 2, :n]
                first = sides[e, :1] > 0
                known = jnp.concatenate(
                    [jnp.where(first, known, theirs), jnp.where(first, theirs, known)]
                )
                got = got[: rows // 2]
            dose = dose + got
        if step == 0:
            levels = jnp.zeros((4, rows // 2, 1, width), F32)
            for c in range(level_table.shape[1]):
                value = level_table[:, c][:, None, None, None]
                levels = jnp.where(known[None, :, None, :] == c, value, levels)
        slope = (
            levels[1] * jax.nn.sigmoid(4.0 * (dose - levels[0]))
            - levels[3] * jax.nn.sigmoid(4.0 * (levels[2] - dose))
        ).astype(BF16)
        slope_others = over_rep(slope)
        (total,) = backward(True, 0, tables, slope, kept_mine, columns)
        far, near = backward(False, rows // 2, tables, slope_others, kept_others, columns, total)
        theirs = over_rep(far)
        near = near_backward(tables, slope, slope_others, kept_mine, kept_others, near) + theirs
        received = over_vox([near[d * own : (d + 1) * own] for d in range(1, n_vox)])
        if step == 0:
            turned_mine = turn(kept_mine, near)
            received, turned_mine = lax.optimization_barrier((received, turned_mine))
        else:
            received = lax.optimization_barrier(received)
        gradient = near[:own]
        for part in received:
            gradient = gradient + part
        weights = jnp.maximum(weights - 0.5 * gradient, 0.0)
        if step < ITERS - 1:
            pieces = gather_weights(weights)
            if step == 0:
                turned_others = turn(kept_others, pieces[0])
                pieces, turned_others = lax.optimization_barrier((pieces, turned_others))

    mine = jnp.stack([weights, gradient])
    return tuple(finish(me, mine, over_rep(mine)))


def solution(mesh):
    placed = (
        P(("groups", "vox"), "spot", "rep", None, None),
        P(("groups", "vox"), "spot", "rep"),
        P(("groups", "vox"), "spot", "rep"),
        P(("groups", "vox"), "spot"),
        P(("groups", "vox", "spot", "rep")),
        P("groups"),
        P("groups"),
        P("groups"),
        P("groups"),
        P("groups", "spot", "vox"),
    )
    sizes = tuple(mesh.shape[a] for a in ("vox", "spot"))
    return jax.shard_map(
        functools.partial(per_device, sizes),
        mesh=mesh,
        in_specs=placed,
        out_specs=(P("groups", "spot", "vox"), P("groups", "spot", "vox")),
        check_vma=False,
    )
```
